32 devices in a mesh: east: 2 (over core), north: 16 (over z, y, x).
Axes of the slice: x: 2, y: 2, z: 4, core: 2. Of those that a mesh axis runs over, the one named last changes fastest.
Arguments:
- adjoint_start: float32 [5, 32, 512, 256], P(None, 'east', 'north'), may hold values from -3 to 3
- adjoint_source: float32 [5, 32, 512, 256], P(None, 'east', 'north'), may hold values from -6 to 6
- base_flow: float32 [3, 32, 512, 256], P(None, 'east', 'north'), may hold values from -3 to 3
- eddy_visc: float32 [32, 512, 256], P('east', 'north'), may hold values from 0.1 to 3
- rotor_count: int32 [2, 16], P('east', 'north'), may hold values from 128 to 1024, as said below
- rotor_cell: int32 [2, 16, 1024], P('east', 'north'), may hold values from 0 to 131071
- rotor_turbine: int32 [2, 16, 1024], P('east', 'north'), may hold values from 0 to 191
- rotor_sector: int32 [2, 16, 1024], P('east', 'north'), may hold values from 0 to 7
- rotor_weight: float32 [2, 16, 1024], P('east', 'north'), may hold values from 0.25 to 1
Outputs:
- adjoint_final: float32 [5, 32, 512, 256], P(None, 'east', 'north')
- thrust_grad: float32 [4, 8, 192], P(None, None, 'north')
The draws below stay inside these ranges and needn't reach their ends.
Inputs may be any that keep to these rules, and one draw needn't show every extreme that they name: `rotor_count`: an eighth of the tiles (at least one), drawn from the seed, hold 1024 live entries; the others hold 128 to 256.
All inputs are finite; a program needn't handle non-finite values.
Results may differ from the reference program's by a relative error of at most 0.0001.
Values sent between devices are 32-bit elements; how exact they have to be, the bound alone decides.
No kernel may reach another device: no remote copies, remote signals or barrier semaphores. Data moves between devices by JAX's collectives and lax.ppermute only.
A program may use at most 192 MiB of HBM per device.

```python
import math
import jax
import jax.numpy as jnp

CE = 16
CN = 32
CZ = 256
SLOTS = 1024
SECT = 8
TURB = 192
NE = 32
NN = 512
N_EAST = 2
N_NORTH = 16


def draw_rotor_count(key, part):
    tiles = N_EAST * N_NORTH
    order = jax.random.permutation(jax.random.fold_in(key, 11), tiles)
    normal_load = jax.random.randint(jax.random.fold_in(key, 12), (tiles,), SLOTS // 8, SLOTS // 4 + 1)
    wake = order < max(1, tiles // 8)
    counts = jnp.where(wake, SLOTS, normal_load).astype(jnp.int32)
    return counts.reshape(N_EAST, N_NORTH)


def set_ends(drawn, stream_key, least, largest):
    extent = drawn.shape
    index_at = [jax.random.randint(jax.random.fold_in(stream_key, axis), (), 0, extent[axis]) for axis in range(len(extent))]
    drawn = drawn.at[tuple(index_at)].set(least)
    longest = extent.index(max(extent))
    index_at[longest] = (index_at[longest] + 1) % extent[longest]
    return drawn.at[tuple(index_at)].set(largest)


def block_levels(rng, dims, cuts, low, high):
    loudness, own = 1.0, jax.random.fold_in(rng, 6)
    for axis_at, blocks in cuts:
        steps = jnp.exp(jax.random.uniform(jax.random.fold_in(own, axis_at), (blocks,), jnp.float32, low / len(cuts), high / len(cuts)))
        loudness = loudness * jnp.repeat(steps, dims[axis_at] // blocks).reshape([-1 if axis == axis_at else 1 for axis in range(len(dims))])
    return loudness


def noise(rng, dims, deviation, limit, pieces=(), held_as=jnp.bfloat16):
    values = deviation * jax.random.normal(rng, dims, jnp.float32)
    if pieces:
        values = values * block_levels(rng, dims, pieces, -0.22, 0.18)
    return jnp.clip(values, -limit, limit).astype(held_as)


def setup_inputs(seed: int = 0) -> dict:
    streams_of = jax.random.split(jax.random.key(seed), 10)
    return {
        "adjoint_start": noise(streams_of[0], (5, NE, NN, CZ), 0.5, 3.0, ((1, 2), (2, 16)), jnp.float32),
        "adjoint_source": noise(streams_of[1], (5, NE, NN, CZ), 1.0, 6.0, ((1, 2), (2, 16)), jnp.float32),
        "base_flow": noise(streams_of[2], (3, NE, NN, CZ), 0.7, 3.0, ((1, 2), (2, 16)), jnp.float32),
        "eddy_visc": jnp.clip(jnp.exp(math.log(3.0) - 3.4011974 * jax.random.uniform(streams_of[3], (NE, NN, CZ), jnp.float32) ** block_levels(streams_of[3], (NE, NN, CZ), ((0, 2), (1, 16)), -0.2, 0.2)), 0.1, 3.0),
        "rotor_count": draw_rotor_count(jax.random.fold_in(streams_of[9], 71), 0),
        "rotor_cell": set_ends(jax.random.randint(streams_of[5], (N_EAST, N_NORTH, SLOTS), 0, CE * CN * CZ), jax.random.fold_in(streams_of[5], 1), 0, (CE * CN * CZ) - 1).astype(jnp.int32),
        "rotor_turbine": set_ends(jax.random.randint(streams_of[6], (N_EAST, N_NORTH, SLOTS), 0, TURB), jax.random.fold_in(streams_of[6], 1), 0, TURB - 1).astype(jnp.int32),
        "rotor_sector": set_ends(jax.random.randint(streams_of[7], (N_EAST, N_NORTH, SLOTS), 0, SECT), jax.random.fold_in(streams_of[7], 1), 0, SECT - 1).astype(jnp.int32),
        "rotor_weight": jnp.clip(0.25 + 0.75 * jax.random.uniform(streams_of[8], (N_EAST, N_NORTH, SLOTS), jnp.float32) ** block_levels(streams_of[8], (N_EAST, N_NORTH, SLOTS), ((0, 2), (1, 16)), -0.2, 0.2), 0.25, 1.0),
    }


def spread(field):
    return jnp.pad(field, ((0, 0), (0, 0), (0, 0), (1, 1)))


def beside_all(padded):
    total = padded[:, 2:, 1:-1, 1:-1] + padded[:, :-2, 1:-1, 1:-1]
    total = total + padded[:, 1:-1, 2:, 1:-1] + padded[:, 1:-1, :-2, 1:-1]
    return total + padded[:, 1:-1, 1:-1, 2:] + padded[:, 1:-1, 1:-1, :-2]


def slopes(padded):
    return [padded[:, 2:, 1:-1, 1:-1] - padded[:, :-2, 1:-1, 1:-1],
            padded[:, 1:-1, 2:, 1:-1] - padded[:, 1:-1, :-2, 1:-1],
            padded[:, 1:-1, 1:-1, 2:] - padded[:, 1:-1, 1:-1, :-2]]


def relax(state_pad, base_pad, source):
    full = spread(state_pad)
    base_full = spread(base_pad)
    centre = full[:, 1:-1, 1:-1, 1:-1]
    base_centre = base_full[:, 1:-1, 1:-1, 1:-1]
    neighbours = beside_all(full)
    diffs = slopes(full)
    velocity_base = base_centre[:3]
    viscous = 1.0 + base_centre[3]
    convect = velocity_base[0] * diffs[0][:3] + velocity_base[1] * diffs[1][:3] + velocity_base[2] * diffs[2][:3]
    pressure_grad = jnp.stack([diffs[0][3], diffs[1][3], diffs[2][3]])
    velocity = (source[:3] + viscous * neighbours[:3] + 0.5 * convect - 0.5 * pressure_grad) / (6.0 * viscous + 1.0)
    diverge = diffs[0][0] + diffs[1][1] + diffs[2][2]
    pressure = (source[3] + neighbours[3] - 0.5 * diverge) / 7.0
    curvature = beside_all(base_full[:3]) - 6.0 * velocity_base
    eddy_new = (source[4] + viscous * neighbours[4] + 0.25 * jnp.sum(centre[:3] * curvature, axis=0)) / (6.0 * viscous + 2.0)
    return jnp.concatenate([velocity, pressure[None], eddy_new[None]], axis=0)


def rim_pad(field):
    return jnp.pad(field, ((0, 0), (1, 1), (1, 1), (0, 0)))


def reference(adjoint_start, adjoint_source, base_flow, eddy_visc, rotor_count, rotor_cell, rotor_turbine, rotor_sector, rotor_weight):
    base_four = jnp.concatenate([base_flow, eddy_visc[None]], axis=0)
    base_pad = rim_pad(base_four)
    state = adjoint_start
    for sweep in range(2):
        state = relax(rim_pad(state), base_pad, adjoint_source)
    east_tile = jnp.arange(N_EAST, dtype=jnp.int32)[:, None, None]
    north_tile = jnp.arange(N_NORTH, dtype=jnp.int32)[None, :, None]
    cell_east = rotor_cell // (CN * CZ) + east_tile * CE
    cell_north = (rotor_cell // CZ) % CN + north_tile * CN
    cell_level = rotor_cell % CZ
    values = state[:, cell_east, cell_north, cell_level]
    chosen = jnp.stack([values[0], values[1], values[2], values[4]])
    upstream = base_flow[0, cell_east, cell_north, cell_level]
    live = jnp.arange(SLOTS, dtype=jnp.int32)[None, None, :] < rotor_count[:, :, None]
    factor = jnp.where(live, rotor_weight * upstream * jnp.abs(upstream), 0.0)
    terms = (chosen * factor[None]).reshape(4, -1)
    segment = (rotor_sector * TURB + rotor_turbine).reshape(-1)
    summed = jax.vmap(lambda row: jax.ops.segment_sum(row, segment, num_segments=SECT * TURB))(terms)
    return state, summed.reshape(4, SECT, TURB)
```

```python
import functools

import jax
import jax.numpy as jnp
from jax import lax
from jax.experimental import pallas as pl
from jax.experimental.pallas import tpu as pltpu
from jax.sharding import PartitionSpec as P

SECT = 8
TURB_DEV = 12
COMPS = 4
LANES = 128
SUB = 8
PACK = 14
EDGE = 6
VMEM = pltpu.VMEM
F32 = jnp.float32


def whole(space=VMEM):
    return pl.BlockSpec(memory_space=space)


def in_vmem(x):
    return pltpu.with_memory_space_constraint(x, VMEM)


def params(mib):
    return pltpu.CompilerParams(vmem_limit_bytes=mib << 20)


def cost(flops, size):
    return pl.CostEstimate(flops=flops, bytes_accessed=size, transcendentals=0)


def face_kernel(at, start, flow, eddy, out, sems):
    e = at[0]
    copies = [
        pltpu.make_async_copy(start.at[:, e], out.at[0:5], sems.at[0]),
        pltpu.make_async_copy(flow.at[:, e], out.at[5:8], sems.at[1]),
        pltpu.make_async_copy(eddy.at[e], out.at[8], sems.at[2]),
    ]
    for c in copies:
        c.start()
    for c in copies:
        c.wait()


def east_face(at, start, flow, eddy):
    _, _, cn, cz = start.shape
    return pl.pallas_call(
        face_kernel,
        out_shape=jax.ShapeDtypeStruct((9, cn, cz), F32),
        in_specs=[whole(pltpu.SMEM), whole(pl.ANY), whole(pl.ANY), whole(pl.ANY)],
        out_specs=whole(pl.ANY),
        scratch_shapes=[pltpu.SemaphoreType.DMA((3,))],
        cost_estimate=cost(0, 18 * cn * cz * 4),
    )(at.reshape(1), start, flow, eddy)


def swap_faces(low, high, size):
    if size == 2:
        got = lax.ppermute(low, "east", [(0, 1), (1, 0)])
        return got, got
    up = [(i, i + 1) for i in range(size - 1)]
    down = [(i + 1, i) for i in range(size - 1)]
    return lax.ppermute(high, "east", up), lax.ppermute(low, "east", down)


class Shifts:
    def __init__(self, rows, cols):
        self.rows, self.cols = rows, cols
        r = lax.broadcasted_iota(jnp.int32, (rows, cols), 0)
        z = lax.broadcasted_iota(jnp.int32, (rows, cols), 1)
        self.not_top, self.not_bottom = r < rows - 1, r > 0
        self.not_high, self.not_low = z < cols - 1, z > 0

    def north(self, x):
        return (
            jnp.where(self.not_top, pltpu.roll(x, self.rows - 1, 0), 0.0),
            jnp.where(self.not_bottom, pltpu.roll(x, 1, 0), 0.0),
        )

    def level(self, x):
        return (
            jnp.where(self.not_high, pltpu.roll(x, self.cols - 1, 1), 0.0),
            jnp.where(self.not_low, pltpu.roll(x, 1, 1), 0.0),
        )


def sweep(sh, mid, nxt, prv, src, flow, visc, curv):
    u = [flow(k) for k in range(3)]
    w = visc()
    inv_v = 1.0 / (6.0 * w + 1.0)
    out = [None] * 5
    q_next, q_prev = nxt(3), prv(3)
    q = mid(3)
    qn, qs = sh.north(q)
    qu, qd = sh.level(q)
    grad = [q_next - q_prev, qn - qs, qu - qd]
    q_sum = (q_next + q_prev) + (qn + qs) + (qu + qd)
    div = None
    bend = None
    for c in range(3):
        v = mid(c)
        a, b = nxt(c), prv(c)
        n, s = sh.north(v)
        h, l = sh.level(v)
        total = (a + b) + (n + s) + (h + l)
        slope = [a - b, n - s, h - l]
        convect = u[0] * slope[0] + u[1] * slope[1] + u[2] * slope[2]
        out[c] = (src(c) + w * total + 0.5 * (convect - grad[c])) * inv_v
        div = slope[c] if div is None else div + slope[c]
        term = v * curv(c)
        bend = term if bend is None else bend + term
    out[3] = (src(3) + q_sum - 0.5 * div) * (1.0 / 7.0)
    m = mid(4)
    n, s = sh.north(m)
    h, l = sh.level(m)
    m_sum = (nxt(4) + prv(4)) + (n + s) + (h + l)
    out[4] = (src(4) + w * m_sum + 0.25 * bend) / (6.0 * w + 2.0)
    return out


def curvature(sh, u, a, b):
    n, s = sh.north(u)
    h, l = sh.level(u)
    return (a + b) + (n + s) + (h + l) - 6.0 * u


def over_slabs(count, body):
    body(0, True, False)

    @pl.loop(1, count - 1)
    def _(e):
        body(e, False, False)

    body(count - 1, False, True)


def first_kernel(ce, cn, cz, flags, start, source, flow, eddy, facep, facen, swept, curv, pdown, pup, cdown, cup):
    sh = Shifts(cn, cz)
    has_prev, has_next = flags[0], flags[1]

    def body(e, first, last):
        def before(ref, f, face_at):
            if first:
                return facep[face_at] * has_prev
            return ref[f, e - 1]

        def after(ref, f, face_at):
            if last:
                return facen[face_at] * has_next
            return ref[f, e + 1]

        for c in range(3):
            curv[c, e] = curvature(sh, flow[c, e], after(flow, c, 5 + c), before(flow, c, 5 + c))
        out = sweep(
            sh,
            lambda f: start[f, e],
            lambda f: after(start, f, f),
            lambda f: before(start, f, f),
            lambda f: source[f, e],
            lambda k: flow[k, e],
            lambda: 1.0 + eddy[e],
            lambda c: curv[c, e],
        )
        for f in range(5):
            swept[f, e] = out[f]

        for pack, coef, row, behind in ((pdown, cdown, 0, 1), (pup, cup, cn - 1, cn - 2)):
            def put(ref, at, line):
                ref[pl.ds(at * ce + e, 1), :] = line

            for f in range(5):
                put(pack, f, start[f, e, row : row + 1, :])
                put(pack, 9 + f, out[f][row : row + 1, :])
            for k in range(3):
                put(pack, 5 + k, flow[k, e, row : row + 1, :])
                put(coef, k, curv[k, e, row : row + 1, :])
            put(pack, 8, eddy[e, row : row + 1, :])
            put(coef, 3, flow[1, e, behind : behind + 1, :])
            put(coef, 4, eddy[e, behind : behind + 1, :])
            put(coef, 5, flow[0, e, behind : behind + 1, :])

    for pack, row in ((pdown, 0), (pup, cn - 1)):
        for f in range(8):
            pack[PACK * ce + f : PACK * ce + f + 1, :] = facep[f, row : row + 1, :] * has_prev
            pack[PACK * ce + 8 + f : PACK * ce + 9 + f, :] = facen[f, row : row + 1, :] * has_next
    over_slabs(ce, body)


def first_sweep(flags, start, source, flow, eddy, facep, facen):
    _, ce, cn, cz = start.shape
    pack = jax.ShapeDtypeStruct((PACK * ce + 16, cz), F32)
    coef = jax.ShapeDtypeStruct((EDGE * ce, cz), F32)
    return pl.pallas_call(
        functools.partial(first_kernel, ce, cn, cz),
        out_shape=(
            VMEM(start.shape, F32),
            VMEM(flow.shape, F32),
            pack,
            pack,
            coef,
            coef,
        ),
        in_specs=[whole(pltpu.SMEM)] + [whole()] * 6,
        out_specs=(whole(),) * 6,
        compiler_params=params(48),
        cost_estimate=cost(120 * start.size // 5, 20 << 20),
    )(flags, in_vmem(start), in_vmem(source), in_vmem(flow), in_vmem(eddy), facep, facen)


def rotor_terms(cells, row_of, high, low, turbine, sector, weight, count, blocks, acc):
    chunks = cells.shape[0]
    rows, width = high.shape
    cz = width // COMPS
    shift = cz.bit_length() - 1
    cell = cells[...]
    tur = turbine[...]
    owner = lax.shift_right_logical(tur * 5462, 16)
    key = owner * SECT + sector[...]
    slot = lax.broadcasted_iota(jnp.int32, cell.shape, 0) * LANES + lax.broadcasted_iota(jnp.int32, cell.shape, 1)
    live = jnp.where(slot < count, weight[...], 0.0)
    row = row_of(lax.shift_right_logical(cell, shift)).astype(F32).T
    level = jnp.bitwise_and(cell, cz - 1).astype(F32).T
    local = (tur - owner * TURB_DEV).astype(F32).T
    live = live.T
    lane_row = lax.broadcasted_iota(jnp.int32, (LANES, rows), 1).astype(F32)
    lane_level = lax.broadcasted_iota(jnp.int32, (LANES, cz), 1).astype(F32)
    lane = lax.broadcasted_iota(jnp.int32, (LANES, LANES), 1)
    lane_comp = lax.shift_right_logical(lane * 5462, 16)
    lane_tur = (lane - lane_comp * TURB_DEV).astype(F32)
    lane_key = lax.broadcasted_iota(jnp.int32, (blocks * SECT, LANES), 0)
    for k in range(chunks):

        @pl.when(k * LANES < count)
        def _(k=k):
            pick = (row[:, k : k + 1] == lane_row).astype(jnp.bfloat16)
            got = jnp.dot(pick, high[...], preferred_element_type=F32)
            got = got + jnp.dot(pick, low[...], preferred_element_type=F32)
            here = level[:, k : k + 1] == lane_level
            spread = jnp.zeros((LANES, LANES), F32)
            for c in range(COMPS):
                part = jnp.where(here, got[:, c * cz : (c + 1) * cz], 0.0)
                val = jnp.sum(part, axis=1, keepdims=True) * live[:, k : k + 1]
                spread = jnp.where(lane_comp == c, val, spread)
            spread = jnp.where(local[:, k : k + 1] == lane_tur, spread, 0.0)
            to = (lane_key == key[k : k + 1, :]).astype(F32)
            acc[...] += jnp.dot(to, spread, precision=lax.Precision.HIGHEST, preferred_element_type=F32)


def split(x):
    high = x.astype(jnp.bfloat16)
    return high, (x - high.astype(F32)).astype(jnp.bfloat16)


def second_kernel(
    ce, cn, cz, blocks,
    flags, count, swept, curv, source, flow, eddy, facep, facen, cells, turbine, sector, weight,
    final, edge_low, edge_high, grad,
    held, high, low, sems,
):
    sh = Shifts(cn, cz)
    has_prev, has_next = flags[0], flags[1]

    def body(e, first, last):
        def before(f):
            if first:
                return facep[f] * has_prev
            return swept[f, e - 1]

        def after(f):
            if last:
                return facen[f] * has_next
            return swept[f, e + 1]

        out = sweep(
            sh,
            lambda f: swept[f, e],
            after,
            before,
            lambda f: source[f, e],
            lambda k: flow[k, e],
            lambda: 1.0 + eddy[e],
            lambda c: curv[c, e],
        )
        u = flow[0, e]
        force = u * jnp.abs(u)
        at = pl.ds(pl.multiple_of(e * cn, cn), cn)
        for f in range(5):
            held[f, e] = out[f]
            edge_low[f, e] = out[f][0:SUB]
            edge_high[f, e] = out[f][cn - SUB : cn]
        for c in range(COMPS):
            hi, lo = split(out[c if c < 3 else 4] * force)
            high[at, c * cz : (c + 1) * cz] = hi
            low[at, c * cz : (c + 1) * cz] = lo

    over_slabs(ce, body)
    copy = pltpu.make_async_copy(held, final, sems.at[0])
    copy.start()
    grad[...] = jnp.zeros_like(grad)
    rotor_terms(cells, lambda r: r, high, low, turbine, sector, weight, count[0], blocks, grad)
    copy.wait()


def second_sweep(flags, count, swept, curv, source, flow, eddy, facep, facen, lists, blocks):
    _, ce, cn, cz = swept.shape
    edge = VMEM((5, ce, SUB, cz), F32)
    return pl.pallas_call(
        functools.partial(second_kernel, ce, cn, cz, blocks),
        out_shape=(
            jax.ShapeDtypeStruct(swept.shape, F32),
            edge,
            edge,
            jax.ShapeDtypeStruct((blocks * SECT, LANES), F32),
        ),
        in_specs=[whole(pltpu.SMEM)] * 2 + [whole()] * 11,
        out_specs=(whole(pl.ANY), whole(), whole(), whole()),
        scratch_shapes=[
            VMEM(swept.shape, F32),
            VMEM((ce * cn, COMPS * cz), jnp.bfloat16),
            VMEM((ce * cn, COMPS * cz), jnp.bfloat16),
            pltpu.SemaphoreType.DMA((1,)),
        ],
        compiler_params=params(48),
        cost_estimate=cost(140 * swept.size // 5, 20 << 20),
    )(flags, count, in_vmem(swept), in_vmem(curv), in_vmem(source), in_vmem(flow), in_vmem(eddy), facep, facen, *lists)


def one_way(sign, w, u1, f, s, inv_v, inv_m, bend=None):
    down = (w + (0.5 * sign) * u1) * inv_v
    out = [down * f[c] for c in range(3)]
    out[1] = out[1] - (0.5 * sign) * f[3] * inv_v
    out.append((f[3] - (0.5 * sign) * f[1]) * (1.0 / 7.0))
    m = w * f[4]
    if bend is not None:
        m = m + 0.25 * bend
    out.append(m * inv_m)
    return out


def edge_kernel(
    ce, cn, cz, blocks, copies_out,
    flags, count, facep, facen, own_low, own_high, coef_low, coef_high, got_prev, got_next,
    edge_low, edge_high, cells, turbine, sector, weight, grad, final_in,
    final, chunks,
    low_out, high_out, high, low, acc, sems,
):
    z = lax.broadcasted_iota(jnp.int32, (ce, cz), 1)
    r = lax.broadcasted_iota(jnp.int32, (ce, cz), 0)
    sub = lax.broadcasted_iota(jnp.int32, (SUB, cz), 0)
    sides = (
        (-1.0, 0, own_low, coef_low, got_prev, flags[2], edge_low, low_out, 0),
        (1.0, cn - 1, own_high, coef_high, got_next, flags[3], edge_high, high_out, cn - SUB),
    )
    waits = []
    for at_side, (sign, row, own, coef, got, exists, edge, out_ref, place) in enumerate(sides):
        def plane(ref, f):
            return ref[f * ce : (f + 1) * ce, :]

        v0 = [plane(own, f) for f in range(5)]
        u = [plane(own, 5 + k) for k in range(3)]
        w = 1.0 + plane(own, 8)
        p1 = [plane(own, 9 + f) for f in range(5)]
        xv = [plane(got, f) for f in range(5)]
        xu = [plane(got, 5 + k) for k in range(3)]
        xw = 1.0 + plane(got, 8)
        xp = [plane(got, 9 + f) for f in range(5)]
        curv = [plane(coef, k) for k in range(3)]
        inv_v, inv_m = 1.0 / (6.0 * w + 1.0), 1.0 / (6.0 * w + 2.0)
        bend = v0[0] * xu[0] + v0[1] * xu[1] + v0[2] * xu[2]
        delta = one_way(sign, w, u[1], xv, None, inv_v, inv_m, bend)
        xinv_v, xinv_m = 1.0 / (6.0 * xw + 1.0), 1.0 / (6.0 * xw + 2.0)
        xbend = xv[0] * u[0] + xv[1] * u[1] + xv[2] * u[2]
        back = one_way(-sign, xw, xu[1], v0, None, xinv_v, xinv_m, xbend)
        x1 = [(xp[f] + back[f]) * exists for f in range(5)]
        ends = []
        for face, has, first in ((facep, flags[0], 0), (facen, flags[1], 8)):
            fv = [face[f, row : row + 1, :] * has for f in range(5)]
            fu = face[6, row : row + 1, :] * has
            fw = 1.0 + face[8, row : row + 1, :] * has
            base = PACK * ce + first
            hv = [got[base + f : base + f + 1, :] for f in range(5)]
            hu = [got[base + 5 + k : base + 6 + k, :] for k in range(3)]
            fb = fv[0] * hu[0] + fv[1] * hu[1] + fv[2] * hu[2]
            line = one_way(sign, fw, fu, hv, None, 1.0 / (6.0 * fw + 1.0), 1.0 / (6.0 * fw + 2.0), fb)
            ends.append([x * has for x in line])
        total, slope0, slope2 = [], [], []
        for f in range(5):
            d = delta[f]
            after = jnp.where(r < ce - 1, pltpu.roll(d, ce - 1, 0), ends[1][f])
            before = jnp.where(r > 0, pltpu.roll(d, 1, 0), ends[0][f])
            up = jnp.where(z < cz - 1, pltpu.roll(d, cz - 1, 1), 0.0)
            down = jnp.where(z > 0, pltpu.roll(d, 1, 1), 0.0)
            total.append((after + before) + (up + down))
            slope0.append(after - before)
            slope2.append(up - down)
        full = [p1[c] + delta[c] for c in range(3)]
        bend = full[0] * xu[0] + full[1] * xu[1] + full[2] * xu[2]
        bend = bend + delta[0] * curv[0] + delta[1] * curv[1] + delta[2] * curv[2]
        add = one_way(sign, w, u[1], x1, None, inv_v, inv_m, bend)
        press = (slope0[3], None, slope2[3])
        for c in range(3):
            more = w * total[c] + 0.5 * (u[0] * slope0[c] + u[2] * slope2[c])
            if press[c] is not None:
                more = more - 0.5 * press[c]
            add[c] = add[c] + more * inv_v
        add[3] = add[3] + (total[3] - 0.5 * (slope0[0] + slope2[2])) * (1.0 / 7.0)
        add[4] = add[4] + w * total[4] * inv_m
        ru1, rw, ru0 = plane(coef, 3), 1.0 + plane(coef, 4), plane(coef, 5)
        rinv_v, rinv_m = 1.0 / (6.0 * rw + 1.0), 1.0 / (6.0 * rw + 2.0)
        behind = one_way(sign, rw, ru1, delta, None, rinv_v, rinv_m)
        near, far = (0, 1) if at_side == 0 else (SUB - 1, SUB - 2)
        for f in range(5):
            for e in range(ce):
                rows = jnp.where(
                    sub == near, add[f][e : e + 1, :], jnp.where(sub == far, behind[f][e : e + 1, :], 0.0)
                )
                out_ref[f, e] = edge[f, e] + rows
        copy = pltpu.make_async_copy(out_ref, final.at[:, :, pl.ds(place, SUB), :], sems.at[at_side])
        copy.start()
        waits.append(copy)
        for source_row, u0, values in ((0, u[0], add), (1, ru0, behind)):
            force = u0 * jnp.abs(u0)
            at = (2 * at_side + source_row) * ce
            for c in range(COMPS):
                hi, lo = split(values[c if c < 3 else 4] * force)
                high[at : at + ce, c * cz : (c + 1) * cz] = hi
                low[at : at + ce, c * cz : (c + 1) * cz] = lo

    shift = cn.bit_length() - 1

    def row_of(line):
        n = jnp.bitwise_and(line, cn - 1)
        e = lax.shift_right_logical(line, shift)
        slot = jnp.where(n == 0, 0, jnp.where(n == 1, 1, jnp.where(n == cn - 1, 2, jnp.where(n == cn - 2, 3, -ce))))
        return slot * ce + e

    acc[...] = grad[...]
    rotor_terms(cells, row_of, high, low, turbine, sector, weight, count[0], blocks, acc)
    for east in range(copies_out):
        chunks[east] = acc[...]
    for copy in waits:
        copy.wait()


def edges(flags, count, faces, packs, coefs, gots, tiles, lists, grad, final, blocks, size):
    _, ce, cn, cz = final.shape
    args = (flags, count, *faces, *packs, *coefs, *gots, *tiles, *lists, grad, final)
    tile = VMEM((5, ce, SUB, cz), F32)
    part = VMEM((4 * ce, COMPS * cz), jnp.bfloat16)
    return pl.pallas_call(
        functools.partial(edge_kernel, ce, cn, cz, blocks, size),
        out_shape=(
            jax.ShapeDtypeStruct(final.shape, F32),
            jax.ShapeDtypeStruct((size, blocks * SECT, LANES), F32),
        ),
        in_specs=[whole(pltpu.SMEM)] * 2 + [whole()] * (len(args) - 3) + [whole(pl.ANY)],
        out_specs=(whole(pl.ANY), whole()),
        scratch_shapes=[
            tile,
            tile,
            part,
            part,
            VMEM((blocks * SECT, LANES), F32),
            pltpu.SemaphoreType.DMA((2,)),
        ],
        input_output_aliases={len(args) - 1: 0},
        compiler_params=params(32),
        cost_estimate=cost(1 << 24, 4 << 20),
    )(*args)


def sum_kernel(parts, out):
    total = jnp.sum(parts[...], axis=0)
    for c in range(COMPS):
        out[c] = total[:, c * TURB_DEV : (c + 1) * TURB_DEV]


def sum_parts(parts):
    return pl.pallas_call(
        sum_kernel,
        out_shape=jax.ShapeDtypeStruct((COMPS, SECT, TURB_DEV), F32),
        in_specs=[whole()],
        out_specs=whole(),
        cost_estimate=cost(parts.size, parts.size * 4),
    )(parts)


def shards(
    adjoint_start,
    adjoint_source,
    base_flow,
    eddy_visc,
    rotor_count,
    rotor_cell,
    rotor_turbine,
    rotor_sector,
    rotor_weight,
):
    _, ce, cn, cz = adjoint_start.shape
    n_east, n_north = lax.axis_size("east"), lax.axis_size("north")
    east, north = lax.axis_index("east"), lax.axis_index("north")
    flags = jnp.stack([east > 0, east < n_east - 1, north > 0, north < n_north - 1]).astype(F32)
    count = rotor_count.reshape(1)
    slots = rotor_cell.shape[-1]
    lists = [x.reshape(slots // LANES, LANES) for x in (rotor_cell, rotor_turbine, rotor_sector, rotor_weight)]

    facing = jnp.where(east == 0, ce - 1, 0).astype(jnp.int32)
    if n_east == 2:
        low = high = east_face(facing, adjoint_start, base_flow, eddy_visc)
    else:
        low, high = (
            east_face(jnp.asarray(e, jnp.int32), adjoint_start, base_flow, eddy_visc) for e in (0, ce - 1)
        )
    faces = swap_faces(low, high, n_east)
    swept, curv, pack_low, pack_high, coef_low, coef_high = first_sweep(
        flags, adjoint_start, adjoint_source, base_flow, eddy_visc, *faces
    )
    up = [(i, i + 1) for i in range(n_north - 1)]
    down = [(i + 1, i) for i in range(n_north - 1)]
    got_prev = lax.ppermute(pack_high, "north", up)
    got_next = lax.ppermute(pack_low, "north", down)
    if n_east == 2:
        low = high = lax.dynamic_index_in_dim(swept, facing, 1, keepdims=False)
    else:
        low, high = swept[:, 0], swept[:, ce - 1]
    faces_swept = swap_faces(low, high, n_east)
    final, edge_low, edge_high, grad = second_sweep(
        flags, count, swept, curv, adjoint_source, base_flow, eddy_visc, *faces_swept, lists, n_north
    )
    final, chunks = edges(
        flags, count, faces, (pack_low, pack_high), (coef_low, coef_high), (got_prev, got_next),
        (edge_low, edge_high), lists, grad, final, n_north, n_east,
    )
    chunks = chunks.reshape(n_east * n_north, SECT, LANES)
    parts = lax.all_to_all(chunks, ("east", "north"), 0, 0, tiled=True)
    return (final, sum_parts(parts))


def solution(mesh):
    placed = (
        P(None, "east", "north", None),
        P(None, "east", "north", None),
        P(None, "east", "north", None),
        P("east", "north", None),
        P("east", "north"),
        P("east", "north", None),
        P("east", "north", None),
        P("east", "north", None),
        P("east", "north", None),
    )
    return jax.shard_map(
        shards,
        mesh=mesh,
        in_specs=placed,
        out_specs=(P(None, "east", "north", None), P(None, None, "north")),
        check_vma=False,
    )
```

```python
import functools

import jax
import jax.numpy as jnp
from jax import lax
from jax.experimental import pallas as pl
from jax.experimental.pallas import tpu as pltpu
from jax.sharding import PartitionSpec as P

SECT = 8
TURB_DEV = 12
COMPS = 4
LANES = 128
SUB = 8
PAD = 8
PACK = 14
FACE = 22
EDGE = 9
ITEM = 8
BLOCK = 256
VMEM = pltpu.VMEM
F32 = jnp.float32
BF16 = jnp.bfloat16


def whole(space=VMEM):
    return pl.BlockSpec(memory_space=space)


def shape(*dims):
    return jax.ShapeDtypeStruct(dims, F32)


def params(mib):
    return pltpu.CompilerParams(vmem_limit_bytes=mib << 20)


def cost(flops, size):
    return pl.CostEstimate(flops=flops, bytes_accessed=size, transcendentals=0)


class Copies:
    def __init__(self, sems):
        self.sems, self.used = sems, 0

    def take(self, *pairs):
        first = self.used
        self.used += len(pairs)
        return first, pairs

    def made(self, taken):
        first, pairs = taken
        return [pltpu.make_async_copy(s, d, self.sems.at[first + k]) for k, (s, d) in enumerate(pairs)]

    def start(self, taken):
        for c in self.made(taken):
            c.start()

    def wait(self, taken):
        for c in self.made(taken):
            c.wait()


def one_way(k, sign, w, u, f, inv_v, inv_m, bend=None):
    pull = (w + (0.5 * sign) * u) * inv_v
    out = [pull * f[c] for c in range(3)]
    out[k] = out[k] - (0.5 * sign) * f[3] * inv_v
    out.append((f[3] - (0.5 * sign) * f[k]) * (1.0 / 7.0))
    m = w * f[4]
    if bend is not None:
        m = m + 0.25 * bend
    out.append(m * inv_m)
    return out


def inverses(w):
    return 1.0 / (6.0 * w + 1.0), 1.0 / (6.0 * w + 2.0)


def dot3(a, b):
    return a[0] * b[0] + a[1] * b[1] + a[2] * b[2]


def plane_shifts(rows, cols):
    r = lax.broadcasted_iota(jnp.int32, (rows, cols), 0)
    z = lax.broadcasted_iota(jnp.int32, (rows, cols), 1)

    def east(x, before=0.0, after=0.0):
        return (
            jnp.where(r < rows - 1, pltpu.roll(x, rows - 1, 0), after),
            jnp.where(r > 0, pltpu.roll(x, 1, 0), before),
        )

    def level(x):
        return (
            jnp.where(z < cols - 1, pltpu.roll(x, cols - 1, 1), 0.0),
            jnp.where(z > 0, pltpu.roll(x, 1, 1), 0.0),
        )

    return east, level


def ends_kernel(cn, n_faces, at, start, flow, *refs):
    outs, tiles_v, tiles_u, sems = refs[:n_faces], *refs[n_faces:]
    copies = Copies(sems)
    taken = []
    for i in range(n_faces):
        e = at[2 * i]
        pairs = []
        for side, first in enumerate((0, cn - SUB)):
            pairs.append((start.at[:, e, pl.ds(first, SUB)], tiles_v.at[i, side]))
            pairs.append((flow.at[:, e, pl.ds(first, SUB)], tiles_u.at[i, side]))
        taken.append(copies.take(*pairs))
        copies.start(taken[-1])
    for i, out in enumerate(outs):
        copies.wait(taken[i])
        for side, row in enumerate((0, SUB - 1)):
            for f in range(8):
                tile = tiles_v[i, side, f] if f < 5 else tiles_u[i, side, f - 5]
                out[side * 8 + f : side * 8 + f + 1, :] = tile[row : row + 1]


def row_ends(at, start, flow, n_faces):
    _, ce, cn, cz = start.shape
    return pl.pallas_call(
        functools.partial(ends_kernel, cn, n_faces),
        out_shape=[shape(16, cz)] * n_faces,
        in_specs=[whole(pltpu.SMEM)] + [whole(pltpu.HBM)] * 2,
        out_specs=[whole()] * n_faces,
        scratch_shapes=[
            VMEM((n_faces, 2, 5, SUB, cz), F32),
            VMEM((n_faces, 2, 3, SUB, cz), F32),
            pltpu.SemaphoreType.DMA((4 * n_faces,)),
        ],
        compiler_params=params(60),
        cost_estimate=cost(0, 1 << 16),
    )(at, start, flow)


def pack_kernel(ce, cn, cz, n_faces, at, flags, endp, endn, start, source, flow, eddy, *refs):
    packs, refs = refs[:2], refs[2:]
    faces, refs = refs[:n_faces], refs[n_faces:]
    tiles_v, tiles_u, tiles_s, tiles_e, sems = refs
    has = [flags[k].astype(F32) for k in range(2)]
    copies = Copies(sems)
    sides = ((0, 0, 1, -1.0), (cn - SUB, SUB - 1, SUB - 2, 1.0))
    needed = []
    for side, (first, _, _, _) in enumerate(sides):
        pairs = []
        for h in range(2):
            cut = (pl.ds(first, SUB), pl.ds(h * LANES, LANES))
            pairs += [
                (start.at[(slice(None), slice(None)) + cut], tiles_v.at[side, :, :, h]),
                (flow.at[(slice(None), slice(None)) + cut], tiles_u.at[side, :, :, h]),
                (eddy.at[(slice(None),) + cut], tiles_e.at[side, 0, :, h]),
                (source.at[(slice(None), slice(None)) + cut], tiles_s.at[side, :, :, h]),
            ]
        needed.append(copies.take(*pairs))
        copies.start(needed[-1])
    later = []
    for i in range(n_faces):
        near, far, face = at[2 * i], at[2 * i + 1], faces[i]
        taken = copies.take(
            (start.at[:, near], face.at[0:5]),
            (flow.at[:, near], face.at[5:8]),
            (eddy.at[near], face.at[8]),
            (source.at[:, near], face.at[9:14]),
            (start.at[:, far], face.at[14:19]),
            (flow.at[:, far], face.at[19:22]),
        )
        copies.start(taken)
        later.append(taken)
    east, level = plane_shifts(ce, cz)

    def line(ref, side, f, row):
        flat = ref.reshape(2, ref.shape[1], ce * 2 * SUB, LANES)
        return jnp.concatenate([flat[side, f, pl.ds(h * SUB + row, ce, stride=2 * SUB), :] for h in range(2)], axis=1)

    for side, (_, row, behind, sign) in enumerate(sides):
        copies.wait(needed[side])
        pack = packs[side]
        v = [line(tiles_v, side, f, row) for f in range(5)]
        u = [line(tiles_u, side, k, row) for k in range(3)]
        eddy_row = line(tiles_e, side, 0, row)
        inner = [line(tiles_v, side, f, behind) for f in range(5)]
        inner_u = [line(tiles_u, side, k, behind) for k in range(3)]
        src = [line(tiles_s, side, f, row) for f in range(5)]
        for f, x in enumerate(v + u + [eddy_row]):
            pack[f * ce : (f + 1) * ce, :] = x
        w = 1.0 + eddy_row
        inv_v, inv_m = inverses(w)
        before = [endp[side * 8 + f : side * 8 + f + 1, :] * has[0] for f in range(8)]
        after = [endn[side * 8 + f : side * 8 + f + 1, :] * has[1] for f in range(8)]
        for f in range(8):
            pack[PACK * ce + f : PACK * ce + f + 1, :] = before[f]
            pack[PACK * ce + 8 + f : PACK * ce + 9 + f, :] = after[f]
        total, slope0, slope2 = [], [], []
        for f in range(5):
            a, b = east(v[f], before[f], after[f])
            h, l = level(v[f])
            total.append((a + b) + (h + l))
            slope0.append(a - b)
            slope2.append(h - l)
        curv = []
        for k in range(3):
            a, b = east(u[k], before[5 + k], after[5 + k])
            h, l = level(u[k])
            curv.append((a + b) + (h + l) + inner_u[k] - 6.0 * u[k])
        out = one_way(1, -sign, w, u[1], inner, inv_v, inv_m, dot3(v, curv))
        press = (slope0[3], None, slope2[3])
        for c in range(3):
            more = src[c] + w * total[c] + 0.5 * (u[0] * slope0[c] + u[2] * slope2[c])
            if press[c] is not None:
                more = more - 0.5 * press[c]
            out[c] = out[c] + more * inv_v
        out[3] = out[3] + (src[3] + total[3] - 0.5 * (slope0[0] + slope2[2])) * (1.0 / 7.0)
        out[4] = out[4] + (src[4] + w * total[4]) * inv_m
        for f in range(5):
            pack[(9 + f) * ce : (10 + f) * ce, :] = out[f]
    for taken in later:
        copies.wait(taken)


def pack(at, flags, ends, start, source, flow, eddy, n_faces):
    _, ce, cn, cz = start.shape
    out = [shape(PACK * ce + 16, cz)] * 2 + [shape(FACE, cn, cz)] * n_faces
    got = pl.pallas_call(
        functools.partial(pack_kernel, ce, cn, cz, n_faces),
        out_shape=out,
        in_specs=[whole(pltpu.SMEM)] * 2 + [whole()] * 2 + [whole(pltpu.HBM)] * 4,
        out_specs=[whole()] * len(out),
        scratch_shapes=[
            VMEM((2, 5, ce, 2, SUB, LANES), F32),
            VMEM((2, 3, ce, 2, SUB, LANES), F32),
            VMEM((2, 5, ce, 2, SUB, LANES), F32),
            VMEM((2, 1, ce, 2, SUB, LANES), F32),
            pltpu.SemaphoreType.DMA((16 + 6 * n_faces,)),
        ],
        compiler_params=params(60),
        cost_estimate=cost(1 << 22, 4 << 20),
    )(at, flags, *ends, start, source, flow, eddy)
    return got[:2], got[2:]


def split(x):
    high = x.astype(BF16)
    return high, (x - high.astype(F32)).astype(BF16)


def owner_of(turbine):
    return lax.shift_right_logical(turbine * 5462, 16)


def columns(x, first, size):
    return jnp.concatenate([x[:, k : k + 1] for k in range(first // LANES, (first + size) // LANES)], axis=0)


def lines(x, first, size):
    return jnp.concatenate([x[k : k + 1, :] for k in range(first // LANES, (first + size) // LANES)], axis=1)


def rotor_terms(row, level, turbine, weight, key, table, blocks, acc):
    size = row.shape[0]
    rows, width = table.shape[0] // 2, table.shape[1]
    cz = width // COMPS
    lane_row = lax.broadcasted_iota(jnp.int32, (size, rows), 1).astype(F32)
    pick = jnp.where(row == lane_row, 1.0, 0.0).astype(BF16)
    got = jnp.dot(jnp.concatenate([pick, pick], axis=1), table[...], preferred_element_type=F32)
    here = level == lax.broadcasted_iota(jnp.int32, (size, cz), 1).astype(F32)
    lane = lax.broadcasted_iota(jnp.int32, (size, LANES), 1)
    lane_comp = owner_of(lane)
    lane_tur = (lane - lane_comp * TURB_DEV).astype(F32)
    spread = jnp.zeros((size, LANES), F32)
    for c in range(COMPS):
        part = jnp.where(here, got[:, c * cz : (c + 1) * cz], 0.0)
        spread = jnp.where(lane_comp == c, jnp.sum(part, axis=1, keepdims=True), spread)
    spread = jnp.where(turbine == lane_tur, spread * weight, 0.0)
    lane_key = lax.broadcasted_iota(jnp.int32, (blocks * SECT, size), 0).astype(F32)
    to = jnp.where(lane_key == key, 1.0, 0.0).astype(BF16)
    high = spread.astype(BF16)
    rest = spread - high.astype(F32)
    mid, low = split(rest)
    parts = jnp.dot(to, jnp.concatenate([high, mid, low], axis=1), preferred_element_type=F32)
    acc[...] += parts[:, :LANES] + parts[:, LANES : 2 * LANES] + parts[:, 2 * LANES :]


def halves(ref, f, i, cn, move=0):
    return [ref[f, i, h, pl.ds(PAD + move, cn), :] for h in range(2)]


def level_shifts(x, first, last):
    up = [pltpu.roll(x[h], LANES - 1, 1) for h in range(2)]
    down = [pltpu.roll(x[h], 1, 1) for h in range(2)]
    return (
        [jnp.where(last, up[1], up[0]), jnp.where(last, 0.0, up[1])],
        [jnp.where(first, 0.0, down[0]), jnp.where(first, down[0], down[1])],
    )


def slab_sweep(ref, i, cn, first, last, src, flow, visc, curv):
    two = range(2)
    w = visc
    inv = [inverses(w[h]) for h in two]
    w2 = [2.0 * w[h] for h in two]

    def sides(f):
        mid = halves(ref, f, i, cn)
        a, b = halves(ref, f, i + 1, cn), halves(ref, f, i - 1, cn)
        n, s = halves(ref, f, i, cn, 1), halves(ref, f, i, cn, -1)
        up, down = level_shifts(mid, first, last)
        return mid, a, b, n, s, up, down

    _, a, b, n, s, up, down = sides(3)
    grad = [[x[h] - y[h] for h in two] for x, y in ((a, b), (n, s), (up, down))]
    q_sum = [(a[h] + b[h]) + (n[h] + s[h]) + (up[h] + down[h]) for h in two]
    out, div, bend = [], [0.0, 0.0], [0.0, 0.0]
    for c in range(3):
        mid, a, b, n, s, up, down = sides(c)
        res = []
        for h in two:
            total = (a[h] + b[h]) + (n[h] + s[h]) + (up[h] + down[h])
            slope = [a[h] - b[h], n[h] - s[h], up[h] - down[h]]
            carried = flow[0][h] * slope[0] + flow[1][h] * slope[1] + flow[2][h] * slope[2]
            res.append((src(c)[h] + 0.5 * (w2[h] * total + (carried - grad[c][h]))) * inv[h][0])
            div[h] = div[h] + slope[c]
            bend[h] = bend[h] + mid[h] * curv[c][h]
        out.append(res)
    out.append([(src(3)[h] + q_sum[h] - 0.5 * div[h]) * (1.0 / 7.0) for h in two])
    _, a, b, n, s, up, down = sides(4)
    res = []
    for h in two:
        total = (a[h] + b[h]) + (n[h] + s[h]) + (up[h] + down[h])
        res.append((src(4)[h] + w[h] * total + 0.25 * bend[h]) * inv[h][1])
    out.append(res)
    return out


def sweeps_kernel(
    ce, cn, cz, blocks,
    flags, count, start, source, flow, eddy, facep, facen, cells, turbine, sector, weight,
    final, edge_low, edge_high, coef_low, coef_high, grad, items, n_items,
    v0, u, src, ed, v1, curv, held, table, sems,
):
    copies = Copies(sems)
    two = range(2)
    has = (flags[0] > 0, flags[1] > 0)
    inner = pl.ds(PAD, cn)

    def part(h):
        return pl.ds(h * LANES, LANES)

    def halo(face, near, far, slab):
        pairs = []
        for h in two:
            pairs += [
                (face.at[0:5, :, part(h)], v0.at[:, near, h, inner]),
                (face.at[5:8, :, part(h)], u.at[:, near, h, inner]),
                (face.at[8, :, part(h)], ed.at[slab, h]),
                (face.at[9:14, :, part(h)], src.at[:, slab, h]),
                (face.at[14:19, :, part(h)], v0.at[:, far, h, inner]),
                (face.at[19:22, :, part(h)], u.at[:, far, h, inner]),
            ]
        return pairs

    ends = ((facep, 1, 0, 0), (facen, ce + 2, ce + 3, ce + 1))
    halos = []
    for exists, (face, near, far, slab) in zip(has, ends):
        taken = copies.take(*halo(face, near, far, slab))
        halos.append(taken)

        @pl.when(exists)
        def _():
            copies.start(taken)

    step = 4
    groups = []
    for g in range(0, ce, step):
        span, own, own2 = pl.ds(g, step), pl.ds(g + 1, step), pl.ds(g + 2, step)
        pairs = []
        for h in two:
            pairs += [
                (start.at[:, span, :, part(h)], v0.at[:, own2, h, inner]),
                (flow.at[:, span, :, part(h)], u.at[:, own2, h, inner]),
                (eddy.at[span, :, part(h)], ed.at[own, h]),
                (source.at[:, span, :, part(h)], src.at[:, own, h]),
            ]
        groups.append(copies.take(*pairs))
        copies.start(groups[-1])

    blank = jnp.zeros((PAD, LANES), F32)
    for ref, fields in ((v0, 5), (u, 3), (v1, 5)):

        @pl.loop(0, ref.shape[1])
        def _(i):
            for f in range(fields):
                for h in two:
                    ref[f, i, h, 0:PAD, :] = blank
                    ref[f, i, h, PAD + cn : PAD + cn + PAD, :] = blank

    for exists, (_, near, _, _) in zip(has, ends):

        @pl.when(jnp.logical_not(exists))
        def _():
            for ref, fields in ((v0, 5), (u, 3)):
                for f in range(fields):
                    for h in two:
                        ref[f, near, h, inner, :] = jnp.zeros((cn, LANES), F32)

    lane = lax.broadcasted_iota(jnp.int32, (cn, LANES), 1)
    first, last = lane == 0, lane == LANES - 1

    for exists, taken in zip(has, halos):

        @pl.when(exists)
        def _():
            copies.wait(taken)

    copies.wait(groups[0])
    copies.wait(groups[1])

    @pl.loop(0, ce + 2)
    def _(i):
        for g in range(2, len(groups)):

            @pl.when(i == 1 + step * (g - 1))
            def _():
                copies.wait(groups[g])

        real = jnp.logical_and(
            jnp.logical_or(i > 0, has[0]), jnp.logical_or(i < ce + 1, has[1])
        )

        @pl.when(real)
        def _():
            mid = i + 1
            flows = [halves(u, k, mid, cn) for k in range(3)]
            bends = []
            for k in range(3):
                a, b = halves(u, k, mid + 1, cn), halves(u, k, mid - 1, cn)
                n, s = halves(u, k, mid, cn, 1), halves(u, k, mid, cn, -1)
                up, down = level_shifts(flows[k], first, last)
                res = [(a[h] + b[h]) + (n[h] + s[h]) + (up[h] + down[h]) - 6.0 * flows[k][h] for h in two]
                for h in two:
                    curv[k, i, h] = res[h]
                bends.append(res)
            out = slab_sweep(
                v0, mid, cn, first, last,
                lambda f: [src[f, i, h] for h in two],
                flows, [1.0 + ed[i, h] for h in two], bends,
            )
            for f in range(5):
                for h in two:
                    v1[f, i, h, inner, :] = out[f][h]

        @pl.when(jnp.logical_not(real))
        def _():
            for f in range(5):
                for h in two:
                    v1[f, i, h, inner, :] = jnp.zeros((cn, LANES), F32)

    @pl.loop(0, ce)
    def _(e):
        i = e + 1
        flows = [halves(u, k, i + 1, cn) for k in range(3)]
        bends = [[curv[k, i, h] for h in two] for k in range(3)]
        out = slab_sweep(
            v1, i, cn, first, last,
            lambda f: [src[f, i, h] for h in two],
            flows, [1.0 + ed[i, h] for h in two], bends,
        )
        def put(coef, k, line):
            coef[pl.ds(k * ce + e, 1), :] = jnp.concatenate(line, axis=1)

        at = pl.ds(pl.multiple_of(e * cn, cn), cn)
        below = pl.ds(pl.multiple_of((ce + e) * cn, cn), cn)
        for h in two:
            force = flows[0][h] * jnp.abs(flows[0][h])
            for f in range(5):
                held[f, e, :, part(h)] = out[f][h]
                edge_low[f, e, :, part(h)] = out[f][h][0:SUB]
                edge_high[f, e, :, part(h)] = out[f][h][cn - SUB : cn]
            for c in range(COMPS):
                hi, lo = split(out[c if c < 3 else 4][h] * force)
                wide = pl.ds(c * cz + h * LANES, LANES)
                table[at, wide] = hi
                table[below, wide] = lo
        for coef, row, behind in ((coef_low, 0, 1), (coef_high, cn - 1, cn - 2)):
            for k in range(3):
                put(coef, k, [bends[k][h][row : row + 1] for h in two])
                put(coef, 6 + k, [v1[k, i, h, PAD + row : PAD + row + 1, :] for h in two])
            put(coef, 3, [flows[1][h][behind : behind + 1] for h in two])
            put(coef, 4, [ed[i, h, behind : behind + 1, :] for h in two])
            put(coef, 5, [flows[0][h][behind : behind + 1] for h in two])

    done = copies.take((held, final))
    copies.start(done)

    live = count[0]
    cell, tur = cells[...], turbine[...]
    owner = owner_of(tur)
    key = (owner * SECT + sector[...]).astype(F32)
    local = (tur - owner * TURB_DEV).astype(F32)
    chunks = cell.shape[0]
    slot = lax.broadcasted_iota(jnp.int32, cell.shape, 0) * LANES + lax.broadcasted_iota(jnp.int32, cell.shape, 1)
    load = jnp.where(slot < live, weight[...], 0.0)
    line = lax.shift_right_logical(cell, cz.bit_length() - 1)
    level = jnp.bitwise_and(cell, cz - 1).astype(F32)
    north = jnp.bitwise_and(line, cn - 1)
    east = lax.shift_right_logical(line, cn.bit_length() - 1)
    place = jnp.where(north == 0, 0, jnp.where(north == 1, 1, jnp.where(north == cn - 1, 2, 3)))
    is_edge = jnp.logical_or(north <= 1, north >= cn - 2)
    chosen = jnp.where(jnp.logical_and(is_edge, slot < live), 1.0, 0.0)
    edge_row = (place * ce + east).astype(F32)

    lower = lax.broadcasted_iota(jnp.int32, (LANES, LANES), 0) < lax.broadcasted_iota(jnp.int32, (LANES, LANES), 1)
    rank = jnp.dot(chosen.astype(BF16), jnp.where(lower, 1.0, 0.0).astype(BF16), preferred_element_type=F32)
    sums = jnp.sum(chosen, axis=1, keepdims=True)
    so_far = jnp.zeros((1, 1), F32)
    starts = []
    for k in range(chunks):
        starts.append(so_far)
        so_far = so_far + sums[k : k + 1]
    rank = jnp.where(chosen > 0.0, rank + jnp.concatenate(starts, axis=0), -1.0)
    total = jnp.sum(chosen).astype(jnp.int32)
    n_items[0] = total
    load_high = load.astype(BF16).astype(F32)
    load_rest = load - load_high
    load_mid = load_rest.astype(BF16).astype(F32)
    load_low = load_rest - load_mid
    blank = jnp.zeros((1, LANES), F32)
    rows = [
        jnp.concatenate([x[k : k + 1] for x in (edge_row, level, key, local, load_high, load_mid, load_low)] + [blank])
        for k in range(chunks)
    ]
    to = lax.broadcasted_iota(jnp.int32, (LANES, LANES), 0).astype(F32)
    items[...] = jnp.zeros_like(items)
    for q in range(chunks):

        @pl.when(q * LANES < total)
        def _():
            where = jnp.concatenate(
                [jnp.where(rank[k : k + 1] - float(q * LANES) == to, 1.0, 0.0) for k in range(chunks)], axis=1
            ).astype(BF16)
            entries = jnp.concatenate(rows, axis=1).astype(BF16)
            items[q] = lax.dot_general(entries, where, (((1,), (1,)), ((), ())), preferred_element_type=F32)

    row_t, level_t, local_t, load_t = line.astype(F32).T, level.T, local.T, load.T
    grad[...] = jnp.zeros_like(grad)
    size = min(BLOCK, chunks * LANES)
    for base in range(0, chunks * LANES, size):

        @pl.when(base < live)
        def _():
            cols = [columns(x, base, size) for x in (row_t, level_t, local_t, load_t)]
            rotor_terms(*cols, lines(key, base, size), table, blocks, grad)

    copies.wait(done)


def sweeps(flags, count, start, source, flow, eddy, faces, lists, blocks):
    _, ce, cn, cz = start.shape
    chunks = lists[0].shape[0]
    edge = shape(5, ce, SUB, cz)
    return pl.pallas_call(
        functools.partial(sweeps_kernel, ce, cn, cz, blocks),
        out_shape=(
            shape(*start.shape),
            edge,
            edge,
            shape(EDGE * ce, cz),
            shape(EDGE * ce, cz),
            shape(blocks * SECT, LANES),
            shape(chunks, ITEM, LANES),
            jax.ShapeDtypeStruct((1,), jnp.int32),
        ),
        in_specs=[whole(pltpu.SMEM)] * 2 + [whole(pltpu.HBM)] * 6 + [whole()] * 4,
        out_specs=(whole(pltpu.HBM),) + (whole(),) * 6 + (whole(pltpu.SMEM),),
        scratch_shapes=[
            VMEM((5, ce + 4, 2, PAD + cn + PAD, LANES), F32),
            VMEM((3, ce + 4, 2, PAD + cn + PAD, LANES), F32),
            VMEM((5, ce + 2, 2, cn, LANES), F32),
            VMEM((ce + 2, 2, cn, LANES), F32),
            VMEM((5, ce + 2, 2, PAD + cn + PAD, LANES), F32),
            VMEM((3, ce + 2, 2, cn, LANES), F32),
            VMEM(start.shape, F32),
            VMEM((2 * ce * cn, COMPS * cz), BF16),
            pltpu.SemaphoreType.DMA((24 + 8 * (ce // 4) + 1,)),
        ],
        compiler_params=params(48),
        cost_estimate=cost(300 * start.size // 5, 10 << 20),
    )(flags, count, start, source, flow, eddy, *faces, *lists)


def edge_kernel(
    ce, cn, cz, blocks, copies_out,
    flags, n_items, facep, facen, own_low, own_high, coef_low, coef_high, got_prev, got_next,
    edge_low, edge_high, items, grad, final_in,
    final, chunks,
    low_out, high_out, table, acc, sems,
):
    east, level = plane_shifts(ce, cz)
    sub = lax.broadcasted_iota(jnp.int32, (SUB, cz), 0)
    has = [flags[k].astype(F32) for k in range(4)]
    sides = (
        (-1.0, 0, own_low, coef_low, got_prev, edge_low, low_out, 0),
        (1.0, cn - 1, own_high, coef_high, got_next, edge_high, high_out, cn - SUB),
    )
    waits = []
    for side, (sign, row, own, coef, got, edge, out_ref, place) in enumerate(sides):

        def plane(ref, f):
            return ref[f * ce : (f + 1) * ce, :]

        v0 = [plane(own, f) for f in range(5)]
        u = [plane(own, 5 + k) for k in range(3)]
        w = 1.0 + plane(own, 8)
        xv = [plane(got, f) for f in range(5)]
        xu = [plane(got, 5 + k) for k in range(3)]
        xw = 1.0 + plane(got, 8)
        xp = [plane(got, 9 + f) for f in range(5)]
        curv = [plane(coef, k) for k in range(3)]
        inv_v, inv_m = inverses(w)
        delta = one_way(1, sign, w, u[1], xv, inv_v, inv_m, dot3(v0, xu))
        back = one_way(1, -sign, xw, xu[1], v0, *inverses(xw), dot3(xv, u))
        x1 = [xp[f] + back[f] for f in range(5)]
        ends = []
        for far, face in enumerate((facep, facen)):
            hv = [got[PACK * ce + 8 * far + f : PACK * ce + 8 * far + f + 1, :] for f in range(8)]
            fv = [face[f, row : row + 1, :] * has[far] for f in range(5)]
            fu = face[6, row : row + 1, :] * has[far]
            fw = 1.0 + face[8, row : row + 1, :] * has[far]
            ends.append(one_way(1, sign, fw, fu, hv, *inverses(fw), dot3(fv, hv[5:])))
        x1 = [x * has[2 + side] for x in x1]
        total, slope0, slope2 = [], [], []
        for f in range(5):
            a, b = east(delta[f], ends[0][f], ends[1][f])
            h, l = level(delta[f])
            total.append((a + b) + (h + l))
            slope0.append(a - b)
            slope2.append(h - l)
        full = [plane(coef, 6 + c) + delta[c] for c in range(3)]
        add = one_way(1, sign, w, u[1], x1, inv_v, inv_m, dot3(full, xu) + dot3(delta, curv))
        press = (slope0[3], None, slope2[3])
        for c in range(3):
            more = w * total[c] + 0.5 * (u[0] * slope0[c] + u[2] * slope2[c])
            if press[c] is not None:
                more = more - 0.5 * press[c]
            add[c] = add[c] + more * inv_v
        add[3] = add[3] + (total[3] - 0.5 * (slope0[0] + slope2[2])) * (1.0 / 7.0)
        add[4] = add[4] + w * total[4] * inv_m
        ru1, rw, ru0 = plane(coef, 3), 1.0 + plane(coef, 4), plane(coef, 5)
        behind = one_way(1, sign, rw, ru1, delta, *inverses(rw))
        near, far = (0, 1) if side == 0 else (SUB - 1, SUB - 2)
        for f in range(5):
            for e in range(ce):
                rows = jnp.where(
                    sub == near, add[f][e : e + 1, :], jnp.where(sub == far, behind[f][e : e + 1, :], 0.0)
                )
                out_ref[f, e] = edge[f, e] + rows
        copy = pltpu.make_async_copy(out_ref, final.at[:, :, pl.ds(place, SUB), :], sems.at[side])
        copy.start()
        waits.append(copy)
        for behind_row, u0, values in ((0, u[0], add), (1, ru0, behind)):
            force = u0 * jnp.abs(u0)
            at = (2 * side + behind_row) * ce
            for c in range(COMPS):
                hi, lo = split(values[c if c < 3 else 4] * force)
                table[at : at + ce, c * cz : (c + 1) * cz] = hi
                table[4 * ce + at : 5 * ce + at, c * cz : (c + 1) * cz] = lo

    acc[...] = grad[...]
    live = n_items[0]
    count = items.shape[0]
    per = min(BLOCK // LANES, count)
    for base in range(0, count, per):

        @pl.when(base * LANES < live)
        def _():
            lists = [items[base + k] for k in range(per)]
            turned = [x.T for x in lists]

            def col(j):
                return jnp.concatenate([x[:, j : j + 1] for x in turned], axis=0)

            key = jnp.concatenate([x[2:3] for x in lists], axis=1)
            rotor_terms(col(0), col(1), col(3), col(4) + col(5) + col(6), key, table, blocks, acc)

    for copy in range(copies_out):
        chunks[copy] = acc[...]
    for copy in waits:
        copy.wait()


def edges(flags, n_items, faces, packs, coefs, gots, tiles, items, grad, final, blocks, size):
    _, ce, cn, cz = final.shape
    args = (flags, n_items, *faces, *packs, *coefs, *gots, *tiles, items, grad, final)
    tile = VMEM((5, ce, SUB, cz), F32)
    return pl.pallas_call(
        functools.partial(edge_kernel, ce, cn, cz, blocks, size),
        out_shape=(shape(*final.shape), shape(size, blocks * SECT, LANES)),
        in_specs=[whole(pltpu.SMEM)] * 2 + [whole()] * (len(args) - 3) + [whole(pltpu.HBM)],
        out_specs=(whole(pltpu.HBM), whole()),
        scratch_shapes=[
            tile,
            tile,
            VMEM((8 * ce, COMPS * cz), BF16),
            VMEM((blocks * SECT, LANES), F32),
            pltpu.SemaphoreType.DMA((2,)),
        ],
        input_output_aliases={len(args) - 1: 0},
        compiler_params=params(32),
        cost_estimate=cost(1 << 24, 4 << 20),
    )(*args)


def sum_kernel(parts, out):
    total = jnp.sum(parts[...], axis=0)
    for c in range(COMPS):
        out[c] = total[:, c * TURB_DEV : (c + 1) * TURB_DEV]


def sum_parts(parts):
    return pl.pallas_call(
        sum_kernel,
        out_shape=shape(COMPS, SECT, TURB_DEV),
        in_specs=[whole()],
        out_specs=whole(),
        cost_estimate=cost(parts.size, parts.size * 4),
    )(parts)


def beside(x, size):
    if size == 2:
        got = lax.ppermute(x[0], "east", [(0, 1), (1, 0)])
        return got, got
    up = [(i, i + 1) for i in range(size - 1)]
    down = [(i + 1, i) for i in range(size - 1)]
    return lax.ppermute(x[1], "east", up), lax.ppermute(x[0], "east", down)


def north_ways(x, size):
    up = [(i, i + 1) for i in range(size - 1)]
    down = [(i + 1, i) for i in range(size - 1)]
    return lax.ppermute(x[1], "north", up), lax.ppermute(x[0], "north", down)


def shards(
    adjoint_start,
    adjoint_source,
    base_flow,
    eddy_visc,
    rotor_count,
    rotor_cell,
    rotor_turbine,
    rotor_sector,
    rotor_weight,
):
    _, ce, cn, cz = adjoint_start.shape
    n_east, n_north = lax.axis_size("east"), lax.axis_size("north")
    east, north = lax.axis_index("east"), lax.axis_index("north")
    flags = jnp.stack([east > 0, east < n_east - 1, north > 0, north < n_north - 1]).astype(jnp.int32)
    count = rotor_count.reshape(1)
    slots = rotor_cell.shape[-1]
    lists = [x.reshape(slots // LANES, LANES) for x in (rotor_cell, rotor_turbine, rotor_sector, rotor_weight)]

    if n_east == 2:
        at = jnp.stack([(1 - east) * (ce - 1), (1 - east) * (ce - 1) + 2 * east - 1])
    else:
        at = jnp.array([0, 1, ce - 1, ce - 2])
    at, n_faces = at.astype(jnp.int32), 1 if n_east == 2 else 2
    ends = beside(row_ends(at, adjoint_start, base_flow, n_faces), n_east)
    packs, own = pack(at, flags, ends, adjoint_start, adjoint_source, base_flow, eddy_visc, n_faces)
    gots = north_ways(packs, n_north)
    faces = beside(own, n_east)
    final, low, high, coef_low, coef_high, grad, items, n_items = sweeps(
        flags, count, adjoint_start, adjoint_source, base_flow, eddy_visc, faces, lists, n_north
    )
    final, chunks = edges(
        flags, n_items, faces, packs, (coef_low, coef_high), gots, (low, high), items, grad, final,
        n_north, n_east,
    )
    chunks = chunks.reshape(n_east * n_north, SECT, LANES)
    parts = lax.all_to_all(chunks, ("east", "north"), 0, 0, tiled=True)
    return (final, sum_parts(parts))


def solution(mesh):
    placed = (
        P(None, "east", "north", None),
        P(None, "east", "north", None),
        P(None, "east", "north", None),
        P("east", "north", None),
        P("east", "north"),
        P("east", "north", None),
        P("east", "north", None),
        P("east", "north", None),
        P("east", "north", None),
    )
    return jax.shard_map(
        shards,
        mesh=mesh,
        in_specs=placed,
        out_specs=(P(None, "east", "north", None), P(None, None, "north")),
        check_vma=False,
    )
```

```python
import functools

import jax
import jax.numpy as jnp
from jax import lax
from jax.experimental import pallas as pl
from jax.experimental.pallas import tpu as pltpu
from jax.sharding import PartitionSpec as P

SECT = 8
TURB_DEV = 12
COMPS = 4
LANES = 128
SUB = 8
PAD = 8
PACK = 14
FACE = 22
EDGE = 9
ITEM = 8
STEP = 2
VMEM = pltpu.VMEM
F32 = jnp.float32
BF16 = jnp.bfloat16


def whole(space=VMEM):
    return pl.BlockSpec(memory_space=space)


def shape(*dims):
    return jax.ShapeDtypeStruct(dims, F32)


def params(mib):
    return pltpu.CompilerParams(vmem_limit_bytes=mib << 20)


def cost(flops, size):
    return pl.CostEstimate(flops=flops, bytes_accessed=size, transcendentals=0)


class Copies:
    def __init__(self, sems):
        self.sems, self.used = sems, 0

    def take(self, *pairs):
        first = self.used
        self.used += len(pairs)
        return first, pairs

    def made(self, taken):
        first, pairs = taken
        return [pltpu.make_async_copy(s, d, self.sems.at[first + k]) for k, (s, d) in enumerate(pairs)]

    def start(self, taken):
        for c in self.made(taken):
            c.start()

    def wait(self, taken):
        for c in self.made(taken):
            c.wait()


def neighbours():
    e, n = lax.axis_index("east"), lax.axis_index("north")
    last_e, last_n = lax.axis_size("east") - 1, lax.axis_size("north") - 1
    return [
        jnp.where(e > 0, 1, 0), jnp.where(e < last_e, 1, 0),
        jnp.where(n > 0, 1, 0), jnp.where(n < last_n, 1, 0),
    ]


def facing(ce):
    if lax.axis_size("east") == 2:
        e = lax.axis_index("east")
        return [((1 - e) * (ce - 1), (1 - e) * (ce - 1) + 2 * e - 1)]
    return [(0, 1), (ce - 1, ce - 2)]


def one_way(k, sign, w, u, f, inv_v, inv_m, bend=None):
    pull = (w + (0.5 * sign) * u) * inv_v
    out = [pull * f[c] for c in range(3)]
    out[k] = out[k] - (0.5 * sign) * f[3] * inv_v
    out.append((f[3] - (0.5 * sign) * f[k]) * (1.0 / 7.0))
    m = w * f[4]
    if bend is not None:
        m = m + 0.25 * bend
    out.append(m * inv_m)
    return out


def inverses(w):
    return 1.0 / (6.0 * w + 1.0), 1.0 / (6.0 * w + 2.0)


def dot3(a, b):
    return a[0] * b[0] + a[1] * b[1] + a[2] * b[2]


def plane_shifts(rows, cols):
    r = lax.broadcasted_iota(jnp.int32, (rows, cols), 0)
    z = lax.broadcasted_iota(jnp.int32, (rows, cols), 1)

    def east(x, before=0.0, after=0.0):
        return (
            jnp.where(r < rows - 1, pltpu.roll(x, rows - 1, 0), after),
            jnp.where(r > 0, pltpu.roll(x, 1, 0), before),
        )

    def level(x):
        return (
            jnp.where(z < cols - 1, pltpu.roll(x, cols - 1, 1), 0.0),
            jnp.where(z > 0, pltpu.roll(x, 1, 1), 0.0),
        )

    return east, level


def ends_kernel(ce, cn, n_faces, start, flow, *refs):
    outs, tiles_v, tiles_u, sems = refs[:n_faces], *refs[n_faces:]
    copies = Copies(sems)
    taken = []
    for i, (e, _) in enumerate(facing(ce)):
        pairs = []
        for side, first in enumerate((0, cn - SUB)):
            pairs.append((start.at[:, e, pl.ds(first, SUB)], tiles_v.at[i, side]))
            pairs.append((flow.at[:, e, pl.ds(first, SUB)], tiles_u.at[i, side]))
        taken.append(copies.take(*pairs))
        copies.start(taken[-1])
    for i, out in enumerate(outs):
        copies.wait(taken[i])
        for side, row in enumerate((0, SUB - 1)):
            for f in range(8):
                tile = tiles_v[i, side, f] if f < 5 else tiles_u[i, side, f - 5]
                out[side * 8 + f : side * 8 + f + 1, :] = tile[row : row + 1]


def row_ends(start, flow, n_faces):
    _, ce, cn, cz = start.shape
    return pl.pallas_call(
        functools.partial(ends_kernel, ce, cn, n_faces),
        out_shape=[shape(16, cz)] * n_faces,
        in_specs=[whole(pltpu.HBM)] * 2,
        out_specs=[whole()] * n_faces,
        scratch_shapes=[
            VMEM((n_faces, 2, 5, SUB, cz), F32),
            VMEM((n_faces, 2, 3, SUB, cz), F32),
            pltpu.SemaphoreType.DMA((4 * n_faces,)),
        ],
        compiler_params=params(60),
        cost_estimate=cost(0, 1 << 16),
    )(start, flow)


def pack_kernel(ce, cn, cz, n_faces, endp, endn, start, source, flow, eddy, *refs):
    packs, refs = refs[:2], refs[2:]
    faces, refs = refs[:n_faces], refs[n_faces:]
    tiles_v, tiles_u, tiles_s, tiles_e, sems = refs
    has = [x.astype(F32) for x in neighbours()[:2]]
    copies = Copies(sems)
    sides = ((0, 0, 1, -1.0), (cn - SUB, SUB - 1, SUB - 2, 1.0))
    needed = []
    for side, (first, _, _, _) in enumerate(sides):
        pairs = []
        for h in range(2):
            cut = (pl.ds(first, SUB), pl.ds(h * LANES, LANES))
            pairs += [
                (start.at[(slice(None), slice(None)) + cut], tiles_v.at[side, :, :, h]),
                (flow.at[(slice(None), slice(None)) + cut], tiles_u.at[side, :, :, h]),
                (eddy.at[(slice(None),) + cut], tiles_e.at[side, 0, :, h]),
                (source.at[(slice(None), slice(None)) + cut], tiles_s.at[side, :, :, h]),
            ]
        needed.append(copies.take(*pairs))
        copies.start(needed[-1])
    later = []
    for (near, far), face in zip(facing(ce), faces):
        taken = copies.take(
            (start.at[:, near], face.at[0:5]),
            (flow.at[:, near], face.at[5:8]),
            (eddy.at[near], face.at[8]),
            (source.at[:, near], face.at[9:14]),
            (start.at[:, far], face.at[14:19]),
            (flow.at[:, far], face.at[19:22]),
        )
        copies.start(taken)
        later.append(taken)
    east, level = plane_shifts(ce, cz)

    def line(ref, side, f, row):
        flat = ref.reshape(2, ref.shape[1], ce * 2 * SUB, LANES)
        return jnp.concatenate([flat[side, f, pl.ds(h * SUB + row, ce, stride=2 * SUB), :] for h in range(2)], axis=1)

    for side, (_, row, behind, sign) in enumerate(sides):
        copies.wait(needed[side])
        pack = packs[side]
        v = [line(tiles_v, side, f, row) for f in range(5)]
        u = [line(tiles_u, side, k, row) for k in range(3)]
        eddy_row = line(tiles_e, side, 0, row)
        inner = [line(tiles_v, side, f, behind) for f in range(5)]
        inner_u = [line(tiles_u, side, k, behind) for k in range(3)]
        src = [line(tiles_s, side, f, row) for f in range(5)]
        for f, x in enumerate(v + u + [eddy_row]):
            pack[f * ce : (f + 1) * ce, :] = x
        w = 1.0 + eddy_row
        inv_v, inv_m = inverses(w)
        before = [endp[side * 8 + f : side * 8 + f + 1, :] * has[0] for f in range(8)]
        after = [endn[side * 8 + f : side * 8 + f + 1, :] * has[1] for f in range(8)]
        for f in range(8):
            pack[PACK * ce + f : PACK * ce + f + 1, :] = before[f]
            pack[PACK * ce + 8 + f : PACK * ce + 9 + f, :] = after[f]
        total, slope0, slope2 = [], [], []
        for f in range(5):
            a, b = east(v[f], before[f], after[f])
            h, l = level(v[f])
            total.append((a + b) + (h + l))
            slope0.append(a - b)
            slope2.append(h - l)
        curv = []
        for k in range(3):
            a, b = east(u[k], before[5 + k], after[5 + k])
            h, l = level(u[k])
            curv.append((a + b) + (h + l) + inner_u[k] - 6.0 * u[k])
        out = one_way(1, -sign, w, u[1], inner, inv_v, inv_m, dot3(v, curv))
        press = (slope0[3], None, slope2[3])
        for c in range(3):
            more = src[c] + w * total[c] + 0.5 * (u[0] * slope0[c] + u[2] * slope2[c])
            if press[c] is not None:
                more = more - 0.5 * press[c]
            out[c] = out[c] + more * inv_v
        out[3] = out[3] + (src[3] + total[3] - 0.5 * (slope0[0] + slope2[2])) * (1.0 / 7.0)
        out[4] = out[4] + (src[4] + w * total[4]) * inv_m
        for f in range(5):
            pack[(9 + f) * ce : (10 + f) * ce, :] = out[f]
    for taken in later:
        copies.wait(taken)


def pack(ends, start, source, flow, eddy, n_faces):
    _, ce, cn, cz = start.shape
    out = [shape(PACK * ce + 16, cz)] * 2 + [shape(FACE, cn, cz)] * n_faces
    got = pl.pallas_call(
        functools.partial(pack_kernel, ce, cn, cz, n_faces),
        out_shape=out,
        in_specs=[whole()] * 2 + [whole(pltpu.HBM)] * 4,
        out_specs=[whole()] * len(out),
        scratch_shapes=[
            VMEM((2, 5, ce, 2, SUB, LANES), F32),
            VMEM((2, 3, ce, 2, SUB, LANES), F32),
            VMEM((2, 5, ce, 2, SUB, LANES), F32),
            VMEM((2, 1, ce, 2, SUB, LANES), F32),
            pltpu.SemaphoreType.DMA((16 + 6 * n_faces,)),
        ],
        compiler_params=params(60),
        cost_estimate=cost(1 << 22, 4 << 20),
    )(*ends, start, source, flow, eddy)
    return got[:2], got[2:]


def split(x):
    high = x.astype(BF16)
    return high, (x - high.astype(F32)).astype(BF16)


def owner_of(turbine):
    return lax.shift_right_logical(turbine * 5462, 16)


def columns(x, first, size):
    return jnp.concatenate([x[:, k : k + 1] for k in range(first // LANES, (first + size) // LANES)], axis=0)


def lines(x, first, size):
    return jnp.concatenate([x[k : k + 1, :] for k in range(first // LANES, (first + size) // LANES)], axis=1)


def steps_of(chunks):
    sizes = [0] + [x for x in (LANES, 2 * LANES) if x < chunks * LANES] + [chunks * LANES]
    return list(zip(sizes[:-1], sizes[1:]))


def rotor_terms(row, level, turbine, weight, key, table, blocks, acc):
    size = row.shape[0]
    rows, width = table.shape[0] // 2, table.shape[1]
    cz = width // COMPS
    lane_row = lax.broadcasted_iota(jnp.int32, (size, rows), 1).astype(F32)
    pick = jnp.where(row == lane_row, 1.0, 0.0).astype(BF16)
    got = jnp.dot(jnp.concatenate([pick, pick], axis=1), table[...], preferred_element_type=F32)
    here = level == lax.broadcasted_iota(jnp.int32, (size, cz), 1).astype(F32)
    lane = lax.broadcasted_iota(jnp.int32, (size, LANES), 1)
    lane_comp = owner_of(lane)
    lane_tur = (lane - lane_comp * TURB_DEV).astype(F32)
    spread = jnp.zeros((size, LANES), F32)
    for c in range(COMPS):
        part = jnp.where(here, got[:, c * cz : (c + 1) * cz], 0.0)
        spread = jnp.where(lane_comp == c, jnp.sum(part, axis=1, keepdims=True), spread)
    spread = jnp.where(turbine == lane_tur, spread * weight, 0.0)
    lane_key = lax.broadcasted_iota(jnp.int32, (blocks * SECT, size), 0).astype(F32)
    to = jnp.where(lane_key == key, 1.0, 0.0).astype(BF16)
    high = spread.astype(BF16)
    rest = spread - high.astype(F32)
    mid, low = split(rest)
    parts = jnp.dot(to, jnp.concatenate([high, mid, low], axis=1), preferred_element_type=F32)
    acc[...] += parts[:, :LANES] + parts[:, LANES : 2 * LANES] + parts[:, 2 * LANES :]


def halves(ref, f, i, cn, move=0):
    return [ref[f, i, h, pl.ds(PAD + move, cn), :] for h in range(2)]


def level_shifts(x, first, last):
    up = [pltpu.roll(x[h], LANES - 1, 1) for h in range(2)]
    down = [pltpu.roll(x[h], 1, 1) for h in range(2)]
    return (
        [jnp.where(last, up[1], up[0]), jnp.where(last, 0.0, up[1])],
        [jnp.where(first, 0.0, down[0]), jnp.where(first, down[0], down[1])],
    )


def slab_sweep(ref, i, cn, first, last, src, flow, visc, curv):
    two = range(2)
    w = visc
    inv = [inverses(w[h]) for h in two]
    w2 = [2.0 * w[h] for h in two]

    def sides(f):
        mid = halves(ref, f, i, cn)
        a, b = halves(ref, f, i + 1, cn), halves(ref, f, i - 1, cn)
        n, s = halves(ref, f, i, cn, 1), halves(ref, f, i, cn, -1)
        up, down = level_shifts(mid, first, last)
        return mid, a, b, n, s, up, down

    _, a, b, n, s, up, down = sides(3)
    grad = [[x[h] - y[h] for h in two] for x, y in ((a, b), (n, s), (up, down))]
    q_sum = [(a[h] + b[h]) + (n[h] + s[h]) + (up[h] + down[h]) for h in two]
    out, div, bend = [], [0.0, 0.0], [0.0, 0.0]
    for c in range(3):
        mid, a, b, n, s, up, down = sides(c)
        res = []
        for h in two:
            total = (a[h] + b[h]) + (n[h] + s[h]) + (up[h] + down[h])
            slope = [a[h] - b[h], n[h] - s[h], up[h] - down[h]]
            carried = flow[0][h] * slope[0] + flow[1][h] * slope[1] + flow[2][h] * slope[2]
            res.append((src(c)[h] + 0.5 * (w2[h] * total + (carried - grad[c][h]))) * inv[h][0])
            div[h] = div[h] + slope[c]
            bend[h] = bend[h] + mid[h] * curv[c][h]
        out.append(res)
    out.append([(src(3)[h] + q_sum[h] - 0.5 * div[h]) * (1.0 / 7.0) for h in two])
    _, a, b, n, s, up, down = sides(4)
    res = []
    for h in two:
        total = (a[h] + b[h]) + (n[h] + s[h]) + (up[h] + down[h])
        res.append((src(4)[h] + w[h] * total + 0.25 * bend[h]) * inv[h][1])
    out.append(res)
    return out


def sweeps_kernel(
    ce, cn, cz, blocks,
    count, start, source, flow, eddy, facep, facen, cells, turbine, sector, weight,
    final, edge_low, edge_high, coef_low, coef_high, grad, items, n_items,
    v0, u, src, ed, v1, curv, held, table, sems,
):
    copies = Copies(sems)
    two = range(2)
    has = [x > 0 for x in neighbours()[:2]]
    inner = pl.ds(PAD, cn)

    def part(h):
        return pl.ds(h * LANES, LANES)

    def halo(face, near, far, slab):
        pairs = []
        for h in two:
            pairs += [
                (face.at[0:5, :, part(h)], v0.at[:, near, h, inner]),
                (face.at[5:8, :, part(h)], u.at[:, near, h, inner]),
                (face.at[8, :, part(h)], ed.at[slab, h]),
                (face.at[9:14, :, part(h)], src.at[:, slab, h]),
                (face.at[14:19, :, part(h)], v0.at[:, far, h, inner]),
                (face.at[19:22, :, part(h)], u.at[:, far, h, inner]),
            ]
        return pairs

    ends = ((facep, 1, 0, 0), (facen, ce + 2, ce + 3, ce + 1))
    halos = [copies.take(*halo(*x)) for x in ends]

    def group(g):
        span, own, own2 = pl.ds(g, STEP), pl.ds(g + 1, STEP), pl.ds(g + 2, STEP)
        pairs = []
        for h in two:
            pairs += [
                (start.at[:, span, :, part(h)], v0.at[:, own2, h, inner]),
                (flow.at[:, span, :, part(h)], u.at[:, own2, h, inner]),
                (eddy.at[span, :, part(h)], ed.at[own, h]),
                (source.at[:, span, :, part(h)], src.at[:, own, h]),
            ]
        return pairs

    groups = [copies.take(*group(g)) for g in range(0, ce, STEP)]
    per = len(groups[0][1])
    copies.start(groups[0])
    for exists, taken in zip(has, halos):

        @pl.when(exists)
        def _():
            copies.start(taken)

    for taken in groups[1:]:
        copies.start(taken)

    blank = jnp.zeros((PAD, LANES), F32)
    for ref, fields in ((v0, 5), (u, 3), (v1, 5)):

        @pl.loop(0, ref.shape[1])
        def _(i):
            for f in range(fields):
                for h in two:
                    ref[f, i, h, 0:PAD, :] = blank
                    ref[f, i, h, PAD + cn : PAD + cn + PAD, :] = blank

    for exists, (_, near, _, _) in zip(has, ends):

        @pl.when(jnp.logical_not(exists))
        def _():
            for ref, fields in ((v0, 5), (u, 3)):
                for f in range(fields):
                    for h in two:
                        ref[f, near, h, inner, :] = jnp.zeros((cn, LANES), F32)

    lane = lax.broadcasted_iota(jnp.int32, (cn, LANES), 1)
    first, last = lane == 0, lane == LANES - 1

    live = count[0]
    cell, tur = cells[...], turbine[...]
    owner = owner_of(tur)
    key = (owner * SECT + sector[...]).astype(F32)
    local = (tur - owner * TURB_DEV).astype(F32)
    chunks = cell.shape[0]
    slot = lax.broadcasted_iota(jnp.int32, cell.shape, 0) * LANES + lax.broadcasted_iota(jnp.int32, cell.shape, 1)
    load = jnp.where(slot < live, weight[...], 0.0)
    line = lax.shift_right_logical(cell, cz.bit_length() - 1)
    level = jnp.bitwise_and(cell, cz - 1).astype(F32)
    north = jnp.bitwise_and(line, cn - 1)
    east = lax.shift_right_logical(line, cn.bit_length() - 1)
    place = jnp.where(north == 0, 0, jnp.where(north == 1, 1, jnp.where(north == cn - 1, 2, 3)))
    is_edge = jnp.logical_or(north <= 1, north >= cn - 2)
    chosen = jnp.where(jnp.logical_and(is_edge, slot < live), 1.0, 0.0)
    edge_row = (place * ce + east).astype(F32)

    lower = lax.broadcasted_iota(jnp.int32, (LANES, LANES), 0) < lax.broadcasted_iota(jnp.int32, (LANES, LANES), 1)
    rank = jnp.dot(chosen.astype(BF16), jnp.where(lower, 1.0, 0.0).astype(BF16), preferred_element_type=F32)
    sums = jnp.sum(chosen, axis=1, keepdims=True)
    so_far = jnp.zeros((1, 1), F32)
    starts = []
    for k in range(chunks):
        starts.append(so_far)
        so_far = so_far + sums[k : k + 1]
    rank = jnp.where(chosen > 0.0, rank + jnp.concatenate(starts, axis=0), -1.0)
    total = jnp.sum(chosen).astype(jnp.int32)
    n_items[0] = total
    load_high = load.astype(BF16).astype(F32)
    load_rest = load - load_high
    load_mid = load_rest.astype(BF16).astype(F32)
    load_low = load_rest - load_mid
    blank = jnp.zeros((1, LANES), F32)
    rows = [
        jnp.concatenate([x[k : k + 1] for x in (edge_row, level, key, local, load_high, load_mid, load_low)] + [blank])
        for k in range(chunks)
    ]
    to = lax.broadcasted_iota(jnp.int32, (LANES, LANES), 0).astype(F32)
    items[...] = jnp.zeros_like(items)
    for q in range(chunks):

        @pl.when(q * LANES < total)
        def _():
            where = jnp.concatenate(
                [jnp.where(rank[k : k + 1] - float(q * LANES) == to, 1.0, 0.0) for k in range(chunks)], axis=1
            ).astype(BF16)
            entries = jnp.concatenate(rows, axis=1).astype(BF16)
            items[q] = lax.dot_general(entries, where, (((1,), (1,)), ((), ())), preferred_element_type=F32)

    @pl.when(has[0])
    def _():
        copies.wait(halos[0])

    @pl.loop(0, ce + 2)
    def _(i):
        @pl.when(jnp.logical_and(i < ce, lax.rem(i, STEP) == 0))
        def _():
            copies.wait((groups[0][0] + lax.div(i, STEP) * per, group(i)))

        @pl.when(jnp.logical_and(i == ce, has[1]))
        def _():
            copies.wait(halos[1])

        real = jnp.logical_and(
            jnp.logical_or(i > 0, has[0]), jnp.logical_or(i < ce + 1, has[1])
        )

        @pl.when(real)
        def _():
            mid = i + 1
            flows = [halves(u, k, mid, cn) for k in range(3)]
            bends = []
            for k in range(3):
                a, b = halves(u, k, mid + 1, cn), halves(u, k, mid - 1, cn)
                n, s = halves(u, k, mid, cn, 1), halves(u, k, mid, cn, -1)
                up, down = level_shifts(flows[k], first, last)
                res = [(a[h] + b[h]) + (n[h] + s[h]) + (up[h] + down[h]) - 6.0 * flows[k][h] for h in two]
                for h in two:
                    curv[k, i, h] = res[h]
                bends.append(res)
            out = slab_sweep(
                v0, mid, cn, first, last,
                lambda f: [src[f, i, h] for h in two],
                flows, [1.0 + ed[i, h] for h in two], bends,
            )
            for f in range(5):
                for h in two:
                    v1[f, i, h, inner, :] = out[f][h]

        @pl.when(jnp.logical_not(real))
        def _():
            for f in range(5):
                for h in two:
                    v1[f, i, h, inner, :] = jnp.zeros((cn, LANES), F32)

    def leave(e):
        return [(held.at[:, pl.ds(e, STEP)], final.at[:, pl.ds(e, STEP)])]

    outs = [copies.take(*leave(e)) for e in range(0, ce, STEP)]

    @pl.loop(0, ce)
    def _(e):
        i = e + 1
        flows = [halves(u, k, i + 1, cn) for k in range(3)]
        bends = [[curv[k, i, h] for h in two] for k in range(3)]
        out = slab_sweep(
            v1, i, cn, first, last,
            lambda f: [src[f, i, h] for h in two],
            flows, [1.0 + ed[i, h] for h in two], bends,
        )
        def put(coef, k, line):
            coef[pl.ds(k * ce + e, 1), :] = jnp.concatenate(line, axis=1)

        at = pl.ds(pl.multiple_of(e * cn, cn), cn)
        below = pl.ds(pl.multiple_of((ce + e) * cn, cn), cn)
        for h in two:
            force = flows[0][h] * jnp.abs(flows[0][h])
            for f in range(5):
                held[f, e, :, part(h)] = out[f][h]
                edge_low[f, e, :, part(h)] = out[f][h][0:SUB]
                edge_high[f, e, :, part(h)] = out[f][h][cn - SUB : cn]
            for c in range(COMPS):
                hi, lo = split(out[c if c < 3 else 4][h] * force)
                wide = pl.ds(c * cz + h * LANES, LANES)
                table[at, wide] = hi
                table[below, wide] = lo
        for coef, row, behind in ((coef_low, 0, 1), (coef_high, cn - 1, cn - 2)):
            for k in range(3):
                put(coef, k, [bends[k][h][row : row + 1] for h in two])
                put(coef, 6 + k, [v1[k, i, h, PAD + row : PAD + row + 1, :] for h in two])
            put(coef, 3, [flows[1][h][behind : behind + 1] for h in two])
            put(coef, 4, [ed[i, h, behind : behind + 1, :] for h in two])
            put(coef, 5, [flows[0][h][behind : behind + 1] for h in two])

        @pl.when(lax.rem(e, STEP) == STEP - 1)
        def _():
            copies.start((outs[0][0] + lax.div(e, STEP), leave(e - (STEP - 1))))


    row_t, level_t, local_t, load_t = line.astype(F32).T, level.T, local.T, load.T
    grad[...] = jnp.zeros_like(grad)
    for least, size in steps_of(chunks):

        @pl.when(jnp.logical_and(live > least, live <= size))
        def _():
            cols = [columns(x, 0, size) for x in (row_t, level_t, local_t, load_t)]
            rotor_terms(*cols, lines(key, 0, size), table, blocks, grad)

    for taken in outs:
        copies.wait(taken)


def sweeps(count, start, source, flow, eddy, faces, lists, blocks):
    _, ce, cn, cz = start.shape
    chunks = lists[0].shape[0]
    edge = shape(5, ce, SUB, cz)
    return pl.pallas_call(
        functools.partial(sweeps_kernel, ce, cn, cz, blocks),
        out_shape=(
            shape(*start.shape),
            edge,
            edge,
            shape(EDGE * ce, cz),
            shape(EDGE * ce, cz),
            shape(blocks * SECT, LANES),
            shape(chunks, ITEM, LANES),
            jax.ShapeDtypeStruct((1,), jnp.int32),
        ),
        in_specs=[whole(pltpu.SMEM)] + [whole(pltpu.HBM)] * 6 + [whole()] * 4,
        out_specs=(whole(pltpu.HBM),) + (whole(),) * 6 + (whole(pltpu.SMEM),),
        scratch_shapes=[
            VMEM((5, ce + 4, 2, PAD + cn + PAD, LANES), F32),
            VMEM((3, ce + 4, 2, PAD + cn + PAD, LANES), F32),
            VMEM((5, ce + 2, 2, cn, LANES), F32),
            VMEM((ce + 2, 2, cn, LANES), F32),
            VMEM((5, ce + 2, 2, PAD + cn + PAD, LANES), F32),
            VMEM((3, ce + 2, 2, cn, LANES), F32),
            VMEM(start.shape, F32),
            VMEM((2 * ce * cn, COMPS * cz), BF16),
            pltpu.SemaphoreType.DMA((24 + 9 * (ce // STEP),)),
        ],
        compiler_params=params(48),
        cost_estimate=cost(300 * start.size // 5, 10 << 20),
    )(count, start, source, flow, eddy, *faces, *lists)


def edge_kernel(
    ce, cn, cz, blocks, copies_out,
    n_items, facep, facen, own_low, own_high, coef_low, coef_high, got_prev, got_next,
    edge_low, edge_high, items, grad, final_in,
    final, chunks,
    low_out, high_out, table, acc, sems,
):
    east, level = plane_shifts(ce, cz)
    sub = lax.broadcasted_iota(jnp.int32, (SUB, cz), 0)
    has = [x.astype(F32) for x in neighbours()]
    sides = (
        (-1.0, 0, own_low, coef_low, got_prev, edge_low, low_out, 0),
        (1.0, cn - 1, own_high, coef_high, got_next, edge_high, high_out, cn - SUB),
    )
    waits = []
    for side, (sign, row, own, coef, got, edge, out_ref, place) in enumerate(sides):

        def plane(ref, f):
            return ref[f * ce : (f + 1) * ce, :]

        v0 = [plane(own, f) for f in range(5)]
        u = [plane(own, 5 + k) for k in range(3)]
        w = 1.0 + plane(own, 8)
        xv = [plane(got, f) for f in range(5)]
        xu = [plane(got, 5 + k) for k in range(3)]
        xw = 1.0 + plane(got, 8)
        xp = [plane(got, 9 + f) for f in range(5)]
        curv = [plane(coef, k) for k in range(3)]
        inv_v, inv_m = inverses(w)
        delta = one_way(1, sign, w, u[1], xv, inv_v, inv_m, dot3(v0, xu))
        back = one_way(1, -sign, xw, xu[1], v0, *inverses(xw), dot3(xv, u))
        x1 = [xp[f] + back[f] for f in range(5)]
        ends = []
        for far, face in enumerate((facep, facen)):
            hv = [got[PACK * ce + 8 * far + f : PACK * ce + 8 * far + f + 1, :] for f in range(8)]
            fv = [face[f, row : row + 1, :] * has[far] for f in range(5)]
            fu = face[6, row : row + 1, :] * has[far]
            fw = 1.0 + face[8, row : row + 1, :] * has[far]
            ends.append(one_way(1, sign, fw, fu, hv, *inverses(fw), dot3(fv, hv[5:])))
        x1 = [x * has[2 + side] for x in x1]
        total, slope0, slope2 = [], [], []
        for f in range(5):
            a, b = east(delta[f], ends[0][f], ends[1][f])
            h, l = level(delta[f])
            total.append((a + b) + (h + l))
            slope0.append(a - b)
            slope2.append(h - l)
        full = [plane(coef, 6 + c) + delta[c] for c in range(3)]
        add = one_way(1, sign, w, u[1], x1, inv_v, inv_m, dot3(full, xu) + dot3(delta, curv))
        press = (slope0[3], None, slope2[3])
        for c in range(3):
            more = w * total[c] + 0.5 * (u[0] * slope0[c] + u[2] * slope2[c])
            if press[c] is not None:
                more = more - 0.5 * press[c]
            add[c] = add[c] + more * inv_v
        add[3] = add[3] + (total[3] - 0.5 * (slope0[0] + slope2[2])) * (1.0 / 7.0)
        add[4] = add[4] + w * total[4] * inv_m
        ru1, rw, ru0 = plane(coef, 3), 1.0 + plane(coef, 4), plane(coef, 5)
        behind = one_way(1, sign, rw, ru1, delta, *inverses(rw))
        near, far = (0, 1) if side == 0 else (SUB - 1, SUB - 2)
        for f in range(5):
            for e in range(ce):
                rows = jnp.where(
                    sub == near, add[f][e : e + 1, :], jnp.where(sub == far, behind[f][e : e + 1, :], 0.0)
                )
                out_ref[f, e] = edge[f, e] + rows
        copy = pltpu.make_async_copy(out_ref, final.at[:, :, pl.ds(place, SUB), :], sems.at[side])
        copy.start()
        waits.append(copy)
        for behind_row, u0, values in ((0, u[0], add), (1, ru0, behind)):
            force = u0 * jnp.abs(u0)
            at = (2 * side + behind_row) * ce
            for c in range(COMPS):
                hi, lo = split(values[c if c < 3 else 4] * force)
                table[at : at + ce, c * cz : (c + 1) * cz] = hi
                table[4 * ce + at : 5 * ce + at, c * cz : (c + 1) * cz] = lo

    acc[...] = grad[...]
    live = n_items[0]
    for least, size in steps_of(items.shape[0]):

        @pl.when(jnp.logical_and(live > least, live <= size))
        def _():
            lists = [items[k] for k in range(size // LANES)]
            turned = [x.T for x in lists]

            def col(j):
                return jnp.concatenate([x[:, j : j + 1] for x in turned], axis=0)

            key = jnp.concatenate([x[2:3] for x in lists], axis=1)
            rotor_terms(col(0), col(1), col(3), col(4) + col(5) + col(6), key, table, blocks, acc)

    for copy in range(copies_out):
        chunks[copy] = acc[...]
    for copy in waits:
        copy.wait()


def edges(n_items, faces, packs, coefs, gots, tiles, items, grad, final, blocks, size):
    _, ce, cn, cz = final.shape
    args = (n_items, *faces, *packs, *coefs, *gots, *tiles, items, grad, final)
    tile = VMEM((5, ce, SUB, cz), F32)
    return pl.pallas_call(
        functools.partial(edge_kernel, ce, cn, cz, blocks, size),
        out_shape=(shape(*final.shape), shape(size, blocks * SECT, LANES)),
        in_specs=[whole(pltpu.SMEM)] + [whole()] * (len(args) - 2) + [whole(pltpu.HBM)],
        out_specs=(whole(pltpu.HBM), whole()),
        scratch_shapes=[
            tile,
            tile,
            VMEM((8 * ce, COMPS * cz), BF16),
            VMEM((blocks * SECT, LANES), F32),
            pltpu.SemaphoreType.DMA((2,)),
        ],
        input_output_aliases={len(args) - 1: 0},
        compiler_params=params(32),
        cost_estimate=cost(1 << 24, 4 << 20),
    )(*args)


def sum_kernel(parts, out):
    total = jnp.sum(parts[...], axis=0)
    for c in range(COMPS):
        out[c] = total[:, c * TURB_DEV : (c + 1) * TURB_DEV]


def sum_parts(parts):
    return pl.pallas_call(
        sum_kernel,
        out_shape=shape(COMPS, SECT, TURB_DEV),
        in_specs=[whole()],
        out_specs=whole(),
        compiler_params=params(4),
        cost_estimate=cost(parts.size, parts.size * 4),
    )(parts)


def beside(x, size):
    if size == 2:
        got = lax.ppermute(x[0], "east", [(0, 1), (1, 0)])
        return got, got
    up = [(i, i + 1) for i in range(size - 1)]
    down = [(i + 1, i) for i in range(size - 1)]
    return lax.ppermute(x[1], "east", up), lax.ppermute(x[0], "east", down)


def north_ways(x, size):
    up = [(i, i + 1) for i in range(size - 1)]
    down = [(i + 1, i) for i in range(size - 1)]
    return lax.ppermute(x[1], "north", up), lax.ppermute(x[0], "north", down)


def shards(
    adjoint_start,
    adjoint_source,
    base_flow,
    eddy_visc,
    rotor_count,
    rotor_cell,
    rotor_turbine,
    rotor_sector,
    rotor_weight,
):
    _, ce, cn, cz = adjoint_start.shape
    n_east, n_north = lax.axis_size("east"), lax.axis_size("north")
    count = rotor_count.reshape(1)
    slots = rotor_cell.shape[-1]
    lists = [x.reshape(slots // LANES, LANES) for x in (rotor_cell, rotor_turbine, rotor_sector, rotor_weight)]

    n_faces = 1 if n_east == 2 else 2
    ends = beside(row_ends(adjoint_start, base_flow, n_faces), n_east)
    packs, own = pack(ends, adjoint_start, adjoint_source, base_flow, eddy_visc, n_faces)
    gots = north_ways(packs, n_north)
    faces = beside(own, n_east)
    final, low, high, coef_low, coef_high, grad, items, n_items = sweeps(
        count, adjoint_start, adjoint_source, base_flow, eddy_visc, faces, lists, n_north
    )
    final, chunks = edges(
        n_items, faces, packs, (coef_low, coef_high), gots, (low, high), items, grad, final,
        n_north, n_east,
    )
    chunks = chunks.reshape(n_east * n_north, SECT, LANES)
    parts = lax.all_to_all(chunks, ("east", "north"), 0, 0, tiled=True)
    return (final, sum_parts(parts))


def solution(mesh):
    placed = (
        P(None, "east", "north", None),
        P(None, "east", "north", None),
        P(None, "east", "north", None),
        P("east", "north", None),
        P("east", "north"),
        P("east", "north", None),
        P("east", "north", None),
        P("east", "north", None),
        P("east", "north", None),
    )
    return jax.shard_map(
        shards,
        mesh=mesh,
        in_specs=placed,
        out_specs=(P(None, "east", "north", None), P(None, None, "north")),
        check_vma=False,
    )
```

```python
import functools

import jax
import jax.numpy as jnp
from jax import lax
from jax.experimental import pallas as pl
from jax.experimental.pallas import tpu as pltpu
from jax.sharding import PartitionSpec as P

SECT = 8
TURB_DEV = 12
COMPS = 4
LANES = 128
SUB = 8
PAD = 8
PACK = 14
FACE = 22
EDGE = 9
RAW = 23
ITEM = 8
STEP = 4
ROWS_1 = 8
ROWS_2 = 16
VMEM = pltpu.VMEM
F32 = jnp.float32
BF16 = jnp.bfloat16


def whole(space=VMEM):
    return pl.BlockSpec(memory_space=space)


def shape(*dims):
    return jax.ShapeDtypeStruct(dims, F32)


def params(mib):
    return pltpu.CompilerParams(vmem_limit_bytes=mib << 20)


def cost(flops, size):
    return pl.CostEstimate(flops=flops, bytes_accessed=size, transcendentals=0)


class Copies:
    def __init__(self, sems):
        self.sems, self.used = sems, 0

    def take(self, *pairs):
        first = self.used
        self.used += len(pairs)
        return first, pairs

    def made(self, taken):
        first, pairs = taken
        return [pltpu.make_async_copy(s, d, self.sems.at[first + k]) for k, (s, d) in enumerate(pairs)]

    def start(self, taken):
        for c in self.made(taken):
            c.start()

    def wait(self, taken):
        for c in self.made(taken):
            c.wait()


def neighbours():
    e, n = lax.axis_index("east"), lax.axis_index("north")
    last_e, last_n = lax.axis_size("east") - 1, lax.axis_size("north") - 1
    return [
        jnp.where(e > 0, 1, 0), jnp.where(e < last_e, 1, 0),
        jnp.where(n > 0, 1, 0), jnp.where(n < last_n, 1, 0),
    ]


def facing(ce):
    if lax.axis_size("east") == 2:
        e = lax.axis_index("east")
        return [((1 - e) * (ce - 1), (1 - e) * (ce - 1) + 2 * e - 1)]
    return [(0, 1), (ce - 1, ce - 2)]


def one_way(k, sign, w, u, f, inv_v, inv_m, bend=None):
    pull = (w + (0.5 * sign) * u) * inv_v
    out = [pull * f[c] for c in range(3)]
    out[k] = out[k] - (0.5 * sign) * f[3] * inv_v
    out.append((f[3] - (0.5 * sign) * f[k]) * (1.0 / 7.0))
    m = w * f[4]
    if bend is not None:
        m = m + 0.25 * bend
    out.append(m * inv_m)
    return out


def inverses(w):
    return 1.0 / (6.0 * w + 1.0), 1.0 / (6.0 * w + 2.0)


def dot3(a, b):
    return a[0] * b[0] + a[1] * b[1] + a[2] * b[2]


def plane_shifts(rows, cols):
    r = lax.broadcasted_iota(jnp.int32, (rows, cols), 0)
    z = lax.broadcasted_iota(jnp.int32, (rows, cols), 1)

    def east(x, before=0.0, after=0.0):
        return (
            jnp.where(r < rows - 1, pltpu.roll(x, rows - 1, 0), after),
            jnp.where(r > 0, pltpu.roll(x, 1, 0), before),
        )

    def level(x):
        return (
            jnp.where(z < cols - 1, pltpu.roll(x, cols - 1, 1), 0.0),
            jnp.where(z > 0, pltpu.roll(x, 1, 1), 0.0),
        )

    return east, level


def ends_kernel(ce, cn, n_faces, start, flow, *refs):
    outs, tiles_v, tiles_u, sems = refs[:n_faces], *refs[n_faces:]
    copies = Copies(sems)
    taken = []
    for i, (e, _) in enumerate(facing(ce)):
        pairs = []
        for side, first in enumerate((0, cn - SUB)):
            pairs.append((start.at[:, e, pl.ds(first, SUB)], tiles_v.at[i, side]))
            pairs.append((flow.at[:, e, pl.ds(first, SUB)], tiles_u.at[i, side]))
        taken.append(copies.take(*pairs))
        copies.start(taken[-1])
    for i, out in enumerate(outs):
        copies.wait(taken[i])
        for side, row in enumerate((0, SUB - 1)):
            for f in range(8):
                tile = tiles_v[i, side, f] if f < 5 else tiles_u[i, side, f - 5]
                out[side * 8 + f : side * 8 + f + 1, :] = tile[row : row + 1]


def row_ends(start, flow, n_faces):
    _, ce, cn, cz = start.shape
    return pl.pallas_call(
        functools.partial(ends_kernel, ce, cn, n_faces),
        out_shape=[shape(16, cz)] * n_faces,
        in_specs=[whole(pltpu.HBM)] * 2,
        out_specs=[whole()] * n_faces,
        scratch_shapes=[
            VMEM((n_faces, 2, 5, SUB, cz), F32),
            VMEM((n_faces, 2, 3, SUB, cz), F32),
            pltpu.SemaphoreType.DMA((4 * n_faces,)),
        ],
        compiler_params=params(60),
        cost_estimate=cost(0, 1 << 16),
    )(start, flow)


def pack_kernel(ce, cn, cz, n_faces, endp, endn, start, source, flow, eddy, *refs):
    packs, refs = refs[:2], refs[2:]
    faces, refs = refs[:n_faces], refs[n_faces:]
    tiles_v, tiles_u, tiles_s, tiles_e, sems = refs
    has = [x.astype(F32) for x in neighbours()[:2]]
    copies = Copies(sems)
    sides = ((0, 0, 1, -1.0), (cn - SUB, SUB - 1, SUB - 2, 1.0))
    needed = []
    for side, (first, _, _, _) in enumerate(sides):
        pairs = []
        for h in range(2):
            cut = (pl.ds(first, SUB), pl.ds(h * LANES, LANES))
            pairs += [
                (start.at[(slice(None), slice(None)) + cut], tiles_v.at[side, :, :, h]),
                (flow.at[(slice(None), slice(None)) + cut], tiles_u.at[side, :, :, h]),
                (eddy.at[(slice(None),) + cut], tiles_e.at[side, 0, :, h]),
                (source.at[(slice(None), slice(None)) + cut], tiles_s.at[side, :, :, h]),
            ]
        needed.append(copies.take(*pairs))
        copies.start(needed[-1])
    later = []
    for (near, far), face in zip(facing(ce), faces):
        taken = copies.take(
            (start.at[:, near], face.at[0:5]),
            (flow.at[:, near], face.at[5:8]),
            (eddy.at[near], face.at[8]),
            (source.at[:, near], face.at[9:14]),
            (start.at[:, far], face.at[14:19]),
            (flow.at[:, far], face.at[19:22]),
        )
        copies.start(taken)
        later.append(taken)
    east, level = plane_shifts(ce, cz)

    def line(ref, side, f, row):
        flat = ref.reshape(2, ref.shape[1], ce * 2 * SUB, LANES)
        return jnp.concatenate([flat[side, f, pl.ds(h * SUB + row, ce, stride=2 * SUB), :] for h in range(2)], axis=1)

    for side, (_, row, behind, sign) in enumerate(sides):
        copies.wait(needed[side])
        pack = packs[side]
        v = [line(tiles_v, side, f, row) for f in range(5)]
        u = [line(tiles_u, side, k, row) for k in range(3)]
        eddy_row = line(tiles_e, side, 0, row)
        inner = [line(tiles_v, side, f, behind) for f in range(5)]
        inner_u = [line(tiles_u, side, k, behind) for k in range(3)]
        src = [line(tiles_s, side, f, row) for f in range(5)]
        for f, x in enumerate(v + u + [eddy_row]):
            pack[f * ce : (f + 1) * ce, :] = x
        w = 1.0 + eddy_row
        inv_v, inv_m = inverses(w)
        before = [endp[side * 8 + f : side * 8 + f + 1, :] * has[0] for f in range(8)]
        after = [endn[side * 8 + f : side * 8 + f + 1, :] * has[1] for f in range(8)]
        for f in range(8):
            pack[PACK * ce + f : PACK * ce + f + 1, :] = before[f]
            pack[PACK * ce + 8 + f : PACK * ce + 9 + f, :] = after[f]
        total, slope0, slope2 = [], [], []
        for f in range(5):
            a, b = east(v[f], before[f], after[f])
            h, l = level(v[f])
            total.append((a + b) + (h + l))
            slope0.append(a - b)
            slope2.append(h - l)
        curv = []
        for k in range(3):
            a, b = east(u[k], before[5 + k], after[5 + k])
            h, l = level(u[k])
            curv.append((a + b) + (h + l) + inner_u[k] - 6.0 * u[k])
        out = one_way(1, -sign, w, u[1], inner, inv_v, inv_m, dot3(v, curv))
        press = (slope0[3], None, slope2[3])
        for c in range(3):
            more = src[c] + w * total[c] + 0.5 * (u[0] * slope0[c] + u[2] * slope2[c])
            if press[c] is not None:
                more = more - 0.5 * press[c]
            out[c] = out[c] + more * inv_v
        out[3] = out[3] + (src[3] + total[3] - 0.5 * (slope0[0] + slope2[2])) * (1.0 / 7.0)
        out[4] = out[4] + (src[4] + w * total[4]) * inv_m
        for f in range(5):
            pack[(9 + f) * ce : (10 + f) * ce, :] = out[f]
    for taken in later:
        copies.wait(taken)


def pack(ends, start, source, flow, eddy, n_faces):
    _, ce, cn, cz = start.shape
    out = [shape(PACK * ce + 16, cz)] * 2 + [shape(FACE, cn, cz)] * n_faces
    got = pl.pallas_call(
        functools.partial(pack_kernel, ce, cn, cz, n_faces),
        out_shape=out,
        in_specs=[whole()] * 2 + [whole(pltpu.HBM)] * 4,
        out_specs=[whole()] * len(out),
        scratch_shapes=[
            VMEM((2, 5, ce, 2, SUB, LANES), F32),
            VMEM((2, 3, ce, 2, SUB, LANES), F32),
            VMEM((2, 5, ce, 2, SUB, LANES), F32),
            VMEM((2, 1, ce, 2, SUB, LANES), F32),
            pltpu.SemaphoreType.DMA((16 + 6 * n_faces,)),
        ],
        compiler_params=params(60),
        cost_estimate=cost(1 << 22, 4 << 20),
    )(*ends, start, source, flow, eddy)
    return got[:2], got[2:]


def split(x):
    high = x.astype(BF16)
    return high, (x - high.astype(F32)).astype(BF16)


def owner_of(turbine):
    return lax.shift_right_logical(turbine * 5462, 16)


def columns(x, first, size):
    return jnp.concatenate([x[:, k : k + 1] for k in range(first // LANES, (first + size) // LANES)], axis=0)


def lines(x, first, size):
    return jnp.concatenate([x[k : k + 1, :] for k in range(first // LANES, (first + size) // LANES)], axis=1)


def steps_of(chunks):
    sizes = [0] + [x for x in (LANES, 2 * LANES) if x < chunks * LANES] + [chunks * LANES]
    return list(zip(sizes[:-1], sizes[1:]))


def entries(live, cells, turbine, sector, weight, cz):
    cell, tur = cells[...], turbine[...]
    owner = owner_of(tur)
    key = (owner * SECT + sector[...]).astype(F32)
    local = (tur - owner * TURB_DEV).astype(F32)
    slot = lax.broadcasted_iota(jnp.int32, cell.shape, 0) * LANES + lax.broadcasted_iota(jnp.int32, cell.shape, 1)
    load = jnp.where(slot < live, weight[...], 0.0)
    line = lax.shift_right_logical(cell, cz.bit_length() - 1)
    level = jnp.bitwise_and(cell, cz - 1).astype(F32)
    return slot, line, level, key, local, load


def gather_edge(chosen, edge_row, level, key, local, load, put):
    chunks = chosen.shape[0]
    lower = lax.broadcasted_iota(jnp.int32, (LANES, LANES), 0) < lax.broadcasted_iota(jnp.int32, (LANES, LANES), 1)
    rank = jnp.dot(chosen.astype(BF16), jnp.where(lower, 1.0, 0.0).astype(BF16), preferred_element_type=F32)
    sums = jnp.sum(chosen, axis=1, keepdims=True)
    so_far = jnp.zeros((1, 1), F32)
    starts = []
    for k in range(chunks):
        starts.append(so_far)
        so_far = so_far + sums[k : k + 1]
    rank = jnp.where(chosen > 0.0, rank + jnp.concatenate(starts, axis=0), -1.0)
    total = jnp.sum(chosen).astype(jnp.int32)
    load_high = load.astype(BF16).astype(F32)
    load_rest = load - load_high
    load_mid = load_rest.astype(BF16).astype(F32)
    load_low = load_rest - load_mid
    blank = jnp.zeros((1, LANES), F32)
    rows = [
        jnp.concatenate([x[k : k + 1] for x in (edge_row, level, key, local, load_high, load_mid, load_low)] + [blank])
        for k in range(chunks)
    ]
    to = lax.broadcasted_iota(jnp.int32, (LANES, LANES), 0).astype(F32)
    for q in range(chunks):

        @pl.when(q * LANES < total)
        def _():
            where = jnp.concatenate(
                [jnp.where(rank[k : k + 1] - float(q * LANES) == to, 1.0, 0.0) for k in range(chunks)], axis=1
            ).astype(BF16)
            entries = jnp.concatenate(rows, axis=1).astype(BF16)
            put(q, lax.dot_general(entries, where, (((1,), (1,)), ((), ())), preferred_element_type=F32))

    return total


def rotor_terms(row, level, turbine, weight, key, table, blocks, acc):
    size = row.shape[0]
    rows, width = table.shape[0] // 2, table.shape[1]
    cz = width // COMPS
    lane_row = lax.broadcasted_iota(jnp.int32, (size, rows), 1).astype(F32)
    pick = jnp.where(row == lane_row, 1.0, 0.0).astype(BF16)
    got = jnp.dot(jnp.concatenate([pick, pick], axis=1), table[...], preferred_element_type=F32)
    here = level == lax.broadcasted_iota(jnp.int32, (size, cz), 1).astype(F32)
    lane = lax.broadcasted_iota(jnp.int32, (size, LANES), 1)
    lane_comp = owner_of(lane)
    lane_tur = (lane - lane_comp * TURB_DEV).astype(F32)
    spread = jnp.zeros((size, LANES), F32)
    for c in range(COMPS):
        part = jnp.where(here, got[:, c * cz : (c + 1) * cz], 0.0)
        spread = jnp.where(lane_comp == c, jnp.sum(part, axis=1, keepdims=True), spread)
    spread = jnp.where(turbine == lane_tur, spread * weight, 0.0)
    lane_key = lax.broadcasted_iota(jnp.int32, (blocks * SECT, size), 0).astype(F32)
    to = jnp.where(lane_key == key, 1.0, 0.0).astype(BF16)
    high = spread.astype(BF16)
    rest = spread - high.astype(F32)
    mid, low = split(rest)
    parts = jnp.dot(to, jnp.concatenate([high, mid, low], axis=1), preferred_element_type=F32)
    acc[...] += parts[:, :LANES] + parts[:, LANES : 2 * LANES] + parts[:, 2 * LANES :]


def halves(ref, f, i, rows, move=0):
    first, size = rows
    return [ref[f, i, h, pl.ds(PAD + first + move, size), :] for h in range(2)]


def level_shifts(x, first, last):
    up = [pltpu.roll(x[h], LANES - 1, 1) for h in range(2)]
    down = [pltpu.roll(x[h], 1, 1) for h in range(2)]
    return (
        [jnp.where(last, up[1], up[0]), jnp.where(last, 0.0, up[1])],
        [jnp.where(first, 0.0, down[0]), jnp.where(first, down[0], down[1])],
    )


def slab_sweep(ref, i, rows, first, last, src, flow, visc, curv):
    two = range(2)
    w = visc
    inv = [inverses(w[h]) for h in two]
    w2 = [2.0 * w[h] for h in two]

    def sides(f):
        mid = halves(ref, f, i, rows)
        a, b = halves(ref, f, i + 1, rows), halves(ref, f, i - 1, rows)
        n, s = halves(ref, f, i, rows, 1), halves(ref, f, i, rows, -1)
        up, down = level_shifts(mid, first, last)
        return mid, a, b, n, s, up, down

    _, a, b, n, s, up, down = sides(3)
    grad = [[x[h] - y[h] for h in two] for x, y in ((a, b), (n, s), (up, down))]
    q_sum = [(a[h] + b[h]) + (n[h] + s[h]) + (up[h] + down[h]) for h in two]
    out, div, bend = [], [0.0, 0.0], [0.0, 0.0]
    for c in range(3):
        mid, a, b, n, s, up, down = sides(c)
        res = []
        for h in two:
            total = (a[h] + b[h]) + (n[h] + s[h]) + (up[h] + down[h])
            slope = [a[h] - b[h], n[h] - s[h], up[h] - down[h]]
            carried = flow[0][h] * slope[0] + flow[1][h] * slope[1] + flow[2][h] * slope[2]
            res.append((src(c)[h] + 0.5 * (w2[h] * total + (carried - grad[c][h]))) * inv[h][0])
            div[h] = div[h] + slope[c]
            bend[h] = bend[h] + mid[h] * curv[c][h]
        out.append(res)
    out.append([(src(3)[h] + q_sum[h] - 0.5 * div[h]) * (1.0 / 7.0) for h in two])
    _, a, b, n, s, up, down = sides(4)
    res = []
    for h in two:
        total = (a[h] + b[h]) + (n[h] + s[h]) + (up[h] + down[h])
        res.append((src(4)[h] + w[h] * total + 0.25 * bend[h]) * inv[h][1])
    out.append(res)
    return out


def sweeps_kernel(
    ce, cn, cz, blocks, pair,
    count, start, source, flow, eddy, facep, facen, cells, turbine, sector, weight,
    final, held, grad, *refs,
):
    if not pair:
        coef_low, coef_high, items, n_items = refs[:4]
    v0, u, src, ed, v1, curv, table, sems = refs[-8:]
    copies = Copies(sems)
    two = range(2)
    has = [x > 0 for x in neighbours()[:2]]
    inner = pl.ds(PAD, cn)

    def part(h):
        return pl.ds(h * LANES, LANES)

    def halo(face, near, far, slab):
        pairs = []
        for h in two:
            pairs += [
                (face.at[0:5, :, part(h)], v0.at[:, near, h, inner]),
                (face.at[5:8, :, part(h)], u.at[:, near, h, inner]),
                (face.at[8, :, part(h)], ed.at[0, slab, h]),
                (face.at[9:14, :, part(h)], src.at[:, slab, h]),
                (face.at[14:19, :, part(h)], v0.at[:, far, h, inner]),
                (face.at[19:22, :, part(h)], u.at[:, far, h, inner]),
            ]
        return pairs

    ends = ((facep, 1, 0, 0), (facen, ce + 2, ce + 3, ce + 1))
    halos = [copies.take(*halo(*x)) for x in ends]

    def group(g):
        span, own, own2 = pl.ds(g, STEP), pl.ds(g + 1, STEP), pl.ds(g + 2, STEP)
        pairs = []
        for h in two:
            pairs += [
                (start.at[:, span, :, part(h)], v0.at[:, own2, h, inner]),
                (flow.at[:, span, :, part(h)], u.at[:, own2, h, inner]),
                (eddy.at[span, :, part(h)], ed.at[0, own, h]),
                (source.at[:, span, :, part(h)], src.at[:, own, h]),
            ]
        return pairs

    groups = [copies.take(*group(g)) for g in range(0, ce, STEP)]
    per = len(groups[0][1])
    copies.start(groups[0])
    for exists, taken in zip(has, halos):

        @pl.when(exists)
        def _():
            copies.start(taken)

    for taken in groups[1:]:
        copies.start(taken)

    blank = jnp.zeros((PAD, LANES), F32)
    for ref, fields in ((v0, 5), (u, 3), (v1, 5)):

        @pl.loop(0, ref.shape[1])
        def _(i):
            for f in range(fields):
                for h in two:
                    ref[f, i, h, 0:PAD, :] = blank
                    ref[f, i, h, PAD + cn : PAD + cn + PAD, :] = blank

    for exists, (_, near, _, _) in zip(has, ends):

        @pl.when(jnp.logical_not(exists))
        def _():
            for ref, fields in ((v0, 5), (u, 3)):
                for f in range(fields):
                    for h in two:
                        ref[f, near, h, inner, :] = jnp.zeros((cn, LANES), F32)

    def ends_of(size):
        lane = lax.broadcasted_iota(jnp.int32, (size, LANES), 1)
        return lane == 0, lane == LANES - 1

    live = count[0]
    slot, line, level, key, local, load = entries(live, cells, turbine, sector, weight, cz)
    chunks = slot.shape[0]
    if not pair:
        north = jnp.bitwise_and(line, cn - 1)
        east = lax.shift_right_logical(line, cn.bit_length() - 1)
        place = jnp.where(north == 0, 0, jnp.where(north == 1, 1, jnp.where(north == cn - 1, 2, 3)))
        is_edge = jnp.logical_or(north <= 1, north >= cn - 2)
        chosen = jnp.where(jnp.logical_and(is_edge, slot < live), 1.0, 0.0)
        edge_row = (place * ce + east).astype(F32)
        items[...] = jnp.zeros_like(items)

        def put(q, x):
            items[q] = x

        n_items[0] = gather_edge(chosen, edge_row, level, key, local, load, put)

    @pl.when(has[0])
    def _():
        copies.wait(halos[0])

    @pl.loop(0, ce + 2)
    def _(i):
        @pl.when(jnp.logical_and(i < ce, lax.rem(i, STEP) == 0))
        def _():
            copies.wait((groups[0][0] + lax.div(i, STEP) * per, group(i)))

        @pl.when(jnp.logical_and(i == ce, has[1]))
        def _():
            copies.wait(halos[1])

        real = jnp.logical_and(
            jnp.logical_or(i > 0, has[0]), jnp.logical_or(i < ce + 1, has[1])
        )

        @pl.when(real)
        def _():
            mid = i + 1
            first, last = ends_of(ROWS_1)
            for r in range(0, cn, ROWS_1):
                rows, at = (r, ROWS_1), pl.ds(r, ROWS_1)
                flows = [halves(u, k, mid, rows) for k in range(3)]
                bends = []
                for k in range(3):
                    a, b = halves(u, k, mid + 1, rows), halves(u, k, mid - 1, rows)
                    n, s = halves(u, k, mid, rows, 1), halves(u, k, mid, rows, -1)
                    up, down = level_shifts(flows[k], first, last)
                    res = [(a[h] + b[h]) + (n[h] + s[h]) + (up[h] + down[h]) - 6.0 * flows[k][h] for h in two]
                    for h in two:
                        curv[k, i, h, at, :] = res[h]
                    bends.append(res)
                out = slab_sweep(
                    v0, mid, rows, first, last,
                    lambda f: [src[f, i, h, at, :] for h in two],
                    flows, [1.0 + ed[0, i, h, at, :] for h in two], bends,
                )
                for f in range(5):
                    for h in two:
                        v1[f, i, h, pl.ds(PAD + r, ROWS_1), :] = out[f][h]

        @pl.when(jnp.logical_not(real))
        def _():
            for f in range(5):
                for h in two:
                    v1[f, i, h, inner, :] = jnp.zeros((cn, LANES), F32)

    def leave(e):
        return [(held.at[:, pl.ds(e, STEP)], final.at[:, pl.ds(e, STEP)])]

    outs = [copies.take(*leave(e)) for e in range(0, ce, STEP)]

    @pl.loop(0, ce)
    def _(e):
        i = e + 1
        first, last = ends_of(ROWS_2)

        for r in range(0, cn, ROWS_2):
            rows, span = (r, ROWS_2), pl.ds(r, ROWS_2)
            flows = [halves(u, k, i + 1, rows) for k in range(3)]
            bends = [[curv[k, i, h, span, :] for h in two] for k in range(3)]
            out = slab_sweep(
                v1, i, rows, first, last,
                lambda f: [src[f, i, h, span, :] for h in two],
                flows, [1.0 + ed[0, i, h, span, :] for h in two], bends,
            )
            at = pl.ds(pl.multiple_of(e * cn + r, ROWS_2), ROWS_2)
            below = pl.ds(pl.multiple_of((ce + e) * cn + r, ROWS_2), ROWS_2)
            for h in two:
                force = flows[0][h] * jnp.abs(flows[0][h])
                for f in range(5):
                    held[f, e, span, part(h)] = out[f][h]
                for c in range(COMPS):
                    hi, lo = split(out[c if c < 3 else 4][h] * force)
                    wide = pl.ds(c * cz + h * LANES, LANES)
                    table[at, wide] = hi
                    table[below, wide] = lo
        @pl.when(lax.rem(e, STEP) == STEP - 1)
        def _():
            copies.start((outs[0][0] + lax.div(e, STEP), leave(e - (STEP - 1))))


    def edge_plane(ref, k, first, tall, row):
        fields, slabs = ref.shape[:2]
        flat = ref.reshape(fields, slabs * 2 * tall, LANES)
        return jnp.concatenate(
            [flat[k, pl.ds((first * 2 + h) * tall + row, ce, stride=2 * tall), :] for h in two], axis=1
        )

    tall = PAD + cn + PAD
    edge_rows = () if pair else ((coef_low, 0, 1), (coef_high, cn - 1, cn - 2))
    for coef, row, behind in edge_rows:
        planes = [edge_plane(curv, k, 1, cn, row) for k in range(3)]
        planes += [edge_plane(u, 1, 2, tall, PAD + behind), edge_plane(ed, 0, 1, cn, behind), edge_plane(u, 0, 2, tall, PAD + behind)]
        planes += [edge_plane(v1, k, 1, tall, PAD + row) for k in range(3)]
        for k, x in enumerate(planes):
            coef[k * ce : (k + 1) * ce, :] = x

    row_t, level_t, local_t, load_t = line.astype(F32).T, level.T, local.T, load.T
    grad[...] = jnp.zeros_like(grad)
    for least, size in steps_of(chunks):

        @pl.when(jnp.logical_and(live > least, live <= size))
        def _():
            cols = [columns(x, 0, size) for x in (row_t, level_t, local_t, load_t)]
            rotor_terms(*cols, lines(key, 0, size), table, blocks, grad)

    for taken in outs:
        copies.wait(taken)


def sweeps(count, start, source, flow, eddy, faces, lists, blocks, pair):
    _, ce, cn, cz = start.shape
    chunks = lists[0].shape[0]
    tall = PAD + cn + PAD
    more = [shape(EDGE * ce, cz)] * 2 + [shape(chunks, ITEM, LANES), jax.ShapeDtypeStruct((1,), jnp.int32)]
    return pl.pallas_call(
        functools.partial(sweeps_kernel, ce, cn, cz, blocks, pair),
        out_shape=[shape(*start.shape)] * 2 + [shape(blocks * SECT, LANES)] + ([] if pair else more),
        in_specs=[whole(pltpu.SMEM)] + [whole(pltpu.HBM)] * 6 + [whole()] * 4,
        out_specs=[whole(pltpu.HBM), whole(), whole()] + ([] if pair else [whole()] * 3 + [whole(pltpu.SMEM)]),
        scratch_shapes=[
            VMEM((5, ce + 4, 2, tall, LANES), F32),
            VMEM((3, ce + 4, 2, tall, LANES), F32),
            VMEM((5, ce + 2, 2, cn, LANES), F32),
            VMEM((1, ce + 2, 2, cn, LANES), F32),
            VMEM((5, ce + 2, 2, tall, LANES), F32),
            VMEM((3, ce + 2, 2, cn, LANES), F32),
            VMEM((2 * ce * cn, COMPS * cz), BF16),
            pltpu.SemaphoreType.DMA((24 + 9 * (ce // STEP),)),
        ],
        compiler_params=params(48),
        cost_estimate=cost(0, 1 << 10),
    )(count, start, source, flow, eddy, *faces, *lists)


def edge_kernel(
    ce, cn, cz, blocks, copies_out,
    n_items, facep, facen, own_low, own_high, coef_low, coef_high, got_prev, got_next,
    held, items, grad, final_in,
    final, chunks,
    low_out, high_out, table, acc, sems,
):
    east, level = plane_shifts(ce, cz)
    sub = lax.broadcasted_iota(jnp.int32, (SUB, cz), 0)
    has = [x.astype(F32) for x in neighbours()]
    sides = (
        (-1.0, 0, own_low, coef_low, got_prev, low_out, 0),
        (1.0, cn - 1, own_high, coef_high, got_next, high_out, cn - SUB),
    )
    waits = []
    for side, (sign, row, own, coef, got, out_ref, place) in enumerate(sides):

        def plane(ref, f):
            return ref[f * ce : (f + 1) * ce, :]

        v0 = [plane(own, f) for f in range(5)]
        u = [plane(own, 5 + k) for k in range(3)]
        w = 1.0 + plane(own, 8)
        xv = [plane(got, f) for f in range(5)]
        xu = [plane(got, 5 + k) for k in range(3)]
        xw = 1.0 + plane(got, 8)
        xp = [plane(got, 9 + f) for f in range(5)]
        curv = [plane(coef, k) for k in range(3)]
        inv_v, inv_m = inverses(w)
        delta = one_way(1, sign, w, u[1], xv, inv_v, inv_m, dot3(v0, xu))
        back = one_way(1, -sign, xw, xu[1], v0, *inverses(xw), dot3(xv, u))
        x1 = [xp[f] + back[f] for f in range(5)]
        ends = []
        for far, face in enumerate((facep, facen)):
            hv = [got[PACK * ce + 8 * far + f : PACK * ce + 8 * far + f + 1, :] for f in range(8)]
            fv = [face[f, row : row + 1, :] * has[far] for f in range(5)]
            fu = face[6, row : row + 1, :] * has[far]
            fw = 1.0 + face[8, row : row + 1, :] * has[far]
            ends.append(one_way(1, sign, fw, fu, hv, *inverses(fw), dot3(fv, hv[5:])))
        x1 = [x * has[2 + side] for x in x1]
        total, slope0, slope2 = [], [], []
        for f in range(5):
            a, b = east(delta[f], ends[0][f], ends[1][f])
            h, l = level(delta[f])
            total.append((a + b) + (h + l))
            slope0.append(a - b)
            slope2.append(h - l)
        full = [plane(coef, 6 + c) + delta[c] for c in range(3)]
        add = one_way(1, sign, w, u[1], x1, inv_v, inv_m, dot3(full, xu) + dot3(delta, curv))
        press = (slope0[3], None, slope2[3])
        for c in range(3):
            more = w * total[c] + 0.5 * (u[0] * slope0[c] + u[2] * slope2[c])
            if press[c] is not None:
                more = more - 0.5 * press[c]
            add[c] = add[c] + more * inv_v
        add[3] = add[3] + (total[3] - 0.5 * (slope0[0] + slope2[2])) * (1.0 / 7.0)
        add[4] = add[4] + w * total[4] * inv_m
        ru1, rw, ru0 = plane(coef, 3), 1.0 + plane(coef, 4), plane(coef, 5)
        behind = one_way(1, sign, rw, ru1, delta, *inverses(rw))
        near, far = (0, 1) if side == 0 else (SUB - 1, SUB - 2)
        for f in range(5):
            for e in range(ce):
                rows = jnp.where(
                    sub == near, add[f][e : e + 1, :], jnp.where(sub == far, behind[f][e : e + 1, :], 0.0)
                )
                out_ref[f, e] = held[f, e, place : place + SUB, :] + rows
        copy = pltpu.make_async_copy(out_ref, final.at[:, :, pl.ds(place, SUB), :], sems.at[side])
        copy.start()
        waits.append(copy)
        for behind_row, u0, values in ((0, u[0], add), (1, ru0, behind)):
            force = u0 * jnp.abs(u0)
            at = (2 * side + behind_row) * ce
            for c in range(COMPS):
                hi, lo = split(values[c if c < 3 else 4] * force)
                table[at : at + ce, c * cz : (c + 1) * cz] = hi
                table[4 * ce + at : 5 * ce + at, c * cz : (c + 1) * cz] = lo

    acc[...] = grad[...]
    live = n_items[0]
    for least, size in steps_of(items.shape[0]):

        @pl.when(jnp.logical_and(live > least, live <= size))
        def _():
            lists = [items[k] for k in range(size // LANES)]
            turned = [x.T for x in lists]

            def col(j):
                return jnp.concatenate([x[:, j : j + 1] for x in turned], axis=0)

            key = jnp.concatenate([x[2:3] for x in lists], axis=1)
            rotor_terms(col(0), col(1), col(3), col(4) + col(5) + col(6), key, table, blocks, acc)

    for copy in range(copies_out):
        chunks[copy] = acc[...]
    for copy in waits:
        copy.wait()


def edges(n_items, faces, packs, coefs, gots, held, items, grad, final, blocks, size):
    _, ce, cn, cz = final.shape
    args = (n_items, *faces, *packs, *coefs, *gots, held, items, grad, final)
    tile = VMEM((5, ce, SUB, cz), F32)
    return pl.pallas_call(
        functools.partial(edge_kernel, ce, cn, cz, blocks, size),
        out_shape=(shape(*final.shape), shape(size, blocks * SECT, LANES)),
        in_specs=[whole(pltpu.SMEM)] + [whole()] * (len(args) - 2) + [whole(pltpu.HBM)],
        out_specs=(whole(pltpu.HBM), whole()),
        scratch_shapes=[
            tile,
            tile,
            VMEM((8 * ce, COMPS * cz), BF16),
            VMEM((blocks * SECT, LANES), F32),
            pltpu.SemaphoreType.DMA((2,)),
        ],
        input_output_aliases={len(args) - 1: 0},
        compiler_params=params(32),
        cost_estimate=cost(1 << 24, 4 << 20),
    )(*args)


def side(own):
    e = lax.axis_index("east")
    return 1 - e if own else e


def raw_kernel(ce, cn, cz, own, *refs):
    count, start, source, flow, eddy, *lists = refs[:9]
    rows, refs = refs[9], refs[10:]
    faces, refs = (refs[:1], refs[1:]) if own else ((), refs)
    tiles_v, tiles_u, tiles_s, tiles_e, cells, turbine, sector, weight, sems = refs
    copies = Copies(sems)
    high = side(own)
    first = pl.multiple_of(high * (cn - SUB), SUB)
    held = copies.take(*zip(lists, (cells, turbine, sector, weight)))
    copies.start(held)
    pairs = []
    for h in range(2):
        cut = (pl.ds(first, SUB), pl.ds(h * LANES, LANES))
        pairs += [
            (start.at[(slice(None), slice(None)) + cut], tiles_v.at[:, :, h]),
            (flow.at[(slice(None), slice(None)) + cut], tiles_u.at[:, :, h]),
            (eddy.at[(slice(None),) + cut], tiles_e.at[0, :, h]),
            (source.at[(slice(None), slice(None)) + cut], tiles_s.at[:, :, h]),
        ]
    needed = copies.take(*pairs)
    copies.start(needed)
    later = []
    for (near, far), face in zip(facing(ce), faces):
        later.append(
            copies.take(
                (start.at[:, near], face.at[0:5]),
                (flow.at[:, near], face.at[5:8]),
                (eddy.at[near], face.at[8]),
                (source.at[:, near], face.at[9:14]),
                (start.at[:, far], face.at[14:19]),
                (flow.at[:, far], face.at[19:22]),
            )
        )
        copies.start(later[-1])

    copies.wait(held)
    live = count[0]
    slot, line, level, key, local, load = entries(live, cells, turbine, sector, weight, cz)
    north = jnp.bitwise_and(line, cn - 1)
    column = lax.shift_right_logical(line, cn.bit_length() - 1) + lax.axis_index("east") * ce
    edge = high * (cn - 1)
    behind = edge + 1 - 2 * high
    chosen = jnp.where(jnp.logical_and(jnp.logical_or(north == edge, north == behind), slot < live), 1.0, 0.0)
    edge_row = (jnp.where(north == behind, 2 * ce, 0) + column).astype(F32)
    base = RAW * ce
    tail = rows.shape[0] - base
    rows[base:, :] = jnp.zeros((tail, cz), F32)

    def put(q, x):
        rows[base + q // 2 * ITEM : base + (q // 2 + 1) * ITEM, q % 2 * LANES : (q % 2 + 1) * LANES] = x

    total = gather_edge(chosen, edge_row, level, key, local, load, put)
    rows[base + tail - ITEM :, :] = jnp.full((ITEM, cz), total.astype(F32))

    def plane(ref, f, low, top):
        flat = ref.reshape(ref.shape[0], ce * 2 * SUB, LANES)
        parts = []
        for h in range(2):
            x, y = (flat[f, pl.ds(h * SUB + at, ce, stride=2 * SUB), :] for at in (low, top))
            parts.append(jnp.where(high > 0, y, x))
        return jnp.concatenate(parts, axis=1)

    copies.wait(needed)
    planes = [(tiles_v, f, 0) for f in range(5)] + [(tiles_u, k, 0) for k in range(3)] + [(tiles_e, 0, 0)]
    planes += [(tiles_s, f, 0) for f in range(5)]
    planes += [(tiles_v, f, 1) for f in range(5)] + [(tiles_u, k, 1) for k in range(3)] + [(tiles_e, 0, 1)]
    for k, (ref, f, at) in enumerate(planes):
        rows[k * ce : (k + 1) * ce, :] = plane(ref, f, at, SUB - 1 - at)
    for taken in later:
        copies.wait(taken)


def raw_rows(own, count, start, source, flow, eddy, lists):
    _, ce, cn, cz = start.shape
    chunks = lists[0].shape[0]
    out = [shape(RAW * ce + (chunks * LANES // cz + 1) * ITEM, cz)] + ([shape(FACE, cn, cz)] if own else [])
    return pl.pallas_call(
        functools.partial(raw_kernel, ce, cn, cz, own),
        out_shape=out,
        in_specs=[whole(pltpu.SMEM)] + [whole(pltpu.HBM)] * 8,
        out_specs=[whole()] * len(out),
        scratch_shapes=[
            VMEM((5, ce, 2, SUB, LANES), F32),
            VMEM((3, ce, 2, SUB, LANES), F32),
            VMEM((5, ce, 2, SUB, LANES), F32),
            VMEM((1, ce, 2, SUB, LANES), F32),
            VMEM((chunks, LANES), jnp.int32),
            VMEM((chunks, LANES), jnp.int32),
            VMEM((chunks, LANES), jnp.int32),
            VMEM((chunks, LANES), F32),
            pltpu.SemaphoreType.DMA((18,)),
        ],
        compiler_params=params(59),
        cost_estimate=cost(0, 1 << 10),
    )(count, start, source, flow, eddy, *lists)


def joined(ce, own, other, k):
    west = lax.axis_index("east") == 0
    a, b = own[k * ce : (k + 1) * ce, :], other[k * ce : (k + 1) * ce, :]
    return jnp.concatenate([jnp.where(west, a, b), jnp.where(west, b, a)], axis=0)


def join_kernel(ce, cz, own, other, pack, coef):
    sign = (2 * side(True) - 1).astype(F32)
    east, level = plane_shifts(2 * ce, cz)
    raw = [joined(ce, own, other, k) for k in range(RAW)]
    v, u, src, inner, inner_u = raw[:5], raw[5:8], raw[9:14], raw[14:19], raw[19:22]
    w = 1.0 + raw[8]
    inv_v, inv_m = inverses(w)
    total, slope0, slope2 = [], [], []
    for f in range(5):
        a, b = east(v[f])
        h, l = level(v[f])
        total.append((a + b) + (h + l))
        slope0.append(a - b)
        slope2.append(h - l)
    curv = []
    for k in range(3):
        a, b = east(u[k])
        h, l = level(u[k])
        curv.append((a + b) + (h + l) + inner_u[k] - 6.0 * u[k])
    out = one_way(1, -sign, w, u[1], inner, inv_v, inv_m, dot3(v, curv))
    press = (slope0[3], None, slope2[3])
    for c in range(3):
        more = src[c] + w * total[c] + 0.5 * (u[0] * slope0[c] + u[2] * slope2[c])
        if press[c] is not None:
            more = more - 0.5 * press[c]
        out[c] = out[c] + more * inv_v
    out[3] = out[3] + (src[3] + total[3] - 0.5 * (slope0[0] + slope2[2])) * (1.0 / 7.0)
    out[4] = out[4] + (src[4] + w * total[4]) * inv_m
    for k, x in enumerate(raw[:9] + out):
        pack[2 * k * ce : 2 * (k + 1) * ce, :] = x
    for k, x in enumerate(curv + [inner_u[1], raw[22], inner_u[0]]):
        coef[2 * k * ce : 2 * (k + 1) * ce, :] = x


def join_rows(own, other, ce):
    cz = own.shape[1]
    return pl.pallas_call(
        functools.partial(join_kernel, ce, cz),
        out_shape=[shape(PACK * 2 * ce, cz), shape(6 * 2 * ce, cz)],
        in_specs=[whole()] * 2,
        out_specs=[whole()] * 2,
        compiler_params=params(16),
        cost_estimate=cost(0, 1 << 10),
    )(own, other)


def put_rows(ce, cn, high, planes, tile, out_ref):
    cz = out_ref.shape[3]
    sub = lax.broadcasted_iota(jnp.int32, (SUB, cz), 0)
    near, far = high * (SUB - 1), 1 + high * (SUB - 3)
    place = pl.multiple_of(high * (cn - SUB), SUB)
    for f in range(5):
        for e in range(ce):
            rows = jnp.where(
                sub == near, planes[f][e : e + 1, :], jnp.where(sub == far, planes[5 + f][e : e + 1, :], 0.0)
            )
            out_ref[f, e] = tile(f, e, pl.ds(place, SUB)) + rows
    return pl.ds(place, SUB)


def both_kernel(
    ce, cn, cz, blocks, copies_out,
    own, other, pack, coef, got, held, grad, final_in,
    final, chunks, fix, rest,
    mine, tile_out, table, acc, sems,
):
    wide = 2 * ce
    high = side(True)
    sign = (2 * high - 1).astype(F32)
    north = lax.axis_index("north")
    exists = jnp.where(high > 0, north < lax.axis_size("north") - 1, north > 0).astype(F32)
    east, level = plane_shifts(wide, cz)

    def plane(ref, f):
        return ref[f * wide : (f + 1) * wide, :]

    v0 = [plane(pack, f) for f in range(5)]
    u = [plane(pack, 5 + k) for k in range(3)]
    w = 1.0 + plane(pack, 8)
    xv = [plane(got, f) for f in range(5)]
    xu = [plane(got, 5 + k) for k in range(3)]
    xw = 1.0 + plane(got, 8)
    curv = [plane(coef, k) for k in range(3)]
    inv_v, inv_m = inverses(w)
    delta = one_way(1, sign, w, u[1], xv, inv_v, inv_m, dot3(v0, xu))
    back = one_way(1, -sign, xw, xu[1], v0, *inverses(xw), dot3(xv, u))
    x1 = [(plane(got, 9 + f) + back[f]) * exists for f in range(5)]
    total, slope0, slope2 = [], [], []
    for f in range(5):
        a, b = east(delta[f])
        h, l = level(delta[f])
        total.append((a + b) + (h + l))
        slope0.append(a - b)
        slope2.append(h - l)
    full = [plane(pack, 9 + c) + delta[c] for c in range(3)]
    add = one_way(1, sign, w, u[1], x1, inv_v, inv_m, dot3(full, xu) + dot3(delta, curv))
    press = (slope0[3], None, slope2[3])
    for c in range(3):
        more = w * total[c] + 0.5 * (u[0] * slope0[c] + u[2] * slope2[c])
        if press[c] is not None:
            more = more - 0.5 * press[c]
        add[c] = add[c] + more * inv_v
    add[3] = add[3] + (total[3] - 0.5 * (slope0[0] + slope2[2])) * (1.0 / 7.0)
    add[4] = add[4] + w * total[4] * inv_m
    ru1, rw, ru0 = plane(coef, 3), 1.0 + plane(coef, 4), plane(coef, 5)
    behind = one_way(1, sign, rw, ru1, delta, *inverses(rw))
    west = lax.axis_index("east") == 0
    for k, x in enumerate(add + behind):
        mine[k] = jnp.where(west, x[:ce], x[ce:])
        fix[k * ce : (k + 1) * ce, :] = jnp.where(west, x[ce:], x[:ce])
    for row, u0, values in ((0, u[0], add), (1, ru0, behind)):
        force = u0 * jnp.abs(u0)
        for c in range(COMPS):
            hi, lo = split(values[c if c < 3 else 4] * force)
            table[row * wide : (row + 1) * wide, c * cz : (c + 1) * cz] = hi
            table[(2 + row) * wide : (3 + row) * wide, c * cz : (c + 1) * cz] = lo
    place = put_rows(ce, cn, high, mine, lambda f, e, at: held[f, e, at, :], tile_out)
    copy = pltpu.make_async_copy(tile_out, final.at[:, :, place, :], sems.at[0])
    copy.start()
    away = pl.ds(pl.multiple_of((1 - high) * (cn - SUB), SUB), SUB)
    for f in range(5):
        for e in range(ce):
            rest[f, e] = held[f, e, away, :]

    acc[...] = grad[...]
    base = RAW * ce
    tail = own.shape[0] - base
    most = (tail - ITEM) // ITEM * (cz // LANES)

    def chunk(ref, q):
        return ref[base + q // 2 * ITEM : base + (q // 2 + 1) * ITEM, q % 2 * LANES : (q % 2 + 1) * LANES]

    def terms(lists):
        turned = [x.T for x in lists]

        def col(j):
            return jnp.concatenate([x[:, j : j + 1] for x in turned], axis=0)

        key = jnp.concatenate([x[2:3] for x in lists], axis=1)
        rotor_terms(col(0), col(1), col(3), col(4) + col(5) + col(6), key, table, blocks, acc)

    terms([chunk(own, 0), chunk(other, 0)])
    for ref in (own, other):
        live = jnp.max(ref[base + tail - ITEM :, :LANES])

        @pl.when(live > float(LANES))
        def _():
            terms([chunk(ref, q) for q in range(1, min(2, most))])

        @pl.when(live > 2.0 * LANES)
        def _():
            terms([chunk(ref, q) for q in range(2, most)])

    for k in range(copies_out):
        chunks[k] = acc[...]
    copy.wait()


def both_edges(own, other, pack, coef, got, held, grad, final, blocks, size):
    _, ce, cn, cz = final.shape
    args = (own, other, pack, coef, got, held, grad, final)
    return pl.pallas_call(
        functools.partial(both_kernel, ce, cn, cz, blocks, size),
        out_shape=(shape(*final.shape), shape(size, blocks * SECT, LANES), shape(10 * ce, cz), shape(5, ce, SUB, cz)),
        in_specs=[whole()] * (len(args) - 1) + [whole(pltpu.HBM)],
        out_specs=(whole(pltpu.HBM), whole(), whole(), whole()),
        scratch_shapes=[
            VMEM((10, ce, cz), F32),
            VMEM((5, ce, SUB, cz), F32),
            VMEM((8 * ce, COMPS * cz), BF16),
            VMEM((blocks * SECT, LANES), F32),
            pltpu.SemaphoreType.DMA((1,)),
        ],
        input_output_aliases={len(args) - 1: 0},
        compiler_params=params(32),
        cost_estimate=cost(0, 1 << 10),
    )(*args)


def home_kernel(ce, cn, fix, rest, final_in, final, mine, tile_out, sems):
    for k in range(10):
        mine[k] = fix[k * ce : (k + 1) * ce, :]
    place = put_rows(ce, cn, side(False), mine, lambda f, e, at: rest[f, e], tile_out)
    copy = pltpu.make_async_copy(tile_out, final.at[:, :, place, :], sems.at[0])
    copy.start()
    copy.wait()


def rows_home(fix, rest, final):
    _, ce, cn, cz = final.shape
    return pl.pallas_call(
        functools.partial(home_kernel, ce, cn),
        out_shape=shape(*final.shape),
        in_specs=[whole()] * 2 + [whole(pltpu.HBM)],
        out_specs=whole(pltpu.HBM),
        scratch_shapes=[
            VMEM((10, ce, cz), F32),
            VMEM((5, ce, SUB, cz), F32),
            pltpu.SemaphoreType.DMA((1,)),
        ],
        input_output_aliases={2: 0},
        compiler_params=params(16),
        cost_estimate=cost(0, 1 << 10),
    )(fix, rest, final)


def sum_kernel(parts, out):
    total = jnp.sum(parts[...], axis=0)
    for c in range(COMPS):
        out[c] = total[:, c * TURB_DEV : (c + 1) * TURB_DEV]


def sum_parts(parts):
    return pl.pallas_call(
        sum_kernel,
        out_shape=shape(COMPS, SECT, TURB_DEV),
        in_specs=[whole()],
        out_specs=whole(),
        compiler_params=params(4),
        cost_estimate=cost(parts.size, parts.size * 4),
    )(parts)


def beside(x, size):
    if size == 2:
        got = lax.ppermute(x[0], "east", [(0, 1), (1, 0)])
        return got, got
    up = [(i, i + 1) for i in range(size - 1)]
    down = [(i + 1, i) for i in range(size - 1)]
    return lax.ppermute(x[1], "east", up), lax.ppermute(x[0], "east", down)


def north_ways(x, size):
    up = [(i, i + 1) for i in range(size - 1)]
    down = [(i + 1, i) for i in range(size - 1)]
    return lax.ppermute(x[1], "north", up), lax.ppermute(x[0], "north", down)


def shards(
    adjoint_start,
    adjoint_source,
    base_flow,
    eddy_visc,
    rotor_count,
    rotor_cell,
    rotor_turbine,
    rotor_sector,
    rotor_weight,
):
    _, ce, cn, cz = adjoint_start.shape
    n_east, n_north = lax.axis_size("east"), lax.axis_size("north")
    count = rotor_count.reshape(1)
    slots = rotor_cell.shape[-1]
    lists = [x.reshape(slots // LANES, LANES) for x in (rotor_cell, rotor_turbine, rotor_sector, rotor_weight)]

    fields = adjoint_start, adjoint_source, base_flow, eddy_visc
    if n_east == 2:
        return pair_shards(count, fields, lists, n_north)
    n_faces = 2
    ends = beside(row_ends(adjoint_start, base_flow, n_faces), n_east)
    packs, own = pack(ends, *fields, n_faces)
    gots = north_ways(packs, n_north)
    faces = beside(own, n_east)
    final, held, grad, coef_low, coef_high, items, n_items = sweeps(count, *fields, faces, lists, n_north, False)
    final, chunks = edges(
        n_items, faces, packs, (coef_low, coef_high), gots, held, items, grad, final, n_north, n_east
    )
    chunks = chunks.reshape(n_east * n_north, SECT, LANES)
    parts = lax.all_to_all(chunks, ("east", "north"), 0, 0, tiled=True)
    return (final, sum_parts(parts))


def pair_shards(count, fields, lists, n_north):
    ce = fields[0].shape[1]
    swap = [(0, 1), (1, 0)]
    (rows,) = raw_rows(False, count, *fields, lists)
    other = lax.ppermute(rows, "east", swap)
    own, face = raw_rows(True, count, *fields, lists)
    pack_both, coef = join_rows(own, other, ce)
    ways = [(n, n_north + n + 1) for n in range(n_north - 1)] + [(n_north + n, n - 1) for n in range(1, n_north)]
    got = lax.ppermute(pack_both, ("east", "north"), ways)
    faces = (lax.ppermute(face, "east", swap),) * 2
    final, held, grad = sweeps(count, *fields, faces, lists, n_north, True)
    final, chunks, fix, rest = both_edges(own, other, pack_both, coef, got, held, grad, final, n_north, 2)
    parts = lax.all_to_all(chunks.reshape(2 * n_north, SECT, LANES), ("east", "north"), 0, 0, tiled=True)
    final = rows_home(lax.ppermute(fix, "east", swap), rest, final)
    return (final, sum_parts(parts))


def solution(mesh):
    placed = (
        P(None, "east", "north", None),
        P(None, "east", "north", None),
        P(None, "east", "north", None),
        P("east", "north", None),
        P("east", "north"),
        P("east", "north", None),
        P("east", "north", None),
        P("east", "north", None),
        P("east", "north", None),
    )
    return jax.shard_map(
        shards,
        mesh=mesh,
        in_specs=placed,
        out_specs=(P(None, "east", "north", None), P(None, None, "north")),
        check_vma=False,
    )
```

```python
import functools

import jax
import jax.numpy as jnp
from jax import lax
from jax.experimental import pallas as pl
from jax.experimental.pallas import tpu as pltpu
from jax.sharding import PartitionSpec as P

SECT = 8
TURB_DEV = 12
COMPS = 4
LANES = 128
SUB = 8
PAD = 8
PACK = 14
FACE = 22
EDGE = 9
RAW = 23
ITEM = 8
STEP = 4
OUT_STEP = 4
ROWS_1 = 8
ROWS_2 = 16
VMEM = pltpu.VMEM
F32 = jnp.float32
BF16 = jnp.bfloat16


def whole(space=VMEM):
    return pl.BlockSpec(memory_space=space)


def in_hbm(*arrays):
    return [pltpu.with_memory_space_constraint(x, pltpu.HBM) for x in arrays]


def shape(*dims):
    return jax.ShapeDtypeStruct(dims, F32)


def params(mib):
    return pltpu.CompilerParams(vmem_limit_bytes=mib << 20)


def cost(flops, size):
    return pl.CostEstimate(flops=flops, bytes_accessed=size, transcendentals=0)


class Copies:
    def __init__(self, sems):
        self.sems, self.used = sems, 0

    def take(self, *pairs):
        first = self.used
        self.used += len(pairs)
        return first, pairs

    def made(self, taken):
        first, pairs = taken
        return [pltpu.make_async_copy(s, d, self.sems.at[first + k]) for k, (s, d) in enumerate(pairs)]

    def start(self, taken):
        for c in self.made(taken):
            c.start()

    def wait(self, taken):
        for c in self.made(taken):
            c.wait()


def neighbours():
    e, n = lax.axis_index("east"), lax.axis_index("north")
    last_e, last_n = lax.axis_size("east") - 1, lax.axis_size("north") - 1
    return [
        jnp.where(e > 0, 1, 0), jnp.where(e < last_e, 1, 0),
        jnp.where(n > 0, 1, 0), jnp.where(n < last_n, 1, 0),
    ]


def facing(ce):
    if lax.axis_size("east") == 2:
        e = lax.axis_index("east")
        return [((1 - e) * (ce - 1), (1 - e) * (ce - 1) + 2 * e - 1)]
    return [(0, 1), (ce - 1, ce - 2)]


def one_way(k, sign, w, u, f, inv_v, inv_m, bend=None):
    pull = (w + (0.5 * sign) * u) * inv_v
    out = [pull * f[c] for c in range(3)]
    out[k] = out[k] - (0.5 * sign) * f[3] * inv_v
    out.append((f[3] - (0.5 * sign) * f[k]) * (1.0 / 7.0))
    m = w * f[4]
    if bend is not None:
        m = m + 0.25 * bend
    out.append(m * inv_m)
    return out


def inverse(x):
    y = pl.reciprocal(x, approx=True)
    return y * (2.0 - x * y)


def inverses(w):
    six = 6.0 * w
    return inverse(six + 1.0), inverse(six + 2.0)


def dot3(a, b):
    return a[0] * b[0] + a[1] * b[1] + a[2] * b[2]


def plane_shifts(rows, cols):
    r = lax.broadcasted_iota(jnp.int32, (rows, cols), 0)
    z = lax.broadcasted_iota(jnp.int32, (rows, cols), 1)

    def east(x, before=0.0, after=0.0):
        return (
            jnp.where(r < rows - 1, pltpu.roll(x, rows - 1, 0), after),
            jnp.where(r > 0, pltpu.roll(x, 1, 0), before),
        )

    def level(x):
        return (
            jnp.where(z < cols - 1, pltpu.roll(x, cols - 1, 1), 0.0),
            jnp.where(z > 0, pltpu.roll(x, 1, 1), 0.0),
        )

    return east, level


def ends_kernel(ce, cn, n_faces, start, flow, *refs):
    outs, tiles_v, tiles_u, sems = refs[:n_faces], *refs[n_faces:]
    copies = Copies(sems)
    taken = []
    for i, (e, _) in enumerate(facing(ce)):
        pairs = []
        for side, first in enumerate((0, cn - SUB)):
            pairs.append((start.at[:, e, pl.ds(first, SUB)], tiles_v.at[i, side]))
            pairs.append((flow.at[:, e, pl.ds(first, SUB)], tiles_u.at[i, side]))
        taken.append(copies.take(*pairs))
        copies.start(taken[-1])
    for i, out in enumerate(outs):
        copies.wait(taken[i])
        for side, row in enumerate((0, SUB - 1)):
            for f in range(8):
                tile = tiles_v[i, side, f] if f < 5 else tiles_u[i, side, f - 5]
                out[side * 8 + f : side * 8 + f + 1, :] = tile[row : row + 1]


def row_ends(start, flow, n_faces):
    _, ce, cn, cz = start.shape
    return pl.pallas_call(
        functools.partial(ends_kernel, ce, cn, n_faces),
        out_shape=[shape(16, cz)] * n_faces,
        in_specs=[whole(pltpu.HBM)] * 2,
        out_specs=[whole()] * n_faces,
        scratch_shapes=[
            VMEM((n_faces, 2, 5, SUB, cz), F32),
            VMEM((n_faces, 2, 3, SUB, cz), F32),
            pltpu.SemaphoreType.DMA((4 * n_faces,)),
        ],
        compiler_params=params(60),
        cost_estimate=cost(0, 1 << 16),
    )(start, flow)


def pack_kernel(ce, cn, cz, n_faces, endp, endn, start, source, flow, eddy, *refs):
    packs, refs = refs[:2], refs[2:]
    faces, refs = refs[:n_faces], refs[n_faces:]
    tiles_v, tiles_u, tiles_s, tiles_e, sems = refs
    has = [x.astype(F32) for x in neighbours()[:2]]
    copies = Copies(sems)
    sides = ((0, 0, 1, -1.0), (cn - SUB, SUB - 1, SUB - 2, 1.0))
    needed = []
    for side, (first, _, _, _) in enumerate(sides):
        pairs = []
        for h in range(2):
            cut = (pl.ds(first, SUB), pl.ds(h * LANES, LANES))
            pairs += [
                (start.at[(slice(None), slice(None)) + cut], tiles_v.at[side, :, :, h]),
                (flow.at[(slice(None), slice(None)) + cut], tiles_u.at[side, :, :, h]),
                (eddy.at[(slice(None),) + cut], tiles_e.at[side, 0, :, h]),
                (source.at[(slice(None), slice(None)) + cut], tiles_s.at[side, :, :, h]),
            ]
        needed.append(copies.take(*pairs))
        copies.start(needed[-1])
    later = []
    for (near, far), face in zip(facing(ce), faces):
        taken = copies.take(
            (start.at[:, near], face.at[0:5]),
            (flow.at[:, near], face.at[5:8]),
            (eddy.at[near], face.at[8]),
            (source.at[:, near], face.at[9:14]),
            (start.at[:, far], face.at[14:19]),
            (flow.at[:, far], face.at[19:22]),
        )
        copies.start(taken)
        later.append(taken)
    east, level = plane_shifts(ce, cz)

    def line(ref, side, f, row):
        flat = ref.reshape(2, ref.shape[1], ce * 2 * SUB, LANES)
        return jnp.concatenate([flat[side, f, pl.ds(h * SUB + row, ce, stride=2 * SUB), :] for h in range(2)], axis=1)

    for side, (_, row, behind, sign) in enumerate(sides):
        copies.wait(needed[side])
        pack = packs[side]
        v = [line(tiles_v, side, f, row) for f in range(5)]
        u = [line(tiles_u, side, k, row) for k in range(3)]
        eddy_row = line(tiles_e, side, 0, row)
        inner = [line(tiles_v, side, f, behind) for f in range(5)]
        inner_u = [line(tiles_u, side, k, behind) for k in range(3)]
        src = [line(tiles_s, side, f, row) for f in range(5)]
        for f, x in enumerate(v + u + [eddy_row]):
            pack[f * ce : (f + 1) * ce, :] = x
        w = 1.0 + eddy_row
        inv_v, inv_m = inverses(w)
        before = [endp[side * 8 + f : side * 8 + f + 1, :] * has[0] for f in range(8)]
        after = [endn[side * 8 + f : side * 8 + f + 1, :] * has[1] for f in range(8)]
        for f in range(8):
            pack[PACK * ce + f : PACK * ce + f + 1, :] = before[f]
            pack[PACK * ce + 8 + f : PACK * ce + 9 + f, :] = after[f]
        total, slope0, slope2 = [], [], []
        for f in range(5):
            a, b = east(v[f], before[f], after[f])
            h, l = level(v[f])
            total.append((a + b) + (h + l))
            slope0.append(a - b)
            slope2.append(h - l)
        curv = []
        for k in range(3):
            a, b = east(u[k], before[5 + k], after[5 + k])
            h, l = level(u[k])
            curv.append((a + b) + (h + l) + inner_u[k] - 6.0 * u[k])
        out = one_way(1, -sign, w, u[1], inner, inv_v, inv_m, dot3(v, curv))
        press = (slope0[3], None, slope2[3])
        for c in range(3):
            more = src[c] + w * total[c] + 0.5 * (u[0] * slope0[c] + u[2] * slope2[c])
            if press[c] is not None:
                more = more - 0.5 * press[c]
            out[c] = out[c] + more * inv_v
        out[3] = out[3] + (src[3] + total[3] - 0.5 * (slope0[0] + slope2[2])) * (1.0 / 7.0)
        out[4] = out[4] + (src[4] + w * total[4]) * inv_m
        for f in range(5):
            pack[(9 + f) * ce : (10 + f) * ce, :] = out[f]
    for taken in later:
        copies.wait(taken)


def pack(ends, start, source, flow, eddy, n_faces):
    _, ce, cn, cz = start.shape
    out = [shape(PACK * ce + 16, cz)] * 2 + [shape(FACE, cn, cz)] * n_faces
    got = pl.pallas_call(
        functools.partial(pack_kernel, ce, cn, cz, n_faces),
        out_shape=out,
        in_specs=[whole()] * 2 + [whole(pltpu.HBM)] * 4,
        out_specs=[whole()] * len(out),
        scratch_shapes=[
            VMEM((2, 5, ce, 2, SUB, LANES), F32),
            VMEM((2, 3, ce, 2, SUB, LANES), F32),
            VMEM((2, 5, ce, 2, SUB, LANES), F32),
            VMEM((2, 1, ce, 2, SUB, LANES), F32),
            pltpu.SemaphoreType.DMA((16 + 6 * n_faces,)),
        ],
        compiler_params=params(60),
        cost_estimate=cost(1 << 22, 4 << 20),
    )(*ends, start, source, flow, eddy)
    return got[:2], got[2:]


def split(x):
    high = x.astype(BF16)
    return high, (x - high.astype(F32)).astype(BF16)


def owner_of(turbine):
    return lax.shift_right_logical(turbine * 5462, 16)


def columns(x, first, size):
    return jnp.concatenate([x[:, k : k + 1] for k in range(first // LANES, (first + size) // LANES)], axis=0)


def lines(x, first, size):
    return jnp.concatenate([x[k : k + 1, :] for k in range(first // LANES, (first + size) // LANES)], axis=1)


def steps_of(chunks):
    sizes = [0] + [x for x in (LANES, 2 * LANES) if x < chunks * LANES] + [chunks * LANES]
    return list(zip(sizes[:-1], sizes[1:]))


def entries(live, cells, turbine, sector, weight, cz):
    cell, tur = cells[...], turbine[...]
    owner = owner_of(tur)
    key = (owner * SECT + sector[...]).astype(F32)
    local = (tur - owner * TURB_DEV).astype(F32)
    slot = lax.broadcasted_iota(jnp.int32, cell.shape, 0) * LANES + lax.broadcasted_iota(jnp.int32, cell.shape, 1)
    load = jnp.where(slot < live, weight[...], 0.0)
    line = lax.shift_right_logical(cell, cz.bit_length() - 1)
    level = jnp.bitwise_and(cell, cz - 1).astype(F32)
    return slot, line, level, key, local, load


def gather_edge(chosen, edge_row, level, key, local, load, put):
    chunks = chosen.shape[0]
    lower = lax.broadcasted_iota(jnp.int32, (LANES, LANES), 0) < lax.broadcasted_iota(jnp.int32, (LANES, LANES), 1)
    rank = jnp.dot(chosen.astype(BF16), jnp.where(lower, 1.0, 0.0).astype(BF16), preferred_element_type=F32)
    sums = jnp.sum(chosen, axis=1, keepdims=True)
    so_far = jnp.zeros((1, 1), F32)
    starts = []
    for k in range(chunks):
        starts.append(so_far)
        so_far = so_far + sums[k : k + 1]
    rank = jnp.where(chosen > 0.0, rank + jnp.concatenate(starts, axis=0), -1.0)
    total = jnp.sum(chosen).astype(jnp.int32)
    load_high = load.astype(BF16).astype(F32)
    load_rest = load - load_high
    load_mid = load_rest.astype(BF16).astype(F32)
    load_low = load_rest - load_mid
    blank = jnp.zeros((1, LANES), F32)
    rows = [
        jnp.concatenate([x[k : k + 1] for x in (edge_row, level, key, local, load_high, load_mid, load_low)] + [blank])
        for k in range(chunks)
    ]
    to = lax.broadcasted_iota(jnp.int32, (LANES, LANES), 0).astype(F32)
    for q in range(chunks):

        @pl.when(q * LANES < total)
        def _():
            where = jnp.concatenate(
                [jnp.where(rank[k : k + 1] - float(q * LANES) == to, 1.0, 0.0) for k in range(chunks)], axis=1
            ).astype(BF16)
            entries = jnp.concatenate(rows, axis=1).astype(BF16)
            put(q, lax.dot_general(entries, where, (((1,), (1,)), ((), ())), preferred_element_type=F32))

    return total


def rotor_terms(row, level, turbine, weight, key, table, blocks, acc):
    size = row.shape[0]
    rows, width = table.shape[0] // 2, table.shape[1]
    cz = width // COMPS
    lane_row = lax.broadcasted_iota(jnp.int32, (size, rows), 1).astype(F32)
    pick = jnp.where(row == lane_row, 1.0, 0.0).astype(BF16)
    got = jnp.dot(jnp.concatenate([pick, pick], axis=1), table[...], preferred_element_type=F32)
    here = level == lax.broadcasted_iota(jnp.int32, (size, cz), 1).astype(F32)
    lane = lax.broadcasted_iota(jnp.int32, (size, LANES), 1)
    lane_comp = owner_of(lane)
    lane_tur = (lane - lane_comp * TURB_DEV).astype(F32)
    spread = jnp.zeros((size, LANES), F32)
    for c in range(COMPS):
        part = jnp.where(here, got[:, c * cz : (c + 1) * cz], 0.0)
        spread = jnp.where(lane_comp == c, jnp.sum(part, axis=1, keepdims=True), spread)
    spread = jnp.where(turbine == lane_tur, spread * weight, 0.0)
    lane_key = lax.broadcasted_iota(jnp.int32, (blocks * SECT, size), 0).astype(F32)
    to = jnp.where(lane_key == key, 1.0, 0.0).astype(BF16)
    high = spread.astype(BF16)
    rest = spread - high.astype(F32)
    mid, low = split(rest)
    parts = jnp.dot(to, jnp.concatenate([high, mid, low], axis=1), preferred_element_type=F32)
    acc[...] += parts[:, :LANES] + parts[:, LANES : 2 * LANES] + parts[:, 2 * LANES :]


def halves(ref, f, i, rows, move=0):
    first, size = rows
    return [ref[f, i, h, pl.ds(PAD + first + move, size), :] for h in range(2)]


def level_shifts(x, first, last):
    up = [pltpu.roll(x[h], LANES - 1, 1) for h in range(2)]
    down = [pltpu.roll(x[h], 1, 1) for h in range(2)]
    return (
        [jnp.where(last, up[1], up[0]), jnp.where(last, 0.0, up[1])],
        [jnp.where(first, 0.0, down[0]), jnp.where(first, down[0], down[1])],
    )


def slab_sweep(ref, i, rows, first, last, src, flow, visc, curv):
    two = range(2)
    w = visc
    inv = [inverses(w[h]) for h in two]
    w2 = [2.0 * w[h] for h in two]

    def sides(f):
        mid = halves(ref, f, i, rows)
        a, b = halves(ref, f, i + 1, rows), halves(ref, f, i - 1, rows)
        n, s = halves(ref, f, i, rows, 1), halves(ref, f, i, rows, -1)
        up, down = level_shifts(mid, first, last)
        return mid, a, b, n, s, up, down

    _, a, b, n, s, up, down = sides(3)
    grad = [[x[h] - y[h] for h in two] for x, y in ((a, b), (n, s), (up, down))]
    q_sum = [(a[h] + b[h]) + (n[h] + s[h]) + (up[h] + down[h]) for h in two]
    out, div, bend = [], [0.0, 0.0], [0.0, 0.0]
    for c in range(3):
        mid, a, b, n, s, up, down = sides(c)
        res = []
        for h in two:
            total = (a[h] + b[h]) + (n[h] + s[h]) + (up[h] + down[h])
            slope = [a[h] - b[h], n[h] - s[h], up[h] - down[h]]
            carried = flow[0][h] * slope[0] + flow[1][h] * slope[1] + flow[2][h] * slope[2]
            res.append((src(c)[h] + 0.5 * (w2[h] * total + (carried - grad[c][h]))) * inv[h][0])
            div[h] = div[h] + slope[c]
            bend[h] = bend[h] + mid[h] * curv[c][h]
        out.append(res)
    out.append([(src(3)[h] + q_sum[h] - 0.5 * div[h]) * (1.0 / 7.0) for h in two])
    _, a, b, n, s, up, down = sides(4)
    res = []
    for h in two:
        total = (a[h] + b[h]) + (n[h] + s[h]) + (up[h] + down[h])
        res.append((src(4)[h] + w[h] * total + 0.25 * bend[h]) * inv[h][1])
    out.append(res)
    return out


def sweeps_kernel(
    ce, cn, cz, blocks, pair,
    count, start, source, flow, eddy, facep, facen, cells, turbine, sector, weight,
    final, edge_low, edge_high, grad, *refs,
):
    if not pair:
        coef_low, coef_high, items, n_items = refs[:4]
    held, v0, u, src, ed, v1, curv, table, sems = refs[-9:]
    copies = Copies(sems)
    two = range(2)
    has = [x > 0 for x in neighbours()[:2]]
    inner = pl.ds(PAD, cn)

    def part(h):
        return pl.ds(h * LANES, LANES)

    def halo(face, near, far, slab):
        pairs = []
        for h in two:
            pairs += [
                (face.at[0:5, :, part(h)], v0.at[:, near, h, inner]),
                (face.at[5:8, :, part(h)], u.at[:, near, h, inner]),
                (face.at[8, :, part(h)], ed.at[0, slab, h]),
                (face.at[9:14, :, part(h)], src.at[:, slab, h]),
                (face.at[14:19, :, part(h)], v0.at[:, far, h, inner]),
                (face.at[19:22, :, part(h)], u.at[:, far, h, inner]),
            ]
        return pairs

    ends = ((facep, 1, 0, 0), (facen, ce + 2, ce + 3, ce + 1))
    halos = [copies.take(*halo(*x)) for x in ends]

    def group(g, size):
        span, own, own2 = pl.ds(g, size), pl.ds(g + 1, size), pl.ds(g + 2, size)
        pairs = []
        for h in two:
            pairs += [
                (start.at[:, span, :, part(h)], v0.at[:, own2, h, inner]),
                (flow.at[:, span, :, part(h)], u.at[:, own2, h, inner]),
                (eddy.at[span, :, part(h)], ed.at[0, own, h]),
                (source.at[:, span, :, part(h)], src.at[:, own, h]),
            ]
        return pairs

    groups = [copies.take(*group(g, STEP)) for g in range(0, ce, STEP)]
    per = len(groups[0][1])
    copies.start(groups[0])
    for exists, taken in zip(has, halos):

        @pl.when(exists)
        def _():
            copies.start(taken)

    for taken in groups[1:]:
        copies.start(taken)

    blank = jnp.zeros((PAD, LANES), F32)
    for ref, fields in ((v0, 5), (u, 3), (v1, 5)):

        @pl.loop(0, ref.shape[1])
        def _(i):
            for f in range(fields):
                for h in two:
                    ref[f, i, h, 0:PAD, :] = blank
                    ref[f, i, h, PAD + cn : PAD + cn + PAD, :] = blank

    for exists, (_, near, _, end) in zip(has, ends):

        @pl.when(jnp.logical_not(exists))
        def _():
            for ref, fields, slab in ((v0, 5, near), (u, 3, near), (v1, 5, end)):
                for f in range(fields):
                    for h in two:
                        ref[f, slab, h, inner, :] = jnp.zeros((cn, LANES), F32)

    def ends_of(size):
        lane = lax.broadcasted_iota(jnp.int32, (size, LANES), 1)
        return lane == 0, lane == LANES - 1

    live = count[0, 0]
    slot, line, level, key, local, load = entries(live, cells, turbine, sector, weight, cz)
    chunks = slot.shape[0]
    if not pair:
        north = jnp.bitwise_and(line, cn - 1)
        east = lax.shift_right_logical(line, cn.bit_length() - 1)
        place = jnp.where(north == 0, 0, jnp.where(north == 1, 1, jnp.where(north == cn - 1, 2, 3)))
        is_edge = jnp.logical_or(north <= 1, north >= cn - 2)
        chosen = jnp.where(jnp.logical_and(is_edge, slot < live), 1.0, 0.0)
        edge_row = (place * ce + east).astype(F32)
        items[...] = jnp.zeros_like(items)

        def put(q, x):
            items[q] = x

        n_items[0] = gather_edge(chosen, edge_row, level, key, local, load, put)

    @pl.when(has[0])
    def _():
        copies.wait(halos[0])

    low_slab, high_slab = jnp.where(has[0], 0, 1), jnp.where(has[1], ce + 2, ce + 1)
    steps = ce // STEP

    @pl.loop(0, steps)
    def _(g):
        copies.wait((groups[0][0] + g * per, group(g * STEP, STEP)))

        @pl.when(jnp.logical_and(g == steps - 1, has[1]))
        def _():
            copies.wait(halos[1])

        @pl.loop(jnp.where(g == 0, low_slab, g * STEP), jnp.where(g == steps - 1, high_slab, (g + 1) * STEP))
        def _(i):
            mid = i + 1
            first, last = ends_of(ROWS_1)
            for r in range(0, cn, ROWS_1):
                rows, at = (r, ROWS_1), pl.ds(r, ROWS_1)
                flows = [halves(u, k, mid, rows) for k in range(3)]
                bends = []
                for k in range(3):
                    a, b = halves(u, k, mid + 1, rows), halves(u, k, mid - 1, rows)
                    n, s = halves(u, k, mid, rows, 1), halves(u, k, mid, rows, -1)
                    up, down = level_shifts(flows[k], first, last)
                    res = [(a[h] + b[h]) + (n[h] + s[h]) + (up[h] + down[h]) - 6.0 * flows[k][h] for h in two]
                    for h in two:
                        curv[k, i, h, at, :] = res[h]
                    bends.append(res)
                out = slab_sweep(
                    v0, mid, rows, first, last,
                    lambda f: [src[f, i, h, at, :] for h in two],
                    flows, [1.0 + ed[0, i, h, at, :] for h in two], bends,
                )
                for f in range(5):
                    for h in two:
                        v1[f, i, h, pl.ds(PAD + r, ROWS_1), :] = out[f][h]

    def leave(e):
        return [(held.at[:, pl.ds(e, OUT_STEP)], final.at[:, pl.ds(e, OUT_STEP)])]

    outs = [copies.take(*leave(e)) for e in range(0, ce, OUT_STEP)]

    @pl.loop(0, ce // OUT_STEP)
    def _(g):
        @pl.loop(0, OUT_STEP)
        def _(k):
            e = g * OUT_STEP + k
            i = e + 1
            first, last = ends_of(ROWS_2)

            for r in range(0, cn, ROWS_2):
                rows, span = (r, ROWS_2), pl.ds(r, ROWS_2)
                flows = [halves(u, k, i + 1, rows) for k in range(3)]
                bends = [[curv[k, i, h, span, :] for h in two] for k in range(3)]
                out = slab_sweep(
                    v1, i, rows, first, last,
                    lambda f: [src[f, i, h, span, :] for h in two],
                    flows, [1.0 + ed[0, i, h, span, :] for h in two], bends,
                )
                at = pl.ds(pl.multiple_of(e * cn + r, ROWS_2), ROWS_2)
                below = pl.ds(pl.multiple_of((ce + e) * cn + r, ROWS_2), ROWS_2)
                for h in two:
                    force = flows[0][h] * jnp.abs(flows[0][h])
                    for f in range(5):
                        held[f, e, span, part(h)] = out[f][h]
                    for c in range(COMPS):
                        hi, lo = split(out[c if c < 3 else 4][h] * force)
                        wide = pl.ds(c * cz + h * LANES, LANES)
                        table[at, wide] = hi
                        table[below, wide] = lo

        copies.start((outs[0][0] + g, leave(g * OUT_STEP)))

    def edge_plane(ref, k, first, tall, row):
        fields, slabs = ref.shape[:2]
        flat = ref.reshape(fields, slabs * 2 * tall, LANES)
        return jnp.concatenate(
            [flat[k, pl.ds((first * 2 + h) * tall + row, ce, stride=2 * tall), :] for h in two], axis=1
        )

    tall = PAD + cn + PAD
    edge_rows = () if pair else ((coef_low, 0, 1), (coef_high, cn - 1, cn - 2))
    for coef, row, behind in edge_rows:
        planes = [edge_plane(curv, k, 1, cn, row) for k in range(3)]
        planes += [edge_plane(u, 1, 2, tall, PAD + behind), edge_plane(ed, 0, 1, cn, behind), edge_plane(u, 0, 2, tall, PAD + behind)]
        planes += [edge_plane(v1, k, 1, tall, PAD + row) for k in range(3)]
        for k, x in enumerate(planes):
            coef[k * ce : (k + 1) * ce, :] = x

    tiles = copies.take((held.at[:, :, 0:SUB, :], edge_low), (held.at[:, :, cn - SUB : cn, :], edge_high))
    copies.start(tiles)

    row_t, level_t, local_t, load_t = line.astype(F32).T, level.T, local.T, load.T
    grad[...] = jnp.zeros_like(grad)
    for least, size in steps_of(chunks):

        @pl.when(jnp.logical_and(live > least, live <= size))
        def _():
            cols = [columns(x, 0, size) for x in (row_t, level_t, local_t, load_t)]
            rotor_terms(*cols, lines(key, 0, size), table, blocks, grad)

    for taken in outs + [tiles]:
        copies.wait(taken)


def sweeps(count, start, source, flow, eddy, faces, lists, blocks, pair):
    _, ce, cn, cz = start.shape
    chunks = lists[0].shape[0]
    tall = PAD + cn + PAD
    more = [shape(EDGE * ce, cz)] * 2 + [shape(chunks, ITEM, LANES), jax.ShapeDtypeStruct((1,), jnp.int32)]
    return pl.pallas_call(
        functools.partial(sweeps_kernel, ce, cn, cz, blocks, pair),
        out_shape=[shape(*start.shape)] + [shape(5, ce, SUB, cz)] * 2 + [shape(blocks * SECT, LANES)] + ([] if pair else more),
        in_specs=[whole(pltpu.SMEM)] + [whole(pltpu.HBM)] * 6 + [whole()] * 4,
        out_specs=[whole(pltpu.HBM), whole(), whole(), whole()] + ([] if pair else [whole()] * 3 + [whole(pltpu.SMEM)]),
        scratch_shapes=[
            VMEM(start.shape, F32),
            VMEM((5, ce + 4, 2, tall, LANES), F32),
            VMEM((3, ce + 4, 2, tall, LANES), F32),
            VMEM((5, ce + 2, 2, cn, LANES), F32),
            VMEM((1, ce + 2, 2, cn, LANES), F32),
            VMEM((5, ce + 2, 2, tall, LANES), F32),
            VMEM((3, ce + 2, 2, cn, LANES), F32),
            VMEM((2 * ce * cn, COMPS * cz), BF16),
            pltpu.SemaphoreType.DMA((26 + 8 * (ce // STEP) + ce // OUT_STEP,)),
        ],
        compiler_params=params(48),
        cost_estimate=cost(0, 1 << 10),
    )(count, *in_hbm(start, source, flow, eddy), *faces, *lists)


def edge_kernel(
    ce, cn, cz, blocks, copies_out,
    n_items, facep, facen, own_low, own_high, coef_low, coef_high, got_prev, got_next,
    edge_low, edge_high, items, grad, final_in,
    final, chunks,
    low_out, high_out, table, acc, sems,
):
    east, level = plane_shifts(ce, cz)
    sub = lax.broadcasted_iota(jnp.int32, (SUB, cz), 0)
    has = [x.astype(F32) for x in neighbours()]
    sides = (
        (-1.0, 0, own_low, coef_low, got_prev, edge_low, low_out, 0),
        (1.0, cn - 1, own_high, coef_high, got_next, edge_high, high_out, cn - SUB),
    )
    waits = []
    for side, (sign, row, own, coef, got, edge, out_ref, place) in enumerate(sides):

        def plane(ref, f):
            return ref[f * ce : (f + 1) * ce, :]

        v0 = [plane(own, f) for f in range(5)]
        u = [plane(own, 5 + k) for k in range(3)]
        w = 1.0 + plane(own, 8)
        xv = [plane(got, f) for f in range(5)]
        xu = [plane(got, 5 + k) for k in range(3)]
        xw = 1.0 + plane(got, 8)
        xp = [plane(got, 9 + f) for f in range(5)]
        curv = [plane(coef, k) for k in range(3)]
        inv_v, inv_m = inverses(w)
        delta = one_way(1, sign, w, u[1], xv, inv_v, inv_m, dot3(v0, xu))
        back = one_way(1, -sign, xw, xu[1], v0, *inverses(xw), dot3(xv, u))
        x1 = [xp[f] + back[f] for f in range(5)]
        ends = []
        for far, face in enumerate((facep, facen)):
            hv = [got[PACK * ce + 8 * far + f : PACK * ce + 8 * far + f + 1, :] for f in range(8)]
            fv = [face[f, row : row + 1, :] * has[far] for f in range(5)]
            fu = face[6, row : row + 1, :] * has[far]
            fw = 1.0 + face[8, row : row + 1, :] * has[far]
            ends.append(one_way(1, sign, fw, fu, hv, *inverses(fw), dot3(fv, hv[5:])))
        x1 = [x * has[2 + side] for x in x1]
        total, slope0, slope2 = [], [], []
        for f in range(5):
            a, b = east(delta[f], ends[0][f], ends[1][f])
            h, l = level(delta[f])
            total.append((a + b) + (h + l))
            slope0.append(a - b)
            slope2.append(h - l)
        full = [plane(coef, 6 + c) + delta[c] for c in range(3)]
        add = one_way(1, sign, w, u[1], x1, inv_v, inv_m, dot3(full, xu) + dot3(delta, curv))
        press = (slope0[3], None, slope2[3])
        for c in range(3):
            more = w * total[c] + 0.5 * (u[0] * slope0[c] + u[2] * slope2[c])
            if press[c] is not None:
                more = more - 0.5 * press[c]
            add[c] = add[c] + more * inv_v
        add[3] = add[3] + (total[3] - 0.5 * (slope0[0] + slope2[2])) * (1.0 / 7.0)
        add[4] = add[4] + w * total[4] * inv_m
        ru1, rw, ru0 = plane(coef, 3), 1.0 + plane(coef, 4), plane(coef, 5)
        behind = one_way(1, sign, rw, ru1, delta, *inverses(rw))
        near, far = (0, 1) if side == 0 else (SUB - 1, SUB - 2)
        for f in range(5):
            for e in range(ce):
                rows = jnp.where(
                    sub == near, add[f][e : e + 1, :], jnp.where(sub == far, behind[f][e : e + 1, :], 0.0)
                )
                out_ref[f, e] = edge[f, e] + rows
        copy = pltpu.make_async_copy(out_ref, final.at[:, :, pl.ds(place, SUB), :], sems.at[side])
        copy.start()
        waits.append(copy)
        for behind_row, u0, values in ((0, u[0], add), (1, ru0, behind)):
            force = u0 * jnp.abs(u0)
            at = (2 * side + behind_row) * ce
            for c in range(COMPS):
                hi, lo = split(values[c if c < 3 else 4] * force)
                table[at : at + ce, c * cz : (c + 1) * cz] = hi
                table[4 * ce + at : 5 * ce + at, c * cz : (c + 1) * cz] = lo

    acc[...] = grad[...]
    live = n_items[0]
    for least, size in steps_of(items.shape[0]):

        @pl.when(jnp.logical_and(live > least, live <= size))
        def _():
            lists = [items[k] for k in range(size // LANES)]
            turned = [x.T for x in lists]

            def col(j):
                return jnp.concatenate([x[:, j : j + 1] for x in turned], axis=0)

            key = jnp.concatenate([x[2:3] for x in lists], axis=1)
            rotor_terms(col(0), col(1), col(3), col(4) + col(5) + col(6), key, table, blocks, acc)

    for copy in range(copies_out):
        chunks[copy] = acc[...]
    for copy in waits:
        copy.wait()


def edges(n_items, faces, packs, coefs, gots, tiles, items, grad, final, blocks, size):
    _, ce, cn, cz = final.shape
    args = (n_items, *faces, *packs, *coefs, *gots, *tiles, items, grad, final)
    tile = VMEM((5, ce, SUB, cz), F32)
    return pl.pallas_call(
        functools.partial(edge_kernel, ce, cn, cz, blocks, size),
        out_shape=(shape(*final.shape), shape(size, blocks * SECT, LANES)),
        in_specs=[whole(pltpu.SMEM)] + [whole()] * (len(args) - 2) + [whole(pltpu.HBM)],
        out_specs=(whole(pltpu.HBM), whole()),
        scratch_shapes=[
            tile,
            tile,
            VMEM((8 * ce, COMPS * cz), BF16),
            VMEM((blocks * SECT, LANES), F32),
            pltpu.SemaphoreType.DMA((2,)),
        ],
        input_output_aliases={len(args) - 1: 0},
        compiler_params=params(32),
        cost_estimate=cost(1 << 24, 4 << 20),
    )(*args)


def side(own):
    e = lax.axis_index("east")
    return 1 - e if own else e


def raw_kernel(ce, cn, cz, own, *refs):
    if own:
        count, refs = refs[0], refs[1:]
    start, source, flow, eddy, refs = *refs[:4], refs[4:]
    if own:
        lists, (rows, face, *items), refs = refs[:4], refs[4:8], refs[8:]
        cells, turbine, sector, weight, sems = refs[4:]
    else:
        rows, sems = refs[0], refs[-1]
        refs = refs[1:]
    tiles_v, tiles_u, tiles_s, tiles_e = refs[:4]
    copies = Copies(sems)
    high = side(own)
    first = pl.multiple_of(high * (cn - SUB), SUB)
    if own:
        held = copies.take(*zip(lists, (cells, turbine, sector, weight)))
        copies.start(held)
    pairs = []
    for h in range(2):
        cut = (pl.ds(first, SUB), pl.ds(h * LANES, LANES))
        pairs += [
            (start.at[(slice(None), slice(None)) + cut], tiles_v.at[:, :, h]),
            (flow.at[(slice(None), slice(None)) + cut], tiles_u.at[:, :, h]),
            (eddy.at[(slice(None),) + cut], tiles_e.at[0, :, h]),
            (source.at[(slice(None), slice(None)) + cut], tiles_s.at[:, :, h]),
        ]
    needed = copies.take(*pairs)
    copies.start(needed)
    if own:
        ((near, far),) = facing(ce)
        later = copies.take(
            (start.at[:, near], face.at[0:5]),
            (flow.at[:, near], face.at[5:8]),
            (eddy.at[near], face.at[8]),
            (source.at[:, near], face.at[9:14]),
            (start.at[:, far], face.at[14:19]),
            (flow.at[:, far], face.at[19:22]),
        )
        copies.start(later)
        copies.wait(held)
        live = count[0, 0]
        listed = entries(live, cells, turbine, sector, weight, cz)
        for ref, which in zip(items, (high, 1 - high)):
            edge_items(ce, cn, cz, live, listed, which, ref)

    def plane(ref, f, low, top):
        flat = ref.reshape(ref.shape[0], ce * 2 * SUB, LANES)
        parts = []
        for h in range(2):
            x, y = (flat[f, pl.ds(h * SUB + at, ce, stride=2 * SUB), :] for at in (low, top))
            parts.append(jnp.where(high > 0, y, x))
        return jnp.concatenate(parts, axis=1)

    copies.wait(needed)
    planes = [(tiles_v, f, 0) for f in range(5)] + [(tiles_u, k, 0) for k in range(3)] + [(tiles_e, 0, 0)]
    planes += [(tiles_s, f, 0) for f in range(5)]
    planes += [(tiles_v, f, 1) for f in range(5)] + [(tiles_u, k, 1) for k in range(3)] + [(tiles_e, 0, 1)]
    for k, (ref, f, at) in enumerate(planes):
        rows[k * ce : (k + 1) * ce, :] = plane(ref, f, at, SUB - 1 - at)
    if own:
        copies.wait(later)


def edge_items(ce, cn, cz, live, listed, high, out):
    slot, line, level, key, local, load = listed
    north = jnp.bitwise_and(line, cn - 1)
    column = lax.shift_right_logical(line, cn.bit_length() - 1) + lax.axis_index("east") * ce
    edge = high * (cn - 1)
    behind = edge + 1 - 2 * high
    chosen = jnp.where(jnp.logical_and(jnp.logical_or(north == edge, north == behind), slot < live), 1.0, 0.0)
    edge_row = (jnp.where(north == behind, 2 * ce, 0) + column).astype(F32)
    out[...] = jnp.zeros_like(out)

    def put(q, x):
        out[q // 2 * ITEM : (q // 2 + 1) * ITEM, q % 2 * LANES : (q % 2 + 1) * LANES] = x

    total = gather_edge(chosen, edge_row, level, key, local, load, put)
    out[out.shape[0] - ITEM :, :] = jnp.full((ITEM, cz), total.astype(F32))


def raw_rows(own, start, source, flow, eddy, count=None, lists=()):
    _, ce, cn, cz = start.shape
    out = [shape(RAW * ce, cz)]
    scratch = [
        VMEM((5, ce, 2, SUB, LANES), F32),
        VMEM((3, ce, 2, SUB, LANES), F32),
        VMEM((5, ce, 2, SUB, LANES), F32),
        VMEM((1, ce, 2, SUB, LANES), F32),
    ]
    if own:
        chunks = lists[0].shape[0]
        out += [shape(FACE, cn, cz)] + [shape((chunks * LANES // cz + 1) * ITEM, cz)] * 2
        scratch += [VMEM((chunks, LANES), x.dtype) for x in lists]
    return pl.pallas_call(
        functools.partial(raw_kernel, ce, cn, cz, own),
        out_shape=out,
        in_specs=([whole(pltpu.SMEM)] if own else []) + [whole(pltpu.HBM)] * (4 + len(lists)),
        out_specs=[whole()] * len(out),
        scratch_shapes=scratch + [pltpu.SemaphoreType.DMA((18,))],
        compiler_params=params(16),
        cost_estimate=cost(0, 1 << 10),
    )(*([count] if own else []), *in_hbm(start, source, flow, eddy, *lists))


def joined(ce, own, other, k):
    west = lax.axis_index("east") == 0
    a, b = own[k * ce : (k + 1) * ce, :], other[k * ce : (k + 1) * ce, :]
    return jnp.concatenate([jnp.where(west, a, b), jnp.where(west, b, a)], axis=0)


def join_kernel(ce, cz, own, other, pack, coef):
    sign = (2 * side(True) - 1).astype(F32)
    east, level = plane_shifts(2 * ce, cz)
    raw = [joined(ce, own, other, k) for k in range(RAW)]
    v, u, src, inner, inner_u = raw[:5], raw[5:8], raw[9:14], raw[14:19], raw[19:22]
    w = 1.0 + raw[8]
    inv_v, inv_m = inverses(w)
    total, slope0, slope2 = [], [], []
    for f in range(5):
        a, b = east(v[f])
        h, l = level(v[f])
        total.append((a + b) + (h + l))
        slope0.append(a - b)
        slope2.append(h - l)
    curv = []
    for k in range(3):
        a, b = east(u[k])
        h, l = level(u[k])
        curv.append((a + b) + (h + l) + inner_u[k] - 6.0 * u[k])
    out = one_way(1, -sign, w, u[1], inner, inv_v, inv_m, dot3(v, curv))
    press = (slope0[3], None, slope2[3])
    for c in range(3):
        more = src[c] + w * total[c] + 0.5 * (u[0] * slope0[c] + u[2] * slope2[c])
        if press[c] is not None:
            more = more - 0.5 * press[c]
        out[c] = out[c] + more * inv_v
    out[3] = out[3] + (src[3] + total[3] - 0.5 * (slope0[0] + slope2[2])) * (1.0 / 7.0)
    out[4] = out[4] + (src[4] + w * total[4]) * inv_m
    for k, x in enumerate(raw[:9] + out):
        pack[2 * k * ce : 2 * (k + 1) * ce, :] = x
    for k, x in enumerate(curv + [inner_u[1], raw[22], inner_u[0]]):
        coef[2 * k * ce : 2 * (k + 1) * ce, :] = x


def join_rows(own, other, ce):
    cz = own.shape[1]
    return pl.pallas_call(
        functools.partial(join_kernel, ce, cz),
        out_shape=[shape(PACK * 2 * ce, cz), shape(6 * 2 * ce, cz)],
        in_specs=[whole()] * 2,
        out_specs=[whole()] * 2,
        compiler_params=params(16),
        cost_estimate=cost(0, 1 << 10),
    )(own, other)


def both_kernel(
    ce, cn, cz, blocks, copies_out,
    own, other, pack, coef, got, grad,
    chunks, mine, fix,
    table, acc,
):
    wide = 2 * ce
    high = side(True)
    sign = (2 * high - 1).astype(F32)
    north = lax.axis_index("north")
    exists = jnp.where(high > 0, north < lax.axis_size("north") - 1, north > 0).astype(F32)
    east, level = plane_shifts(wide, cz)

    def plane(ref, f):
        return ref[f * wide : (f + 1) * wide, :]

    v0 = [plane(pack, f) for f in range(5)]
    u = [plane(pack, 5 + k) for k in range(3)]
    w = 1.0 + plane(pack, 8)
    xv = [plane(got, f) for f in range(5)]
    xu = [plane(got, 5 + k) for k in range(3)]
    xw = 1.0 + plane(got, 8)
    curv = [plane(coef, k) for k in range(3)]
    inv_v, inv_m = inverses(w)
    delta = one_way(1, sign, w, u[1], xv, inv_v, inv_m, dot3(v0, xu))
    back = one_way(1, -sign, xw, xu[1], v0, *inverses(xw), dot3(xv, u))
    x1 = [(plane(got, 9 + f) + back[f]) * exists for f in range(5)]
    total, slope0, slope2 = [], [], []
    for f in range(5):
        a, b = east(delta[f])
        h, l = level(delta[f])
        total.append((a + b) + (h + l))
        slope0.append(a - b)
        slope2.append(h - l)
    full = [plane(pack, 9 + c) + delta[c] for c in range(3)]
    add = one_way(1, sign, w, u[1], x1, inv_v, inv_m, dot3(full, xu) + dot3(delta, curv))
    press = (slope0[3], None, slope2[3])
    for c in range(3):
        more = w * total[c] + 0.5 * (u[0] * slope0[c] + u[2] * slope2[c])
        if press[c] is not None:
            more = more - 0.5 * press[c]
        add[c] = add[c] + more * inv_v
    add[3] = add[3] + (total[3] - 0.5 * (slope0[0] + slope2[2])) * (1.0 / 7.0)
    add[4] = add[4] + w * total[4] * inv_m
    ru1, rw, ru0 = plane(coef, 3), 1.0 + plane(coef, 4), plane(coef, 5)
    behind = one_way(1, sign, rw, ru1, delta, *inverses(rw))
    west = lax.axis_index("east") == 0
    for k, x in enumerate(add + behind):
        mine[k * ce : (k + 1) * ce, :] = jnp.where(west, x[:ce], x[ce:])
        fix[k * ce : (k + 1) * ce, :] = jnp.where(west, x[ce:], x[:ce])
    for row, u0, values in ((0, u[0], add), (1, ru0, behind)):
        force = u0 * jnp.abs(u0)
        for c in range(COMPS):
            hi, lo = split(values[c if c < 3 else 4] * force)
            table[row * wide : (row + 1) * wide, c * cz : (c + 1) * cz] = hi
            table[(2 + row) * wide : (3 + row) * wide, c * cz : (c + 1) * cz] = lo

    acc[...] = grad[...]
    most = (own.shape[0] // ITEM - 1) * (cz // LANES)

    def chunk(ref, q):
        return ref[q // 2 * ITEM : (q // 2 + 1) * ITEM, q % 2 * LANES : (q % 2 + 1) * LANES]

    def terms(lists):
        turned = [x.T for x in lists]

        def col(j):
            return jnp.concatenate([x[:, j : j + 1] for x in turned], axis=0)

        key = jnp.concatenate([x[2:3] for x in lists], axis=1)
        rotor_terms(col(0), col(1), col(3), col(4) + col(5) + col(6), key, table, blocks, acc)

    terms([chunk(own, 0), chunk(other, 0)])
    for ref in (own, other):
        live = jnp.max(ref[ref.shape[0] - ITEM :, :LANES])

        @pl.when(live > float(LANES))
        def _():
            terms([chunk(ref, q) for q in range(1, min(2, most))])

        @pl.when(live > 2.0 * LANES)
        def _():
            terms([chunk(ref, q) for q in range(2, most)])

    for k in range(copies_out):
        chunks[k] = acc[...]


def both_edges(own, other, pack, coef, got, grad, size, blocks, copies_out):
    _, ce, cn, cz = size
    return pl.pallas_call(
        functools.partial(both_kernel, ce, cn, cz, blocks, copies_out),
        out_shape=(shape(copies_out, blocks * SECT, LANES), shape(10 * ce, cz), shape(10 * ce, cz)),
        in_specs=[whole()] * 6,
        out_specs=(whole(), whole(), whole()),
        scratch_shapes=[
            VMEM((8 * ce, COMPS * cz), BF16),
            VMEM((blocks * SECT, LANES), F32),
        ],
        compiler_params=params(32),
        cost_estimate=cost(0, 1 << 10),
    )(own, other, pack, coef, got, grad)


def home_kernel(ce, cn, mine, fix, edge_low, edge_high, final_in, final, low_out, high_out, sems):
    cz = edge_low.shape[3]
    sub = lax.broadcasted_iota(jnp.int32, (SUB, cz), 0)
    high = side(True) > 0
    waits = []
    for k, (edge, out, near, far, place) in enumerate(
        ((edge_low, low_out, 0, 1, 0), (edge_high, high_out, SUB - 1, SUB - 2, cn - SUB))
    ):
        from_mine = high if k else jnp.logical_not(high)
        for f in range(5):

            def plane(at):
                span = pl.ds(at * ce, ce)
                return jnp.where(from_mine, mine[span, :], fix[span, :])

            a, b = plane(f), plane(5 + f)
            for e in range(ce):
                rows = jnp.where(sub == near, a[e : e + 1, :], jnp.where(sub == far, b[e : e + 1, :], 0.0))
                out[f, e] = edge[f, e] + rows
        copy = pltpu.make_async_copy(out, final.at[:, :, pl.ds(place, SUB), :], sems.at[k])
        copy.start()
        waits.append(copy)
    for copy in waits:
        copy.wait()


def rows_home(mine, fix, tiles, final):
    _, ce, cn, cz = final.shape
    return pl.pallas_call(
        functools.partial(home_kernel, ce, cn),
        out_shape=shape(*final.shape),
        in_specs=[whole()] * 4 + [whole(pltpu.HBM)],
        out_specs=whole(pltpu.HBM),
        scratch_shapes=[
            VMEM((5, ce, SUB, cz), F32),
            VMEM((5, ce, SUB, cz), F32),
            pltpu.SemaphoreType.DMA((2,)),
        ],
        input_output_aliases={4: 0},
        compiler_params=params(16),
        cost_estimate=cost(0, 1 << 10),
    )(mine, fix, *tiles, final)


def sum_kernel(parts, out):
    total = jnp.sum(parts[...], axis=0)
    for c in range(COMPS):
        out[c] = total[:, c * TURB_DEV : (c + 1) * TURB_DEV]


def sum_parts(parts):
    return pl.pallas_call(
        sum_kernel,
        out_shape=shape(COMPS, SECT, TURB_DEV),
        in_specs=[whole()],
        out_specs=whole(),
        compiler_params=params(4),
        cost_estimate=cost(parts.size, parts.size * 4),
    )(parts)


def beside(x, size):
    if size == 2:
        got = lax.ppermute(x[0], "east", [(0, 1), (1, 0)])
        return got, got
    up = [(i, i + 1) for i in range(size - 1)]
    down = [(i + 1, i) for i in range(size - 1)]
    return lax.ppermute(x[1], "east", up), lax.ppermute(x[0], "east", down)


def north_ways(x, size):
    up = [(i, i + 1) for i in range(size - 1)]
    down = [(i + 1, i) for i in range(size - 1)]
    return lax.ppermute(x[1], "north", up), lax.ppermute(x[0], "north", down)


def shards(
    adjoint_start,
    adjoint_source,
    base_flow,
    eddy_visc,
    rotor_count,
    rotor_cell,
    rotor_turbine,
    rotor_sector,
    rotor_weight,
):
    _, ce, cn, cz = adjoint_start.shape
    n_east, n_north = lax.axis_size("east"), lax.axis_size("north")
    count = rotor_count
    slots = rotor_cell.shape[-1]
    lists = [x.reshape(slots // LANES, LANES) for x in (rotor_cell, rotor_turbine, rotor_sector, rotor_weight)]

    fields = adjoint_start, adjoint_source, base_flow, eddy_visc
    if n_east == 2:
        return pair_shards(count, fields, lists, n_north)
    n_faces = 2
    ends = beside(row_ends(adjoint_start, base_flow, n_faces), n_east)
    packs, own = pack(ends, *fields, n_faces)
    gots = north_ways(packs, n_north)
    faces = beside(own, n_east)
    final, *tiles, grad, coef_low, coef_high, items, n_items = sweeps(count, *fields, faces, lists, n_north, False)
    final, chunks = edges(
        n_items, faces, packs, (coef_low, coef_high), gots, tiles, items, grad, final, n_north, n_east
    )
    chunks = chunks.reshape(n_east * n_north, SECT, LANES)
    parts = lax.all_to_all(chunks, ("east", "north"), 0, 0, tiled=True)
    return (final, sum_parts(parts))


def pair_shards(count, fields, lists, n_north):
    ce = fields[0].shape[1]
    swap = [(0, 1), (1, 0)]
    (rows,) = raw_rows(False, *fields)
    other = lax.ppermute(rows, "east", swap)
    own, face, items, items_out = raw_rows(True, *fields, count, lists)
    pack_both, coef = join_rows(own, other, ce)
    ways = [(n, n_north + n + 1) for n in range(n_north - 1)] + [(n_north + n, n - 1) for n in range(1, n_north)]
    got = lax.ppermute(pack_both, ("east", "north"), ways)
    faces = (lax.ppermute(face, "east", swap),) * 2
    items_in = lax.ppermute(items_out, "east", swap)
    final, *tiles, grad = sweeps(count, *fields, faces, lists, n_north, True)
    chunks, mine, fix = both_edges(items, items_in, pack_both, coef, got, grad, fields[0].shape, n_north, 2)
    parts = lax.all_to_all(chunks.reshape(2 * n_north, SECT, LANES), ("east", "north"), 0, 0, tiled=True)
    final = rows_home(mine, lax.ppermute(fix, "east", swap), tiles, final)
    return (final, sum_parts(parts))


def solution(mesh):
    placed = (
        P(None, "east", "north", None),
        P(None, "east", "north", None),
        P(None, "east", "north", None),
        P("east", "north", None),
        P("east", "north"),
        P("east", "north", None),
        P("east", "north", None),
        P("east", "north", None),
        P("east", "north", None),
    )
    return jax.shard_map(
        shards,
        mesh=mesh,
        in_specs=placed,
        out_specs=(P(None, "east", "north", None), P(None, None, "north")),
        check_vma=False,
    )
```

```python
import functools

import jax
import jax.numpy as jnp
from jax import lax
from jax.experimental import pallas as pl
from jax.experimental.pallas import tpu as pltpu
from jax.sharding import PartitionSpec as P

SECT = 8
TURB_DEV = 12
COMPS = 4
LANES = 128
SUB = 8
PAD = 8
PACK = 14
FACE = 22
EDGE = 9
RAW = 23
ITEM = 8
STEP = 4
OUT_STEP = 4
ROWS_1 = 8
ROWS_2 = 16
VMEM = pltpu.VMEM
F32 = jnp.float32
BF16 = jnp.bfloat16


def whole(space=VMEM):
    return pl.BlockSpec(memory_space=space)


def in_hbm(*arrays):
    return [pltpu.with_memory_space_constraint(x, pltpu.HBM) for x in arrays]


def shape(*dims):
    return jax.ShapeDtypeStruct(dims, F32)


def params(mib):
    return pltpu.CompilerParams(vmem_limit_bytes=mib << 20)


def cost(flops, size):
    return pl.CostEstimate(flops=flops, bytes_accessed=size, transcendentals=0)


class Copies:
    def __init__(self, sems):
        self.sems, self.used = sems, 0

    def take(self, *pairs):
        first = self.used
        self.used += len(pairs)
        return first, pairs

    def made(self, taken):
        first, pairs = taken
        return [pltpu.make_async_copy(s, d, self.sems.at[first + k]) for k, (s, d) in enumerate(pairs)]

    def start(self, taken):
        for c in self.made(taken):
            c.start()

    def wait(self, taken):
        for c in self.made(taken):
            c.wait()


def neighbours():
    e, n = lax.axis_index("east"), lax.axis_index("north")
    last_e, last_n = lax.axis_size("east") - 1, lax.axis_size("north") - 1
    return [
        jnp.where(e > 0, 1, 0), jnp.where(e < last_e, 1, 0),
        jnp.where(n > 0, 1, 0), jnp.where(n < last_n, 1, 0),
    ]


def facing(ce):
    if lax.axis_size("east") == 2:
        e = lax.axis_index("east")
        return [((1 - e) * (ce - 1), (1 - e) * (ce - 1) + 2 * e - 1)]
    return [(0, 1), (ce - 1, ce - 2)]


def one_way(k, sign, w, u, f, inv_v, inv_m, bend=None):
    pull = (w + (0.5 * sign) * u) * inv_v
    out = [pull * f[c] for c in range(3)]
    out[k] = out[k] - (0.5 * sign) * f[3] * inv_v
    out.append((f[3] - (0.5 * sign) * f[k]) * (1.0 / 7.0))
    m = w * f[4]
    if bend is not None:
        m = m + 0.25 * bend
    out.append(m * inv_m)
    return out


def inverse(x):
    y = pl.reciprocal(x, approx=True)
    return y * (2.0 - x * y)


def inverses(w):
    six = 6.0 * w
    return inverse(six + 1.0), inverse(six + 2.0)


def dot3(a, b):
    return a[0] * b[0] + a[1] * b[1] + a[2] * b[2]


def plane_shifts(rows, cols):
    r = lax.broadcasted_iota(jnp.int32, (rows, cols), 0)
    z = lax.broadcasted_iota(jnp.int32, (rows, cols), 1)

    def east(x, before=0.0, after=0.0):
        return (
            jnp.where(r < rows - 1, pltpu.roll(x, rows - 1, 0), after),
            jnp.where(r > 0, pltpu.roll(x, 1, 0), before),
        )

    def level(x):
        return (
            jnp.where(z < cols - 1, pltpu.roll(x, cols - 1, 1), 0.0),
            jnp.where(z > 0, pltpu.roll(x, 1, 1), 0.0),
        )

    return east, level


def ends_kernel(ce, cn, n_faces, start, flow, *refs):
    outs, tiles_v, tiles_u, sems = refs[:n_faces], *refs[n_faces:]
    copies = Copies(sems)
    taken = []
    for i, (e, _) in enumerate(facing(ce)):
        pairs = []
        for side, first in enumerate((0, cn - SUB)):
            pairs.append((start.at[:, e, pl.ds(first, SUB)], tiles_v.at[i, side]))
            pairs.append((flow.at[:, e, pl.ds(first, SUB)], tiles_u.at[i, side]))
        taken.append(copies.take(*pairs))
        copies.start(taken[-1])
    for i, out in enumerate(outs):
        copies.wait(taken[i])
        for side, row in enumerate((0, SUB - 1)):
            for f in range(8):
                tile = tiles_v[i, side, f] if f < 5 else tiles_u[i, side, f - 5]
                out[side * 8 + f : side * 8 + f + 1, :] = tile[row : row + 1]


def row_ends(start, flow, n_faces):
    _, ce, cn, cz = start.shape
    return pl.pallas_call(
        functools.partial(ends_kernel, ce, cn, n_faces),
        out_shape=[shape(16, cz)] * n_faces,
        in_specs=[whole(pltpu.HBM)] * 2,
        out_specs=[whole()] * n_faces,
        scratch_shapes=[
            VMEM((n_faces, 2, 5, SUB, cz), F32),
            VMEM((n_faces, 2, 3, SUB, cz), F32),
            pltpu.SemaphoreType.DMA((4 * n_faces,)),
        ],
        compiler_params=params(60),
        cost_estimate=cost(0, 1 << 16),
    )(start, flow)


def pack_kernel(ce, cn, cz, n_faces, endp, endn, start, source, flow, eddy, *refs):
    packs, refs = refs[:2], refs[2:]
    faces, refs = refs[:n_faces], refs[n_faces:]
    tiles_v, tiles_u, tiles_s, tiles_e, sems = refs
    has = [x.astype(F32) for x in neighbours()[:2]]
    copies = Copies(sems)
    sides = ((0, 0, 1, -1.0), (cn - SUB, SUB - 1, SUB - 2, 1.0))
    needed = []
    for side, (first, _, _, _) in enumerate(sides):
        pairs = []
        for h in range(2):
            cut = (pl.ds(first, SUB), pl.ds(h * LANES, LANES))
            pairs += [
                (start.at[(slice(None), slice(None)) + cut], tiles_v.at[side, :, :, h]),
                (flow.at[(slice(None), slice(None)) + cut], tiles_u.at[side, :, :, h]),
                (eddy.at[(slice(None),) + cut], tiles_e.at[side, 0, :, h]),
                (source.at[(slice(None), slice(None)) + cut], tiles_s.at[side, :, :, h]),
            ]
        needed.append(copies.take(*pairs))
        copies.start(needed[-1])
    later = []
    for (near, far), face in zip(facing(ce), faces):
        taken = copies.take(
            (start.at[:, near], face.at[0:5]),
            (flow.at[:, near], face.at[5:8]),
            (eddy.at[near], face.at[8]),
            (source.at[:, near], face.at[9:14]),
            (start.at[:, far], face.at[14:19]),
            (flow.at[:, far], face.at[19:22]),
        )
        copies.start(taken)
        later.append(taken)
    east, level = plane_shifts(ce, cz)

    def line(ref, side, f, row):
        flat = ref.reshape(2, ref.shape[1], ce * 2 * SUB, LANES)
        return jnp.concatenate([flat[side, f, pl.ds(h * SUB + row, ce, stride=2 * SUB), :] for h in range(2)], axis=1)

    for side, (_, row, behind, sign) in enumerate(sides):
        copies.wait(needed[side])
        pack = packs[side]
        v = [line(tiles_v, side, f, row) for f in range(5)]
        u = [line(tiles_u, side, k, row) for k in range(3)]
        eddy_row = line(tiles_e, side, 0, row)
        inner = [line(tiles_v, side, f, behind) for f in range(5)]
        inner_u = [line(tiles_u, side, k, behind) for k in range(3)]
        src = [line(tiles_s, side, f, row) for f in range(5)]
        for f, x in enumerate(v + u + [eddy_row]):
            pack[f * ce : (f + 1) * ce, :] = x
        w = 1.0 + eddy_row
        inv_v, inv_m = inverses(w)
        before = [endp[side * 8 + f : side * 8 + f + 1, :] * has[0] for f in range(8)]
        after = [endn[side * 8 + f : side * 8 + f + 1, :] * has[1] for f in range(8)]
        for f in range(8):
            pack[PACK * ce + f : PACK * ce + f + 1, :] = before[f]
            pack[PACK * ce + 8 + f : PACK * ce + 9 + f, :] = after[f]
        total, slope0, slope2 = [], [], []
        for f in range(5):
            a, b = east(v[f], before[f], after[f])
            h, l = level(v[f])
            total.append((a + b) + (h + l))
            slope0.append(a - b)
            slope2.append(h - l)
        curv = []
        for k in range(3):
            a, b = east(u[k], before[5 + k], after[5 + k])
            h, l = level(u[k])
            curv.append((a + b) + (h + l) + inner_u[k] - 6.0 * u[k])
        out = one_way(1, -sign, w, u[1], inner, inv_v, inv_m, dot3(v, curv))
        press = (slope0[3], None, slope2[3])
        for c in range(3):
            more = src[c] + w * total[c] + 0.5 * (u[0] * slope0[c] + u[2] * slope2[c])
            if press[c] is not None:
                more = more - 0.5 * press[c]
            out[c] = out[c] + more * inv_v
        out[3] = out[3] + (src[3] + total[3] - 0.5 * (slope0[0] + slope2[2])) * (1.0 / 7.0)
        out[4] = out[4] + (src[4] + w * total[4]) * inv_m
        for f in range(5):
            pack[(9 + f) * ce : (10 + f) * ce, :] = out[f]
    for taken in later:
        copies.wait(taken)


def pack(ends, start, source, flow, eddy, n_faces):
    _, ce, cn, cz = start.shape
    out = [shape(PACK * ce + 16, cz)] * 2 + [shape(FACE, cn, cz)] * n_faces
    got = pl.pallas_call(
        functools.partial(pack_kernel, ce, cn, cz, n_faces),
        out_shape=out,
        in_specs=[whole()] * 2 + [whole(pltpu.HBM)] * 4,
        out_specs=[whole()] * len(out),
        scratch_shapes=[
            VMEM((2, 5, ce, 2, SUB, LANES), F32),
            VMEM((2, 3, ce, 2, SUB, LANES), F32),
            VMEM((2, 5, ce, 2, SUB, LANES), F32),
            VMEM((2, 1, ce, 2, SUB, LANES), F32),
            pltpu.SemaphoreType.DMA((16 + 6 * n_faces,)),
        ],
        compiler_params=params(60),
        cost_estimate=cost(1 << 22, 4 << 20),
    )(*ends, start, source, flow, eddy)
    return got[:2], got[2:]


def split(x):
    high = x.astype(BF16)
    return high, (x - high.astype(F32)).astype(BF16)


def owner_of(turbine):
    return lax.shift_right_logical(turbine * 5462, 16)


def columns(x, first, size):
    return jnp.concatenate([x[:, k : k + 1] for k in range(first // LANES, (first + size) // LANES)], axis=0)


def lines(x, first, size):
    return jnp.concatenate([x[k : k + 1, :] for k in range(first // LANES, (first + size) // LANES)], axis=1)


def steps_of(chunks):
    sizes = [0] + [x for x in (2 * LANES,) if x < chunks * LANES] + [chunks * LANES]
    return list(zip(sizes[:-1], sizes[1:]))


def entries(live, cells, turbine, sector, weight, cz):
    cell, tur = cells[...], turbine[...]
    owner = owner_of(tur)
    key = (owner * SECT + sector[...]).astype(F32)
    local = (tur - owner * TURB_DEV).astype(F32)
    slot = lax.broadcasted_iota(jnp.int32, cell.shape, 0) * LANES + lax.broadcasted_iota(jnp.int32, cell.shape, 1)
    load = jnp.where(slot < live, weight[...], 0.0)
    line = lax.shift_right_logical(cell, cz.bit_length() - 1)
    level = jnp.bitwise_and(cell, cz - 1).astype(F32)
    return slot, line, level, key, local, load


def gather_edge(chosen, edge_row, level, key, local, load, put):
    chunks = chosen.shape[0]
    lower = lax.broadcasted_iota(jnp.int32, (LANES, LANES), 0) < lax.broadcasted_iota(jnp.int32, (LANES, LANES), 1)
    rank = jnp.dot(chosen.astype(BF16), jnp.where(lower, 1.0, 0.0).astype(BF16), preferred_element_type=F32)
    sums = jnp.sum(chosen, axis=1, keepdims=True)
    so_far = jnp.zeros((1, 1), F32)
    starts = []
    for k in range(chunks):
        starts.append(so_far)
        so_far = so_far + sums[k : k + 1]
    rank = jnp.where(chosen > 0.0, rank + jnp.concatenate(starts, axis=0), -1.0)
    total = jnp.sum(chosen).astype(jnp.int32)
    load_high = load.astype(BF16).astype(F32)
    load_rest = load - load_high
    load_mid = load_rest.astype(BF16).astype(F32)
    load_low = load_rest - load_mid
    blank = jnp.zeros((1, LANES), F32)
    rows = [
        jnp.concatenate([x[k : k + 1] for x in (edge_row, level, key, local, load_high, load_mid, load_low)] + [blank])
        for k in range(chunks)
    ]
    to = lax.broadcasted_iota(jnp.int32, (LANES, LANES), 0).astype(F32)
    listed = jnp.concatenate(rows, axis=1).astype(BF16)

    @pl.loop(0, lax.div(total + (LANES - 1), LANES))
    def _(q):
        first = lax.convert_element_type(q * LANES, F32)
        where = jnp.concatenate(
            [jnp.where(rank[k : k + 1] - first == to, 1.0, 0.0) for k in range(chunks)], axis=1
        ).astype(BF16)
        put(q, lax.dot_general(listed, where, (((1,), (1,)), ((), ())), preferred_element_type=F32))

    return total


def rotor_terms(row, level, turbine, weight, key, table, blocks, acc):
    size = row.shape[0]
    rows, width = table.shape[0] // 2, table.shape[1]
    cz = width // COMPS
    lane_row = lax.broadcasted_iota(jnp.int32, (size, rows), 1).astype(F32)
    pick = jnp.where(row == lane_row, 1.0, 0.0).astype(BF16)
    got = jnp.dot(jnp.concatenate([pick, pick], axis=1), table[...], preferred_element_type=F32)
    here = level == lax.broadcasted_iota(jnp.int32, (size, cz), 1).astype(F32)
    lane = lax.broadcasted_iota(jnp.int32, (size, LANES), 1)
    lane_comp = owner_of(lane)
    lane_tur = (lane - lane_comp * TURB_DEV).astype(F32)
    spread = jnp.zeros((size, LANES), F32)
    for c in range(COMPS):
        part = jnp.where(here, got[:, c * cz : (c + 1) * cz], 0.0)
        spread = jnp.where(lane_comp == c, jnp.sum(part, axis=1, keepdims=True), spread)
    spread = jnp.where(turbine == lane_tur, spread * weight, 0.0)
    lane_key = lax.broadcasted_iota(jnp.int32, (blocks * SECT, size), 0).astype(F32)
    to = jnp.where(lane_key == key, 1.0, 0.0).astype(BF16)
    high = spread.astype(BF16)
    rest = spread - high.astype(F32)
    mid, low = split(rest)
    parts = jnp.dot(to, jnp.concatenate([high, mid, low], axis=1), preferred_element_type=F32)
    acc[...] += parts[:, :LANES] + parts[:, LANES : 2 * LANES] + parts[:, 2 * LANES :]


def halves(ref, f, i, rows, move=0):
    first, size = rows
    return [ref[f, i, h, pl.ds(PAD + first + move, size), :] for h in range(2)]


def level_shifts(x, first, last):
    up = [pltpu.roll(x[h], LANES - 1, 1) for h in range(2)]
    down = [pltpu.roll(x[h], 1, 1) for h in range(2)]
    return (
        [jnp.where(last, up[1], up[0]), jnp.where(last, 0.0, up[1])],
        [jnp.where(first, 0.0, down[0]), jnp.where(first, down[0], down[1])],
    )


def slab_sweep(ref, i, rows, first, last, src, flow, visc, curv):
    two = range(2)
    w = visc
    inv = [inverses(w[h]) for h in two]
    w2 = [2.0 * w[h] for h in two]

    def sides(f):
        mid = halves(ref, f, i, rows)
        a, b = halves(ref, f, i + 1, rows), halves(ref, f, i - 1, rows)
        n, s = halves(ref, f, i, rows, 1), halves(ref, f, i, rows, -1)
        up, down = level_shifts(mid, first, last)
        return mid, a, b, n, s, up, down

    _, a, b, n, s, up, down = sides(3)
    grad = [[x[h] - y[h] for h in two] for x, y in ((a, b), (n, s), (up, down))]
    q_sum = [(a[h] + b[h]) + (n[h] + s[h]) + (up[h] + down[h]) for h in two]
    out, div, bend = [], [0.0, 0.0], [0.0, 0.0]
    for c in range(3):
        mid, a, b, n, s, up, down = sides(c)
        res = []
        for h in two:
            total = (a[h] + b[h]) + (n[h] + s[h]) + (up[h] + down[h])
            slope = [a[h] - b[h], n[h] - s[h], up[h] - down[h]]
            carried = flow[0][h] * slope[0] + flow[1][h] * slope[1] + flow[2][h] * slope[2]
            res.append((src(c)[h] + 0.5 * (w2[h] * total + (carried - grad[c][h]))) * inv[h][0])
            div[h] = div[h] + slope[c]
            bend[h] = bend[h] + mid[h] * curv[c][h]
        out.append(res)
    out.append([(src(3)[h] + q_sum[h] - 0.5 * div[h]) * (1.0 / 7.0) for h in two])
    _, a, b, n, s, up, down = sides(4)
    res = []
    for h in two:
        total = (a[h] + b[h]) + (n[h] + s[h]) + (up[h] + down[h])
        res.append((src(4)[h] + w[h] * total + 0.25 * bend[h]) * inv[h][1])
    out.append(res)
    return out


def sweeps_kernel(
    ce, cn, cz, blocks, pair,
    count, start, source, flow, eddy, facep, facen, cells, turbine, sector, weight,
    final, edge_low, edge_high, grad, *refs,
):
    if not pair:
        coef_low, coef_high, items, n_items = refs[:4]
    held, v0, u, src, ed, v1, curv, table, sems = refs[-9:]
    copies = Copies(sems)
    two = range(2)
    has = [x > 0 for x in neighbours()[:2]]
    inner = pl.ds(PAD, cn)

    def part(h):
        return pl.ds(h * LANES, LANES)

    def halo(face, near, far, slab):
        pairs = []
        for h in two:
            pairs += [
                (face.at[0:5, :, part(h)], v0.at[:, near, h, inner]),
                (face.at[5:8, :, part(h)], u.at[:, near, h, inner]),
                (face.at[8, :, part(h)], ed.at[0, slab, h]),
                (face.at[9:14, :, part(h)], src.at[:, slab, h]),
                (face.at[14:19, :, part(h)], v0.at[:, far, h, inner]),
                (face.at[19:22, :, part(h)], u.at[:, far, h, inner]),
            ]
        return pairs

    ends = ((facep, 1, 0, 0), (facen, ce + 2, ce + 3, ce + 1))
    halos = [copies.take(*halo(*x)) for x in ends]

    def group(g, size):
        span, own, own2 = pl.ds(g, size), pl.ds(g + 1, size), pl.ds(g + 2, size)
        pairs = []
        for h in two:
            pairs += [
                (start.at[:, span, :, part(h)], v0.at[:, own2, h, inner]),
                (flow.at[:, span, :, part(h)], u.at[:, own2, h, inner]),
                (eddy.at[span, :, part(h)], ed.at[0, own, h]),
                (source.at[:, span, :, part(h)], src.at[:, own, h]),
            ]
        return pairs

    groups = [copies.take(*group(g, STEP)) for g in range(0, ce, STEP)]
    per = len(groups[0][1])
    copies.start(groups[0])
    for exists, taken in zip(has, halos):

        @pl.when(exists)
        def _():
            copies.start(taken)

    for taken in groups[1:]:
        copies.start(taken)

    blank = jnp.zeros((PAD, LANES), F32)
    for ref, fields in ((v0, 5), (u, 3), (v1, 5)):

        @pl.loop(0, ref.shape[1])
        def _(i):
            for f in range(fields):
                for h in two:
                    ref[f, i, h, 0:PAD, :] = blank
                    ref[f, i, h, PAD + cn : PAD + cn + PAD, :] = blank

    for exists, (_, near, _, end) in zip(has, ends):

        @pl.when(jnp.logical_not(exists))
        def _():
            for ref, fields, slab in ((v0, 5, near), (u, 3, near), (v1, 5, end)):
                for f in range(fields):
                    for h in two:
                        ref[f, slab, h, inner, :] = jnp.zeros((cn, LANES), F32)

    def ends_of(size):
        lane = lax.broadcasted_iota(jnp.int32, (size, LANES), 1)
        return lane == 0, lane == LANES - 1

    live = count[0, 0]
    slot, line, level, key, local, load = entries(live, cells, turbine, sector, weight, cz)
    chunks = slot.shape[0]
    if not pair:
        north = jnp.bitwise_and(line, cn - 1)
        east = lax.shift_right_logical(line, cn.bit_length() - 1)
        place = jnp.where(north == 0, 0, jnp.where(north == 1, 1, jnp.where(north == cn - 1, 2, 3)))
        is_edge = jnp.logical_or(north <= 1, north >= cn - 2)
        chosen = jnp.where(jnp.logical_and(is_edge, slot < live), 1.0, 0.0)
        edge_row = (place * ce + east).astype(F32)
        items[...] = jnp.zeros_like(items)

        def put(q, x):
            items[q] = x

        n_items[0] = gather_edge(chosen, edge_row, level, key, local, load, put)

    @pl.when(has[0])
    def _():
        copies.wait(halos[0])

    low_slab, high_slab = jnp.where(has[0], 0, 1), jnp.where(has[1], ce + 2, ce + 1)
    steps = ce // STEP

    @pl.loop(0, steps)
    def _(g):
        copies.wait((groups[0][0] + g * per, group(g * STEP, STEP)))

        @pl.when(jnp.logical_and(g == steps - 1, has[1]))
        def _():
            copies.wait(halos[1])

        @pl.loop(jnp.where(g == 0, low_slab, g * STEP), jnp.where(g == steps - 1, high_slab, (g + 1) * STEP))
        def _(i):
            mid = i + 1
            first, last = ends_of(ROWS_1)
            for r in range(0, cn, ROWS_1):
                rows, at = (r, ROWS_1), pl.ds(r, ROWS_1)
                flows = [halves(u, k, mid, rows) for k in range(3)]
                bends = []
                for k in range(3):
                    a, b = halves(u, k, mid + 1, rows), halves(u, k, mid - 1, rows)
                    n, s = halves(u, k, mid, rows, 1), halves(u, k, mid, rows, -1)
                    up, down = level_shifts(flows[k], first, last)
                    res = [(a[h] + b[h]) + (n[h] + s[h]) + (up[h] + down[h]) - 6.0 * flows[k][h] for h in two]
                    for h in two:
                        curv[k, i, h, at, :] = res[h]
                    bends.append(res)
                out = slab_sweep(
                    v0, mid, rows, first, last,
                    lambda f: [src[f, i, h, at, :] for h in two],
                    flows, [1.0 + ed[0, i, h, at, :] for h in two], bends,
                )
                for f in range(5):
                    for h in two:
                        v1[f, i, h, pl.ds(PAD + r, ROWS_1), :] = out[f][h]

    def leave(e):
        return [(held.at[:, pl.ds(e, OUT_STEP)], final.at[:, pl.ds(e, OUT_STEP)])]

    outs = [copies.take(*leave(e)) for e in range(0, ce, OUT_STEP)]

    @pl.loop(0, ce // OUT_STEP)
    def _(g):
        @pl.loop(0, OUT_STEP)
        def _(k):
            e = g * OUT_STEP + k
            i = e + 1
            first, last = ends_of(ROWS_2)

            for r in range(0, cn, ROWS_2):
                rows, span = (r, ROWS_2), pl.ds(r, ROWS_2)
                flows = [halves(u, k, i + 1, rows) for k in range(3)]
                bends = [[curv[k, i, h, span, :] for h in two] for k in range(3)]
                out = slab_sweep(
                    v1, i, rows, first, last,
                    lambda f: [src[f, i, h, span, :] for h in two],
                    flows, [1.0 + ed[0, i, h, span, :] for h in two], bends,
                )
                at = pl.ds(pl.multiple_of(e * cn + r, ROWS_2), ROWS_2)
                below = pl.ds(pl.multiple_of((ce + e) * cn + r, ROWS_2), ROWS_2)
                for h in two:
                    force = flows[0][h] * jnp.abs(flows[0][h])
                    for f in range(5):
                        held[f, e, span, part(h)] = out[f][h]
                    for c in range(COMPS):
                        hi, lo = split(out[c if c < 3 else 4][h] * force)
                        wide = pl.ds(c * cz + h * LANES, LANES)
                        table[at, wide] = hi
                        table[below, wide] = lo

        copies.start((outs[0][0] + g, leave(g * OUT_STEP)))

    def edge_plane(ref, k, first, tall, row):
        fields, slabs = ref.shape[:2]
        flat = ref.reshape(fields, slabs * 2 * tall, LANES)
        return jnp.concatenate(
            [flat[k, pl.ds((first * 2 + h) * tall + row, ce, stride=2 * tall), :] for h in two], axis=1
        )

    tall = PAD + cn + PAD
    edge_rows = () if pair else ((coef_low, 0, 1), (coef_high, cn - 1, cn - 2))
    for coef, row, behind in edge_rows:
        planes = [edge_plane(curv, k, 1, cn, row) for k in range(3)]
        planes += [edge_plane(u, 1, 2, tall, PAD + behind), edge_plane(ed, 0, 1, cn, behind), edge_plane(u, 0, 2, tall, PAD + behind)]
        planes += [edge_plane(v1, k, 1, tall, PAD + row) for k in range(3)]
        for k, x in enumerate(planes):
            coef[k * ce : (k + 1) * ce, :] = x

    tiles = copies.take((held.at[:, :, 0:SUB, :], edge_low), (held.at[:, :, cn - SUB : cn, :], edge_high))
    copies.start(tiles)

    row_t, level_t, local_t, load_t = line.astype(F32).T, level.T, local.T, load.T
    grad[...] = jnp.zeros_like(grad)
    for least, size in steps_of(chunks):

        @pl.when(jnp.logical_and(live > least, live <= size))
        def _():
            cols = [columns(x, 0, size) for x in (row_t, level_t, local_t, load_t)]
            rotor_terms(*cols, lines(key, 0, size), table, blocks, grad)

    for taken in outs + [tiles]:
        copies.wait(taken)


def sweeps(count, start, source, flow, eddy, faces, lists, blocks, pair):
    _, ce, cn, cz = start.shape
    chunks = lists[0].shape[0]
    tall = PAD + cn + PAD
    more = [shape(EDGE * ce, cz)] * 2 + [shape(chunks, ITEM, LANES), jax.ShapeDtypeStruct((1,), jnp.int32)]
    return pl.pallas_call(
        functools.partial(sweeps_kernel, ce, cn, cz, blocks, pair),
        out_shape=[shape(*start.shape)] + [shape(5, ce, SUB, cz)] * 2 + [shape(blocks * SECT, LANES)] + ([] if pair else more),
        in_specs=[whole(pltpu.SMEM)] + [whole(pltpu.HBM)] * 6 + [whole()] * 4,
        out_specs=[whole(pltpu.HBM), whole(), whole(), whole()] + ([] if pair else [whole()] * 3 + [whole(pltpu.SMEM)]),
        scratch_shapes=[
            VMEM(start.shape, F32),
            VMEM((5, ce + 4, 2, tall, LANES), F32),
            VMEM((3, ce + 4, 2, tall, LANES), F32),
            VMEM((5, ce + 2, 2, cn, LANES), F32),
            VMEM((1, ce + 2, 2, cn, LANES), F32),
            VMEM((5, ce + 2, 2, tall, LANES), F32),
            VMEM((3, ce + 2, 2, cn, LANES), F32),
            VMEM((2 * ce * cn, COMPS * cz), BF16),
            pltpu.SemaphoreType.DMA((26 + 8 * (ce // STEP) + ce // OUT_STEP,)),
        ],
        compiler_params=params(48),
        cost_estimate=cost(0, 1 << 10),
    )(count, *in_hbm(start, source, flow, eddy), *faces, *lists)


def edge_kernel(
    ce, cn, cz, blocks, copies_out,
    n_items, facep, facen, own_low, own_high, coef_low, coef_high, got_prev, got_next,
    edge_low, edge_high, items, grad, final_in,
    final, chunks,
    low_out, high_out, table, acc, sems,
):
    east, level = plane_shifts(ce, cz)
    sub = lax.broadcasted_iota(jnp.int32, (SUB, cz), 0)
    has = [x.astype(F32) for x in neighbours()]
    sides = (
        (-1.0, 0, own_low, coef_low, got_prev, edge_low, low_out, 0),
        (1.0, cn - 1, own_high, coef_high, got_next, edge_high, high_out, cn - SUB),
    )
    waits = []
    for side, (sign, row, own, coef, got, edge, out_ref, place) in enumerate(sides):

        def plane(ref, f):
            return ref[f * ce : (f + 1) * ce, :]

        v0 = [plane(own, f) for f in range(5)]
        u = [plane(own, 5 + k) for k in range(3)]
        w = 1.0 + plane(own, 8)
        xv = [plane(got, f) for f in range(5)]
        xu = [plane(got, 5 + k) for k in range(3)]
        xw = 1.0 + plane(got, 8)
        xp = [plane(got, 9 + f) for f in range(5)]
        curv = [plane(coef, k) for k in range(3)]
        inv_v, inv_m = inverses(w)
        delta = one_way(1, sign, w, u[1], xv, inv_v, inv_m, dot3(v0, xu))
        back = one_way(1, -sign, xw, xu[1], v0, *inverses(xw), dot3(xv, u))
        x1 = [xp[f] + back[f] for f in range(5)]
        ends = []
        for far, face in enumerate((facep, facen)):
            hv = [got[PACK * ce + 8 * far + f : PACK * ce + 8 * far + f + 1, :] for f in range(8)]
            fv = [face[f, row : row + 1, :] * has[far] for f in range(5)]
            fu = face[6, row : row + 1, :] * has[far]
            fw = 1.0 + face[8, row : row + 1, :] * has[far]
            ends.append(one_way(1, sign, fw, fu, hv, *inverses(fw), dot3(fv, hv[5:])))
        x1 = [x * has[2 + side] for x in x1]
        total, slope0, slope2 = [], [], []
        for f in range(5):
            a, b = east(delta[f], ends[0][f], ends[1][f])
            h, l = level(delta[f])
            total.append((a + b) + (h + l))
            slope0.append(a - b)
            slope2.append(h - l)
        full = [plane(coef, 6 + c) + delta[c] for c in range(3)]
        add = one_way(1, sign, w, u[1], x1, inv_v, inv_m, dot3(full, xu) + dot3(delta, curv))
        press = (slope0[3], None, slope2[3])
        for c in range(3):
            more = w * total[c] + 0.5 * (u[0] * slope0[c] + u[2] * slope2[c])
            if press[c] is not None:
                more = more - 0.5 * press[c]
            add[c] = add[c] + more * inv_v
        add[3] = add[3] + (total[3] - 0.5 * (slope0[0] + slope2[2])) * (1.0 / 7.0)
        add[4] = add[4] + w * total[4] * inv_m
        ru1, rw, ru0 = plane(coef, 3), 1.0 + plane(coef, 4), plane(coef, 5)
        behind = one_way(1, sign, rw, ru1, delta, *inverses(rw))
        near, far = (0, 1) if side == 0 else (SUB - 1, SUB - 2)
        for f in range(5):
            for e in range(ce):
                rows = jnp.where(
                    sub == near, add[f][e : e + 1, :], jnp.where(sub == far, behind[f][e : e + 1, :], 0.0)
                )
                out_ref[f, e] = edge[f, e] + rows
        copy = pltpu.make_async_copy(out_ref, final.at[:, :, pl.ds(place, SUB), :], sems.at[side])
        copy.start()
        waits.append(copy)
        for behind_row, u0, values in ((0, u[0], add), (1, ru0, behind)):
            force = u0 * jnp.abs(u0)
            at = (2 * side + behind_row) * ce
            for c in range(COMPS):
                hi, lo = split(values[c if c < 3 else 4] * force)
                table[at : at + ce, c * cz : (c + 1) * cz] = hi
                table[4 * ce + at : 5 * ce + at, c * cz : (c + 1) * cz] = lo

    acc[...] = grad[...]
    live = n_items[0]
    for least, size in steps_of(items.shape[0]):

        @pl.when(jnp.logical_and(live > least, live <= size))
        def _():
            lists = [items[k] for k in range(size // LANES)]
            turned = [x.T for x in lists]

            def col(j):
                return jnp.concatenate([x[:, j : j + 1] for x in turned], axis=0)

            key = jnp.concatenate([x[2:3] for x in lists], axis=1)
            rotor_terms(col(0), col(1), col(3), col(4) + col(5) + col(6), key, table, blocks, acc)

    for copy in range(copies_out):
        chunks[copy] = acc[...]
    for copy in waits:
        copy.wait()


def edges(n_items, faces, packs, coefs, gots, tiles, items, grad, final, blocks, size):
    _, ce, cn, cz = final.shape
    args = (n_items, *faces, *packs, *coefs, *gots, *tiles, items, grad, final)
    tile = VMEM((5, ce, SUB, cz), F32)
    return pl.pallas_call(
        functools.partial(edge_kernel, ce, cn, cz, blocks, size),
        out_shape=(shape(*final.shape), shape(size, blocks * SECT, LANES)),
        in_specs=[whole(pltpu.SMEM)] + [whole()] * (len(args) - 2) + [whole(pltpu.HBM)],
        out_specs=(whole(pltpu.HBM), whole()),
        scratch_shapes=[
            tile,
            tile,
            VMEM((8 * ce, COMPS * cz), BF16),
            VMEM((blocks * SECT, LANES), F32),
            pltpu.SemaphoreType.DMA((2,)),
        ],
        input_output_aliases={len(args) - 1: 0},
        compiler_params=params(32),
        cost_estimate=cost(1 << 24, 4 << 20),
    )(*args)


def side(own):
    e = lax.axis_index("east")
    return 1 - e if own else e


def raw_kernel(ce, cn, cz, own, *refs):
    if own:
        count, refs = refs[0], refs[1:]
    start, source, flow, eddy, refs = *refs[:4], refs[4:]
    if own:
        lists, (rows, face, items), refs = refs[:4], refs[4:7], refs[7:]
        cells, turbine, sector, weight, sems = refs[4:]
    else:
        rows, sems = refs[0], refs[-1]
        refs = refs[1:]
    tiles_v, tiles_u, tiles_s, tiles_e = refs[:4]
    copies = Copies(sems)
    high = side(own)
    if own:
        held = copies.take(*zip(lists, (cells, turbine, sector, weight)))
        copies.start(held)
    def two_rows(at, to):
        pairs = []
        for h in range(2):
            cut, place = (pl.ds(at, 2), pl.ds(h * LANES, LANES)), pl.ds(to, 2)
            pairs += [
                (start.at[(slice(None), slice(None)) + cut], tiles_v.at[:, :, h, place]),
                (flow.at[(slice(None), slice(None)) + cut], tiles_u.at[:, :, h, place]),
                (eddy.at[(slice(None),) + cut], tiles_e.at[0, :, h, place]),
                (source.at[(slice(None), slice(None)) + cut], tiles_s.at[:, :, h, place]),
            ]
        return pairs

    sides = [copies.take(*two_rows(0, 0)), copies.take(*two_rows(cn - 2, SUB - 2))]

    def both_ways(act):
        for k, taken in enumerate(sides):

            @pl.when(high == k)
            def _():
                act(taken)

    both_ways(copies.start)
    if own:
        ((near, far),) = facing(ce)
        later = copies.take(
            (start.at[:, near], face.at[0:5]),
            (flow.at[:, near], face.at[5:8]),
            (eddy.at[near], face.at[8]),
            (source.at[:, near], face.at[9:14]),
            (start.at[:, far], face.at[14:19]),
            (flow.at[:, far], face.at[19:22]),
        )
        copies.start(later)
        copies.wait(held)
        live = count[0, 0]
        listed = entries(live, cells, turbine, sector, weight, cz)
        edge_items(ce, cn, cz, live, listed, high, items)
        edge_items(ce, cn, cz, live, listed, 1 - high, face.at[FACE:].reshape(-1, cz))

    def plane(ref, f, low, top):
        flat = ref.reshape(ref.shape[0], ce * 2 * SUB, LANES)
        parts = []
        for h in range(2):
            x, y = (flat[f, pl.ds(h * SUB + at, ce, stride=2 * SUB), :] for at in (low, top))
            parts.append(jnp.where(high > 0, y, x))
        return jnp.concatenate(parts, axis=1)

    both_ways(copies.wait)
    planes = [(tiles_v, f, 0) for f in range(5)] + [(tiles_u, k, 0) for k in range(3)] + [(tiles_e, 0, 0)]
    planes += [(tiles_s, f, 0) for f in range(5)]
    planes += [(tiles_v, f, 1) for f in range(5)] + [(tiles_u, k, 1) for k in range(3)] + [(tiles_e, 0, 1)]
    for k, (ref, f, at) in enumerate(planes):
        rows[k * ce : (k + 1) * ce, :] = plane(ref, f, at, SUB - 1 - at)
    if own:
        copies.wait(later)


def edge_items(ce, cn, cz, live, listed, high, out):
    slot, line, level, key, local, load = listed
    north = jnp.bitwise_and(line, cn - 1)
    column = lax.shift_right_logical(line, cn.bit_length() - 1) + lax.axis_index("east") * ce
    edge = high * (cn - 1)
    behind = edge + 1 - 2 * high
    chosen = jnp.where(jnp.logical_and(jnp.logical_or(north == edge, north == behind), slot < live), 1.0, 0.0)
    edge_row = (jnp.where(north == behind, 2 * ce, 0) + column).astype(F32)
    out[...] = jnp.zeros(out.shape, F32)

    def put(q, x):
        out[pl.ds(pl.multiple_of(q * ITEM, ITEM), ITEM), :LANES] = x

    total = gather_edge(chosen, edge_row, level, key, local, load, put)
    out[out.shape[0] - ITEM :, :] = jnp.full((ITEM, cz), total.astype(F32))


def raw_rows(own, start, source, flow, eddy, count=None, lists=()):
    _, ce, cn, cz = start.shape
    out = [shape(RAW * ce, cz)]
    scratch = [
        VMEM((5, ce, 2, SUB, LANES), F32),
        VMEM((3, ce, 2, SUB, LANES), F32),
        VMEM((5, ce, 2, SUB, LANES), F32),
        VMEM((1, ce, 2, SUB, LANES), F32),
    ]
    if own:
        chunks = lists[0].shape[0]
        most = (chunks + 1) * ITEM
        planes = pl.cdiv(most, cn)
        out += [shape(FACE + planes, cn, cz), shape(planes * cn, cz)]
        scratch += [VMEM((chunks, LANES), x.dtype) for x in lists]
    return pl.pallas_call(
        functools.partial(raw_kernel, ce, cn, cz, own),
        out_shape=out,
        in_specs=([whole(pltpu.SMEM)] if own else []) + [whole(pltpu.HBM)] * (4 + len(lists)),
        out_specs=[whole()] * len(out),
        scratch_shapes=scratch + [pltpu.SemaphoreType.DMA((26,))],
        compiler_params=params(16),
        cost_estimate=cost(0, 1 << 10),
    )(*([count] if own else []), *in_hbm(start, source, flow, eddy, *lists))


def joined(ce, own, other, k):
    west = lax.axis_index("east") == 0
    a, b = own[k * ce : (k + 1) * ce, :], other[k * ce : (k + 1) * ce, :]
    return jnp.concatenate([jnp.where(west, a, b), jnp.where(west, b, a)], axis=0)


def join_kernel(ce, cz, own, other, pack, coef):
    sign = (2 * side(True) - 1).astype(F32)
    east, level = plane_shifts(2 * ce, cz)
    raw = [joined(ce, own, other, k) for k in range(RAW)]
    v, u, src, inner, inner_u = raw[:5], raw[5:8], raw[9:14], raw[14:19], raw[19:22]
    w = 1.0 + raw[8]
    inv_v, inv_m = inverses(w)
    total, slope0, slope2 = [], [], []
    for f in range(5):
        a, b = east(v[f])
        h, l = level(v[f])
        total.append((a + b) + (h + l))
        slope0.append(a - b)
        slope2.append(h - l)
    curv = []
    for k in range(3):
        a, b = east(u[k])
        h, l = level(u[k])
        curv.append((a + b) + (h + l) + inner_u[k] - 6.0 * u[k])
    out = one_way(1, -sign, w, u[1], inner, inv_v, inv_m, dot3(v, curv))
    press = (slope0[3], None, slope2[3])
    for c in range(3):
        more = src[c] + w * total[c] + 0.5 * (u[0] * slope0[c] + u[2] * slope2[c])
        if press[c] is not None:
            more = more - 0.5 * press[c]
        out[c] = out[c] + more * inv_v
    out[3] = out[3] + (src[3] + total[3] - 0.5 * (slope0[0] + slope2[2])) * (1.0 / 7.0)
    out[4] = out[4] + (src[4] + w * total[4]) * inv_m
    for k, x in enumerate(raw[:9] + out):
        pack[2 * k * ce : 2 * (k + 1) * ce, :] = x
    for k, x in enumerate(curv + [inner_u[1], raw[22], inner_u[0]]):
        coef[2 * k * ce : 2 * (k + 1) * ce, :] = x


def join_rows(own, other, ce):
    cz = own.shape[1]
    return pl.pallas_call(
        functools.partial(join_kernel, ce, cz),
        out_shape=[shape(PACK * 2 * ce, cz), shape(6 * 2 * ce, cz)],
        in_specs=[whole()] * 2,
        out_specs=[whole()] * 2,
        compiler_params=params(16),
        cost_estimate=cost(0, 1 << 10),
    )(own, other)


def both_kernel(
    ce, cn, cz, blocks, copies_out, n_chunks,
    own, other, pack, coef, got, grad,
    chunks, mine, fix,
    table, acc,
):
    other = other.at[FACE:].reshape(-1, cz)
    wide = 2 * ce
    high = side(True)
    sign = (2 * high - 1).astype(F32)
    north = lax.axis_index("north")
    exists = jnp.where(high > 0, north < lax.axis_size("north") - 1, north > 0).astype(F32)
    east, level = plane_shifts(wide, cz)

    def plane(ref, f):
        return ref[f * wide : (f + 1) * wide, :]

    v0 = [plane(pack, f) for f in range(5)]
    u = [plane(pack, 5 + k) for k in range(3)]
    w = 1.0 + plane(pack, 8)
    xv = [plane(got, f) for f in range(5)]
    xu = [plane(got, 5 + k) for k in range(3)]
    xw = 1.0 + plane(got, 8)
    curv = [plane(coef, k) for k in range(3)]
    inv_v, inv_m = inverses(w)
    delta = one_way(1, sign, w, u[1], xv, inv_v, inv_m, dot3(v0, xu))
    back = one_way(1, -sign, xw, xu[1], v0, *inverses(xw), dot3(xv, u))
    x1 = [(plane(got, 9 + f) + back[f]) * exists for f in range(5)]
    total, slope0, slope2 = [], [], []
    for f in range(5):
        a, b = east(delta[f])
        h, l = level(delta[f])
        total.append((a + b) + (h + l))
        slope0.append(a - b)
        slope2.append(h - l)
    full = [plane(pack, 9 + c) + delta[c] for c in range(3)]
    add = one_way(1, sign, w, u[1], x1, inv_v, inv_m, dot3(full, xu) + dot3(delta, curv))
    press = (slope0[3], None, slope2[3])
    for c in range(3):
        more = w * total[c] + 0.5 * (u[0] * slope0[c] + u[2] * slope2[c])
        if press[c] is not None:
            more = more - 0.5 * press[c]
        add[c] = add[c] + more * inv_v
    add[3] = add[3] + (total[3] - 0.5 * (slope0[0] + slope2[2])) * (1.0 / 7.0)
    add[4] = add[4] + w * total[4] * inv_m
    ru1, rw, ru0 = plane(coef, 3), 1.0 + plane(coef, 4), plane(coef, 5)
    behind = one_way(1, sign, rw, ru1, delta, *inverses(rw))
    west = lax.axis_index("east") == 0
    for k, x in enumerate(add + behind):
        mine[k * ce : (k + 1) * ce, :] = jnp.where(west, x[:ce], x[ce:])
        fix[k * ce : (k + 1) * ce, :] = jnp.where(west, x[ce:], x[:ce])
    for row, u0, values in ((0, u[0], add), (1, ru0, behind)):
        force = u0 * jnp.abs(u0)
        for c in range(COMPS):
            hi, lo = split(values[c if c < 3 else 4] * force)
            table[row * wide : (row + 1) * wide, c * cz : (c + 1) * cz] = hi
            table[(2 + row) * wide : (3 + row) * wide, c * cz : (c + 1) * cz] = lo

    acc[...] = grad[...]
    most = n_chunks

    def chunk(ref, q):
        return ref[q * ITEM : (q + 1) * ITEM, :LANES]

    def terms(lists):
        turned = [x.T for x in lists]

        def col(j):
            return jnp.concatenate([x[:, j : j + 1] for x in turned], axis=0)

        key = jnp.concatenate([x[2:3] for x in lists], axis=1)
        rotor_terms(col(0), col(1), col(3), col(4) + col(5) + col(6), key, table, blocks, acc)

    terms([chunk(own, 0), chunk(other, 0)])
    longest = jnp.max(jnp.maximum(own[own.shape[0] - ITEM :, :LANES], other[other.shape[0] - ITEM :, :LANES]))

    @pl.when(longest > float(LANES))
    def _():
        terms([chunk(ref, q) for ref in (own, other) for q in range(1, most)])

    for k in range(copies_out):
        chunks[k] = acc[...]


def both_edges(own, other, pack, coef, got, grad, size, blocks, copies_out, n_chunks):
    _, ce, cn, cz = size
    return pl.pallas_call(
        functools.partial(both_kernel, ce, cn, cz, blocks, copies_out, n_chunks),
        out_shape=(shape(copies_out, blocks * SECT, LANES), shape(10 * ce, cz), shape(10 * ce, cz)),
        in_specs=[whole()] * 6,
        out_specs=(whole(), whole(), whole()),
        scratch_shapes=[
            VMEM((8 * ce, COMPS * cz), BF16),
            VMEM((blocks * SECT, LANES), F32),
        ],
        compiler_params=params(32),
        cost_estimate=cost(0, 1 << 10),
    )(own, other, pack, coef, got, grad)


def home_kernel(ce, cn, mine, fix, edge_low, edge_high, final_in, final, low_out, high_out, sems):
    cz = edge_low.shape[3]
    sub = lax.broadcasted_iota(jnp.int32, (SUB, cz), 0)
    high = side(True) > 0
    waits = []
    for k, (edge, out, near, far, place) in enumerate(
        ((edge_low, low_out, 0, 1, 0), (edge_high, high_out, SUB - 1, SUB - 2, cn - SUB))
    ):
        from_mine = high if k else jnp.logical_not(high)
        for f in range(5):

            def plane(at):
                span = pl.ds(at * ce, ce)
                return jnp.where(from_mine, mine[span, :], fix[span, :])

            a, b = plane(f), plane(5 + f)
            for e in range(ce):
                rows = jnp.where(sub == near, a[e : e + 1, :], jnp.where(sub == far, b[e : e + 1, :], 0.0))
                out[f, e] = edge[f, e] + rows
        copy = pltpu.make_async_copy(out, final.at[:, :, pl.ds(place, SUB), :], sems.at[k])
        copy.start()
        waits.append(copy)
    for copy in waits:
        copy.wait()


def rows_home(mine, fix, tiles, final):
    _, ce, cn, cz = final.shape
    return pl.pallas_call(
        functools.partial(home_kernel, ce, cn),
        out_shape=shape(*final.shape),
        in_specs=[whole()] * 4 + [whole(pltpu.HBM)],
        out_specs=whole(pltpu.HBM),
        scratch_shapes=[
            VMEM((5, ce, SUB, cz), F32),
            VMEM((5, ce, SUB, cz), F32),
            pltpu.SemaphoreType.DMA((2,)),
        ],
        input_output_aliases={4: 0},
        compiler_params=params(16),
        cost_estimate=cost(0, 1 << 10),
    )(mine, fix, *tiles, final)


def sum_kernel(parts, out):
    total = jnp.sum(parts[...], axis=0)
    for c in range(COMPS):
        out[c] = total[:, c * TURB_DEV : (c + 1) * TURB_DEV]


def sum_parts(parts):
    return pl.pallas_call(
        sum_kernel,
        out_shape=shape(COMPS, SECT, TURB_DEV),
        in_specs=[whole()],
        out_specs=whole(),
        compiler_params=params(4),
        cost_estimate=cost(parts.size, parts.size * 4),
    )(parts)


def beside(x, size):
    if size == 2:
        got = lax.ppermute(x[0], "east", [(0, 1), (1, 0)])
        return got, got
    up = [(i, i + 1) for i in range(size - 1)]
    down = [(i + 1, i) for i in range(size - 1)]
    return lax.ppermute(x[1], "east", up), lax.ppermute(x[0], "east", down)


def north_ways(x, size):
    up = [(i, i + 1) for i in range(size - 1)]
    down = [(i + 1, i) for i in range(size - 1)]
    return lax.ppermute(x[1], "north", up), lax.ppermute(x[0], "north", down)


def shards(
    adjoint_start,
    adjoint_source,
    base_flow,
    eddy_visc,
    rotor_count,
    rotor_cell,
    rotor_turbine,
    rotor_sector,
    rotor_weight,
):
    _, ce, cn, cz = adjoint_start.shape
    n_east, n_north = lax.axis_size("east"), lax.axis_size("north")
    count = rotor_count
    slots = rotor_cell.shape[-1]
    lists = [x.reshape(slots // LANES, LANES) for x in (rotor_cell, rotor_turbine, rotor_sector, rotor_weight)]

    fields = adjoint_start, adjoint_source, base_flow, eddy_visc
    if n_east == 2:
        return pair_shards(count, fields, lists, n_north)
    n_faces = 2
    ends = beside(row_ends(adjoint_start, base_flow, n_faces), n_east)
    packs, own = pack(ends, *fields, n_faces)
    gots = north_ways(packs, n_north)
    faces = beside(own, n_east)
    final, *tiles, grad, coef_low, coef_high, items, n_items = sweeps(count, *fields, faces, lists, n_north, False)
    final, chunks = edges(
        n_items, faces, packs, (coef_low, coef_high), gots, tiles, items, grad, final, n_north, n_east
    )
    chunks = chunks.reshape(n_east * n_north, SECT, LANES)
    parts = lax.all_to_all(chunks, ("east", "north"), 0, 0, tiled=True)
    return (final, sum_parts(parts))


def pair_shards(count, fields, lists, n_north):
    ce = fields[0].shape[1]
    swap = [(0, 1), (1, 0)]
    (rows,) = raw_rows(False, *fields)
    other = lax.ppermute(rows, "east", swap)
    own, face, items = raw_rows(True, *fields, count, lists)
    pack_both, coef = join_rows(own, other, ce)
    ways = [(n, n_north + n + 1) for n in range(n_north - 1)] + [(n_north + n, n - 1) for n in range(1, n_north)]
    got = lax.ppermute(pack_both, ("east", "north"), ways)
    faces = (lax.ppermute(face, "east", swap),) * 2
    final, *tiles, grad = sweeps(count, *fields, faces, lists, n_north, True)
    chunks, mine, fix = both_edges(
        items, faces[0], pack_both, coef, got, grad, fields[0].shape, n_north, 2, lists[0].shape[0]
    )
    parts = lax.all_to_all(chunks.reshape(2 * n_north, SECT, LANES), ("east", "north"), 0, 0, tiled=True)
    final = rows_home(mine, lax.ppermute(fix, "east", swap), tiles, final)
    return (final, sum_parts(parts))


def solution(mesh):
    placed = (
        P(None, "east", "north", None),
        P(None, "east", "north", None),
        P(None, "east", "north", None),
        P("east", "north", None),
        P("east", "north"),
        P("east", "north", None),
        P("east", "north", None),
        P("east", "north", None),
        P("east", "north", None),
    )
    return jax.shard_map(
        shards,
        mesh=mesh,
        in_specs=placed,
        out_specs=(P(None, "east", "north", None), P(None, None, "north")),
        check_vma=False,
    )
```

```python
import functools

import jax
import jax.numpy as jnp
from jax import lax
from jax.experimental import pallas as pl
from jax.experimental.pallas import tpu as pltpu
from jax.sharding import PartitionSpec as P

SECT = 8
HALF = SECT // 2
TURB_DEV = 12
COMPS = 4
LANES = 128
SUB = 8
PAD = 8
PACK = 14
FACE = 22
EDGE = 9
RAW = 23
ITEM = 8
STEP = 4
OUT_STEP = 4
ROWS_1 = 8
ROWS_2 = 16
VMEM = pltpu.VMEM
F32 = jnp.float32
BF16 = jnp.bfloat16


def whole(space=VMEM):
    return pl.BlockSpec(memory_space=space)


def in_hbm(*arrays):
    return [pltpu.with_memory_space_constraint(x, pltpu.HBM) for x in arrays]


def shape(*dims):
    return jax.ShapeDtypeStruct(dims, F32)


def params(mib):
    return pltpu.CompilerParams(vmem_limit_bytes=mib << 20)


def cost(flops, size):
    return pl.CostEstimate(flops=flops, bytes_accessed=size, transcendentals=0)


class Copies:
    def __init__(self, sems):
        self.sems, self.used = sems, 0

    def take(self, *pairs):
        first = self.used
        self.used += len(pairs)
        return first, pairs

    def made(self, taken):
        first, pairs = taken
        return [pltpu.make_async_copy(s, d, self.sems.at[first + k]) for k, (s, d) in enumerate(pairs)]

    def start(self, taken):
        for c in self.made(taken):
            c.start()

    def wait(self, taken):
        for c in self.made(taken):
            c.wait()


def neighbours():
    e, n = lax.axis_index("east"), lax.axis_index("north")
    last_e, last_n = lax.axis_size("east") - 1, lax.axis_size("north") - 1
    return [
        jnp.where(e > 0, 1, 0), jnp.where(e < last_e, 1, 0),
        jnp.where(n > 0, 1, 0), jnp.where(n < last_n, 1, 0),
    ]


def facing(ce):
    if lax.axis_size("east") == 2:
        e = lax.axis_index("east")
        return [((1 - e) * (ce - 1), (1 - e) * (ce - 1) + 2 * e - 1)]
    return [(0, 1), (ce - 1, ce - 2)]


def one_way(k, sign, w, u, f, inv_v, inv_m, bend=None):
    pull = (w + (0.5 * sign) * u) * inv_v
    out = [pull * f[c] for c in range(3)]
    out[k] = out[k] - (0.5 * sign) * f[3] * inv_v
    out.append((f[3] - (0.5 * sign) * f[k]) * (1.0 / 7.0))
    m = w * f[4]
    if bend is not None:
        m = m + 0.25 * bend
    out.append(m * inv_m)
    return out


def inverse(x):
    y = pl.reciprocal(x, approx=True)
    return y * (2.0 - x * y)


def inverses(w):
    six = 6.0 * w
    return inverse(six + 1.0), inverse(six + 2.0)


def dot3(a, b):
    return a[0] * b[0] + a[1] * b[1] + a[2] * b[2]


def plane_shifts(rows, cols):
    r = lax.broadcasted_iota(jnp.int32, (rows, cols), 0)
    z = lax.broadcasted_iota(jnp.int32, (rows, cols), 1)

    def east(x, before=0.0, after=0.0):
        return (
            jnp.where(r < rows - 1, pltpu.roll(x, rows - 1, 0), after),
            jnp.where(r > 0, pltpu.roll(x, 1, 0), before),
        )

    def level(x):
        return (
            jnp.where(z < cols - 1, pltpu.roll(x, cols - 1, 1), 0.0),
            jnp.where(z > 0, pltpu.roll(x, 1, 1), 0.0),
        )

    return east, level


def ends_kernel(ce, cn, n_faces, start, flow, *refs):
    outs, tiles_v, tiles_u, sems = refs[:n_faces], *refs[n_faces:]
    copies = Copies(sems)
    taken = []
    for i, (e, _) in enumerate(facing(ce)):
        pairs = []
        for side, first in enumerate((0, cn - SUB)):
            pairs.append((start.at[:, e, pl.ds(first, SUB)], tiles_v.at[i, side]))
            pairs.append((flow.at[:, e, pl.ds(first, SUB)], tiles_u.at[i, side]))
        taken.append(copies.take(*pairs))
        copies.start(taken[-1])
    for i, out in enumerate(outs):
        copies.wait(taken[i])
        for side, row in enumerate((0, SUB - 1)):
            for f in range(8):
                tile = tiles_v[i, side, f] if f < 5 else tiles_u[i, side, f - 5]
                out[side * 8 + f : side * 8 + f + 1, :] = tile[row : row + 1]


def row_ends(start, flow, n_faces):
    _, ce, cn, cz = start.shape
    return pl.pallas_call(
        functools.partial(ends_kernel, ce, cn, n_faces),
        out_shape=[shape(16, cz)] * n_faces,
        in_specs=[whole(pltpu.HBM)] * 2,
        out_specs=[whole()] * n_faces,
        scratch_shapes=[
            VMEM((n_faces, 2, 5, SUB, cz), F32),
            VMEM((n_faces, 2, 3, SUB, cz), F32),
            pltpu.SemaphoreType.DMA((4 * n_faces,)),
        ],
        compiler_params=params(60),
        cost_estimate=cost(0, 1 << 16),
    )(start, flow)


def pack_kernel(ce, cn, cz, n_faces, endp, endn, start, source, flow, eddy, *refs):
    packs, refs = refs[:2], refs[2:]
    faces, refs = refs[:n_faces], refs[n_faces:]
    tiles_v, tiles_u, tiles_s, tiles_e, sems = refs
    has = [x.astype(F32) for x in neighbours()[:2]]
    copies = Copies(sems)
    sides = ((0, 0, 1, -1.0), (cn - SUB, SUB - 1, SUB - 2, 1.0))
    needed = []
    for side, (first, _, _, _) in enumerate(sides):
        pairs = []
        for h in range(2):
            cut = (pl.ds(first, SUB), pl.ds(h * LANES, LANES))
            pairs += [
                (start.at[(slice(None), slice(None)) + cut], tiles_v.at[side, :, :, h]),
                (flow.at[(slice(None), slice(None)) + cut], tiles_u.at[side, :, :, h]),
                (eddy.at[(slice(None),) + cut], tiles_e.at[side, 0, :, h]),
                (source.at[(slice(None), slice(None)) + cut], tiles_s.at[side, :, :, h]),
            ]
        needed.append(copies.take(*pairs))
        copies.start(needed[-1])
    later = []
    for (near, far), face in zip(facing(ce), faces):
        taken = copies.take(
            (start.at[:, near], face.at[0:5]),
            (flow.at[:, near], face.at[5:8]),
            (eddy.at[near], face.at[8]),
            (source.at[:, near], face.at[9:14]),
            (start.at[:, far], face.at[14:19]),
            (flow.at[:, far], face.at[19:22]),
        )
        copies.start(taken)
        later.append(taken)
    east, level = plane_shifts(ce, cz)

    def line(ref, side, f, row):
        flat = ref.reshape(2, ref.shape[1], ce * 2 * SUB, LANES)
        return jnp.concatenate([flat[side, f, pl.ds(h * SUB + row, ce, stride=2 * SUB), :] for h in range(2)], axis=1)

    for side, (_, row, behind, sign) in enumerate(sides):
        copies.wait(needed[side])
        pack = packs[side]
        v = [line(tiles_v, side, f, row) for f in range(5)]
        u = [line(tiles_u, side, k, row) for k in range(3)]
        eddy_row = line(tiles_e, side, 0, row)
        inner = [line(tiles_v, side, f, behind) for f in range(5)]
        inner_u = [line(tiles_u, side, k, behind) for k in range(3)]
        src = [line(tiles_s, side, f, row) for f in range(5)]
        for f, x in enumerate(v + u + [eddy_row]):
            pack[f * ce : (f + 1) * ce, :] = x
        w = 1.0 + eddy_row
        inv_v, inv_m = inverses(w)
        before = [endp[side * 8 + f : side * 8 + f + 1, :] * has[0] for f in range(8)]
        after = [endn[side * 8 + f : side * 8 + f + 1, :] * has[1] for f in range(8)]
        for f in range(8):
            pack[PACK * ce + f : PACK * ce + f + 1, :] = before[f]
            pack[PACK * ce + 8 + f : PACK * ce + 9 + f, :] = after[f]
        total, slope0, slope2 = [], [], []
        for f in range(5):
            a, b = east(v[f], before[f], after[f])
            h, l = level(v[f])
            total.append((a + b) + (h + l))
            slope0.append(a - b)
            slope2.append(h - l)
        curv = []
        for k in range(3):
            a, b = east(u[k], before[5 + k], after[5 + k])
            h, l = level(u[k])
            curv.append((a + b) + (h + l) + inner_u[k] - 6.0 * u[k])
        out = one_way(1, -sign, w, u[1], inner, inv_v, inv_m, dot3(v, curv))
        press = (slope0[3], None, slope2[3])
        for c in range(3):
            more = src[c] + w * total[c] + 0.5 * (u[0] * slope0[c] + u[2] * slope2[c])
            if press[c] is not None:
                more = more - 0.5 * press[c]
            out[c] = out[c] + more * inv_v
        out[3] = out[3] + (src[3] + total[3] - 0.5 * (slope0[0] + slope2[2])) * (1.0 / 7.0)
        out[4] = out[4] + (src[4] + w * total[4]) * inv_m
        for f in range(5):
            pack[(9 + f) * ce : (10 + f) * ce, :] = out[f]
    for taken in later:
        copies.wait(taken)


def pack(ends, start, source, flow, eddy, n_faces):
    _, ce, cn, cz = start.shape
    out = [shape(PACK * ce + 16, cz)] * 2 + [shape(FACE, cn, cz)] * n_faces
    got = pl.pallas_call(
        functools.partial(pack_kernel, ce, cn, cz, n_faces),
        out_shape=out,
        in_specs=[whole()] * 2 + [whole(pltpu.HBM)] * 4,
        out_specs=[whole()] * len(out),
        scratch_shapes=[
            VMEM((2, 5, ce, 2, SUB, LANES), F32),
            VMEM((2, 3, ce, 2, SUB, LANES), F32),
            VMEM((2, 5, ce, 2, SUB, LANES), F32),
            VMEM((2, 1, ce, 2, SUB, LANES), F32),
            pltpu.SemaphoreType.DMA((16 + 6 * n_faces,)),
        ],
        compiler_params=params(60),
        cost_estimate=cost(1 << 22, 4 << 20),
    )(*ends, start, source, flow, eddy)
    return got[:2], got[2:]


def leave_chunks(chunks, acc, copies_out):
    whole_acc = acc[...]
    blocks = whole_acc.shape[0] // HALF
    for n in range(blocks):
        chunk = whole_acc[n * HALF : (n + 1) * HALF]
        for k in range(copies_out):
            chunks[k * blocks + n] = chunk


def split(x):
    high = x.astype(BF16)
    return high, (x - high.astype(F32)).astype(BF16)


def owner_of(turbine):
    return lax.shift_right_logical(turbine * 5462, 16)


def columns(x, first, size):
    return jnp.concatenate([x[:, k : k + 1] for k in range(first // LANES, (first + size) // LANES)], axis=0)


def lines(x, first, size):
    return jnp.concatenate([x[k : k + 1, :] for k in range(first // LANES, (first + size) // LANES)], axis=1)


def steps_of(chunks):
    sizes = [0] + [x for x in (2 * LANES,) if x < chunks * LANES] + [chunks * LANES]
    return list(zip(sizes[:-1], sizes[1:]))


def entries(live, cells, turbine, sector, weight, cz):
    cell, tur = cells[...], turbine[...]
    owner = owner_of(tur)
    pair = sector[...]
    key = (owner * HALF + lax.shift_right_logical(pair, 1)).astype(F32)
    local = (tur - owner * TURB_DEV + jnp.bitwise_and(pair, 1) * (COMPS * TURB_DEV)).astype(F32)
    slot = lax.broadcasted_iota(jnp.int32, cell.shape, 0) * LANES + lax.broadcasted_iota(jnp.int32, cell.shape, 1)
    load = jnp.where(slot < live, weight[...], 0.0)
    line = lax.shift_right_logical(cell, cz.bit_length() - 1)
    level = jnp.bitwise_and(cell, cz - 1).astype(F32)
    return slot, line, level, key, local, load


def gather_edge(chosen, edge_row, level, key, local, load, put):
    chunks = chosen.shape[0]
    lower = lax.broadcasted_iota(jnp.int32, (LANES, LANES), 0) < lax.broadcasted_iota(jnp.int32, (LANES, LANES), 1)
    rank = jnp.dot(chosen.astype(BF16), jnp.where(lower, 1.0, 0.0).astype(BF16), preferred_element_type=F32)
    sums = jnp.sum(chosen, axis=1, keepdims=True)
    so_far = jnp.zeros((1, 1), F32)
    starts = []
    for k in range(chunks):
        starts.append(so_far)
        so_far = so_far + sums[k : k + 1]
    rank = jnp.where(chosen > 0.0, rank + jnp.concatenate(starts, axis=0), -1.0)
    total = jnp.sum(chosen).astype(jnp.int32)
    load_high = load.astype(BF16).astype(F32)
    load_rest = load - load_high
    load_mid = load_rest.astype(BF16).astype(F32)
    load_low = load_rest - load_mid
    blank = jnp.zeros((1, LANES), F32)
    rows = [
        jnp.concatenate([x[k : k + 1] for x in (edge_row, level, key, local, load_high, load_mid, load_low)] + [blank])
        for k in range(chunks)
    ]
    to = lax.broadcasted_iota(jnp.int32, (LANES, LANES), 0).astype(F32)
    listed = jnp.concatenate(rows, axis=1).astype(BF16)

    @pl.loop(0, lax.div(total + (LANES - 1), LANES))
    def _(q):
        first = lax.convert_element_type(q * LANES, F32)
        where = jnp.concatenate(
            [jnp.where(rank[k : k + 1] - first == to, 1.0, 0.0) for k in range(chunks)], axis=1
        ).astype(BF16)
        put(q, lax.dot_general(listed, where, (((1,), (1,)), ((), ())), preferred_element_type=F32))

    return total


def rotor_terms(row, level, turbine, weight, key, table, blocks, acc):
    size = row.shape[0]
    rows, width = table.shape[0] // 2, table.shape[1]
    cz = width // COMPS
    lane_row = lax.broadcasted_iota(jnp.int32, (size, rows), 1).astype(F32)
    pick = jnp.where(row == lane_row, 1.0, 0.0).astype(BF16)
    got = jnp.dot(jnp.concatenate([pick, pick], axis=1), table[...], preferred_element_type=F32)
    here = level == lax.broadcasted_iota(jnp.int32, (size, cz), 1).astype(F32)
    lane = lax.broadcasted_iota(jnp.int32, (size, LANES), 1)
    lane_comp = jnp.bitwise_and(owner_of(lane), COMPS - 1)
    lane_tur = (lane - lane_comp * TURB_DEV).astype(F32)
    spread = jnp.zeros((size, LANES), F32)
    for c in range(COMPS):
        part = jnp.where(here, got[:, c * cz : (c + 1) * cz], 0.0)
        spread = jnp.where(lane_comp == c, jnp.sum(part, axis=1, keepdims=True), spread)
    spread = jnp.where(turbine == lane_tur, spread * weight, 0.0)
    lane_key = lax.broadcasted_iota(jnp.int32, (blocks * HALF, size), 0).astype(F32)
    to = jnp.where(lane_key == key, 1.0, 0.0).astype(BF16)
    high = spread.astype(BF16)
    rest = spread - high.astype(F32)
    mid, low = split(rest)
    parts = jnp.dot(to, jnp.concatenate([high, mid, low], axis=1), preferred_element_type=F32)
    acc[...] += parts[:, :LANES] + parts[:, LANES : 2 * LANES] + parts[:, 2 * LANES :]


def halves(ref, f, i, rows, move=0):
    first, size = rows
    return [ref[f, i, h, pl.ds(PAD + first + move, size), :] for h in range(2)]


def level_shifts(x, first, last):
    up = [pltpu.roll(x[h], LANES - 1, 1) for h in range(2)]
    down = [pltpu.roll(x[h], 1, 1) for h in range(2)]
    return (
        [jnp.where(last, up[1], up[0]), jnp.where(last, 0.0, up[1])],
        [jnp.where(first, 0.0, down[0]), jnp.where(first, down[0], down[1])],
    )


def slab_sweep(ref, i, rows, first, last, src, flow, visc, curv):
    two = range(2)
    w = visc
    inv = [inverses(w[h]) for h in two]
    w2 = [2.0 * w[h] for h in two]

    def sides(f):
        mid = halves(ref, f, i, rows)
        a, b = halves(ref, f, i + 1, rows), halves(ref, f, i - 1, rows)
        n, s = halves(ref, f, i, rows, 1), halves(ref, f, i, rows, -1)
        up, down = level_shifts(mid, first, last)
        return mid, a, b, n, s, up, down

    _, a, b, n, s, up, down = sides(3)
    grad = [[x[h] - y[h] for h in two] for x, y in ((a, b), (n, s), (up, down))]
    q_sum = [(a[h] + b[h]) + (n[h] + s[h]) + (up[h] + down[h]) for h in two]
    out, div, bend = [], [0.0, 0.0], [0.0, 0.0]
    for c in range(3):
        mid, a, b, n, s, up, down = sides(c)
        res = []
        for h in two:
            total = (a[h] + b[h]) + (n[h] + s[h]) + (up[h] + down[h])
            slope = [a[h] - b[h], n[h] - s[h], up[h] - down[h]]
            carried = flow[0][h] * slope[0] + flow[1][h] * slope[1] + flow[2][h] * slope[2]
            res.append((src(c)[h] + 0.5 * (w2[h] * total + (carried - grad[c][h]))) * inv[h][0])
            div[h] = div[h] + slope[c]
            bend[h] = bend[h] + mid[h] * curv[c][h]
        out.append(res)
    out.append([(src(3)[h] + q_sum[h] - 0.5 * div[h]) * (1.0 / 7.0) for h in two])
    _, a, b, n, s, up, down = sides(4)
    res = []
    for h in two:
        total = (a[h] + b[h]) + (n[h] + s[h]) + (up[h] + down[h])
        res.append((src(4)[h] + w[h] * total + 0.25 * bend[h]) * inv[h][1])
    out.append(res)
    return out


def sweeps_kernel(
    ce, cn, cz, blocks, pair,
    count, start, source, flow, eddy, facep, facen, cells, turbine, sector, weight,
    final, edge_low, edge_high, grad, *refs,
):
    if not pair:
        coef_low, coef_high, items, n_items = refs[:4]
    held, v0, u, src, ed, v1, curv, table, sems = refs[-9:]
    copies = Copies(sems)
    two = range(2)
    has = [x > 0 for x in neighbours()[:2]]
    inner = pl.ds(PAD, cn)

    def part(h):
        return pl.ds(h * LANES, LANES)

    def halo(face, near, far, slab):
        pairs = []
        for h in two:
            pairs += [
                (face.at[0:5, :, part(h)], v0.at[:, near, h, inner]),
                (face.at[5:8, :, part(h)], u.at[:, near, h, inner]),
                (face.at[8, :, part(h)], ed.at[0, slab, h]),
                (face.at[9:14, :, part(h)], src.at[:, slab, h]),
                (face.at[14:19, :, part(h)], v0.at[:, far, h, inner]),
                (face.at[19:22, :, part(h)], u.at[:, far, h, inner]),
            ]
        return pairs

    ends = ((facep, 1, 0, 0), (facen, ce + 2, ce + 3, ce + 1))
    halos = [copies.take(*halo(*x)) for x in ends]

    def group(g, size):
        span, own, own2 = pl.ds(g, size), pl.ds(g + 1, size), pl.ds(g + 2, size)
        pairs = []
        for h in two:
            pairs += [
                (start.at[:, span, :, part(h)], v0.at[:, own2, h, inner]),
                (flow.at[:, span, :, part(h)], u.at[:, own2, h, inner]),
                (eddy.at[span, :, part(h)], ed.at[0, own, h]),
                (source.at[:, span, :, part(h)], src.at[:, own, h]),
            ]
        return pairs

    groups = [copies.take(*group(g, STEP)) for g in range(0, ce, STEP)]
    per = len(groups[0][1])
    copies.start(groups[0])
    for exists, taken in zip(has, halos):

        @pl.when(exists)
        def _():
            copies.start(taken)

    for taken in groups[1:]:
        copies.start(taken)

    blank = jnp.zeros((PAD, LANES), F32)
    for ref, fields in ((v0, 5), (u, 3), (v1, 5)):

        @pl.loop(0, ref.shape[1])
        def _(i):
            for f in range(fields):
                for h in two:
                    ref[f, i, h, 0:PAD, :] = blank
                    ref[f, i, h, PAD + cn : PAD + cn + PAD, :] = blank

    for exists, (_, near, _, end) in zip(has, ends):

        @pl.when(jnp.logical_not(exists))
        def _():
            for ref, fields, slab in ((v0, 5, near), (u, 3, near), (v1, 5, end)):
                for f in range(fields):
                    for h in two:
                        ref[f, slab, h, inner, :] = jnp.zeros((cn, LANES), F32)

    def ends_of(size):
        lane = lax.broadcasted_iota(jnp.int32, (size, LANES), 1)
        return lane == 0, lane == LANES - 1

    live = count[0, 0]
    slot, line, level, key, local, load = entries(live, cells, turbine, sector, weight, cz)
    chunks = slot.shape[0]
    if not pair:
        north = jnp.bitwise_and(line, cn - 1)
        east = lax.shift_right_logical(line, cn.bit_length() - 1)
        place = jnp.where(north == 0, 0, jnp.where(north == 1, 1, jnp.where(north == cn - 1, 2, 3)))
        is_edge = jnp.logical_or(north <= 1, north >= cn - 2)
        chosen = jnp.where(jnp.logical_and(is_edge, slot < live), 1.0, 0.0)
        edge_row = (place * ce + east).astype(F32)
        items[...] = jnp.zeros_like(items)

        def put(q, x):
            items[q] = x

        n_items[0] = gather_edge(chosen, edge_row, level, key, local, load, put)

    @pl.when(has[0])
    def _():
        copies.wait(halos[0])

    low_slab, high_slab = jnp.where(has[0], 0, 1), jnp.where(has[1], ce + 2, ce + 1)
    steps = ce // STEP

    @pl.loop(0, steps)
    def _(g):
        copies.wait((groups[0][0] + g * per, group(g * STEP, STEP)))

        @pl.when(jnp.logical_and(g == steps - 1, has[1]))
        def _():
            copies.wait(halos[1])

        @pl.loop(jnp.where(g == 0, low_slab, g * STEP), jnp.where(g == steps - 1, high_slab, (g + 1) * STEP))
        def _(i):
            mid = i + 1
            first, last = ends_of(ROWS_1)
            for r in range(0, cn, ROWS_1):
                rows, at = (r, ROWS_1), pl.ds(r, ROWS_1)
                flows = [halves(u, k, mid, rows) for k in range(3)]
                bends = []
                for k in range(3):
                    a, b = halves(u, k, mid + 1, rows), halves(u, k, mid - 1, rows)
                    n, s = halves(u, k, mid, rows, 1), halves(u, k, mid, rows, -1)
                    up, down = level_shifts(flows[k], first, last)
                    res = [(a[h] + b[h]) + (n[h] + s[h]) + (up[h] + down[h]) - 6.0 * flows[k][h] for h in two]
                    for h in two:
                        curv[k, i, h, at, :] = res[h]
                    bends.append(res)
                out = slab_sweep(
                    v0, mid, rows, first, last,
                    lambda f: [src[f, i, h, at, :] for h in two],
                    flows, [1.0 + ed[0, i, h, at, :] for h in two], bends,
                )
                for f in range(5):
                    for h in two:
                        v1[f, i, h, pl.ds(PAD + r, ROWS_1), :] = out[f][h]

    def leave(e):
        return [(held.at[:, pl.ds(e, OUT_STEP)], final.at[:, pl.ds(e, OUT_STEP)])]

    outs = [copies.take(*leave(e)) for e in range(0, ce, OUT_STEP)]

    @pl.loop(0, ce // OUT_STEP)
    def _(g):
        @pl.loop(0, OUT_STEP)
        def _(k):
            e = g * OUT_STEP + k
            i = e + 1
            first, last = ends_of(ROWS_2)

            for r in range(0, cn, ROWS_2):
                rows, span = (r, ROWS_2), pl.ds(r, ROWS_2)
                flows = [halves(u, k, i + 1, rows) for k in range(3)]
                bends = [[curv[k, i, h, span, :] for h in two] for k in range(3)]
                out = slab_sweep(
                    v1, i, rows, first, last,
                    lambda f: [src[f, i, h, span, :] for h in two],
                    flows, [1.0 + ed[0, i, h, span, :] for h in two], bends,
                )
                at = pl.ds(pl.multiple_of(e * cn + r, ROWS_2), ROWS_2)
                below = pl.ds(pl.multiple_of((ce + e) * cn + r, ROWS_2), ROWS_2)
                for h in two:
                    force = flows[0][h] * jnp.abs(flows[0][h])
                    for f in range(5):
                        held[f, e, span, part(h)] = out[f][h]
                    for c in range(COMPS):
                        hi, lo = split(out[c if c < 3 else 4][h] * force)
                        wide = pl.ds(c * cz + h * LANES, LANES)
                        table[at, wide] = hi
                        table[below, wide] = lo

        copies.start((outs[0][0] + g, leave(g * OUT_STEP)))

    def edge_plane(ref, k, first, tall, row):
        fields, slabs = ref.shape[:2]
        flat = ref.reshape(fields, slabs * 2 * tall, LANES)
        return jnp.concatenate(
            [flat[k, pl.ds((first * 2 + h) * tall + row, ce, stride=2 * tall), :] for h in two], axis=1
        )

    tall = PAD + cn + PAD
    edge_rows = () if pair else ((coef_low, 0, 1), (coef_high, cn - 1, cn - 2))
    for coef, row, behind in edge_rows:
        planes = [edge_plane(curv, k, 1, cn, row) for k in range(3)]
        planes += [edge_plane(u, 1, 2, tall, PAD + behind), edge_plane(ed, 0, 1, cn, behind), edge_plane(u, 0, 2, tall, PAD + behind)]
        planes += [edge_plane(v1, k, 1, tall, PAD + row) for k in range(3)]
        for k, x in enumerate(planes):
            coef[k * ce : (k + 1) * ce, :] = x

    tiles = copies.take((held.at[:, :, 0:SUB, :], edge_low), (held.at[:, :, cn - SUB : cn, :], edge_high))
    copies.start(tiles)

    row_t, level_t, local_t, load_t = line.astype(F32).T, level.T, local.T, load.T
    grad[...] = jnp.zeros_like(grad)
    for least, size in steps_of(chunks):

        @pl.when(jnp.logical_and(live > least, live <= size))
        def _():
            cols = [columns(x, 0, size) for x in (row_t, level_t, local_t, load_t)]
            rotor_terms(*cols, lines(key, 0, size), table, blocks, grad)

    for taken in outs + [tiles]:
        copies.wait(taken)


def sweeps(count, start, source, flow, eddy, faces, lists, blocks, pair):
    _, ce, cn, cz = start.shape
    chunks = lists[0].shape[0]
    tall = PAD + cn + PAD
    more = [shape(EDGE * ce, cz)] * 2 + [shape(chunks, ITEM, LANES), jax.ShapeDtypeStruct((1,), jnp.int32)]
    return pl.pallas_call(
        functools.partial(sweeps_kernel, ce, cn, cz, blocks, pair),
        out_shape=[shape(*start.shape)] + [shape(5, ce, SUB, cz)] * 2 + [shape(blocks * HALF, LANES)] + ([] if pair else more),
        in_specs=[whole(pltpu.SMEM)] + [whole(pltpu.HBM)] * 6 + [whole()] * 4,
        out_specs=[whole(pltpu.HBM), whole(), whole(), whole()] + ([] if pair else [whole()] * 3 + [whole(pltpu.SMEM)]),
        scratch_shapes=[
            VMEM(start.shape, F32),
            VMEM((5, ce + 4, 2, tall, LANES), F32),
            VMEM((3, ce + 4, 2, tall, LANES), F32),
            VMEM((5, ce + 2, 2, cn, LANES), F32),
            VMEM((1, ce + 2, 2, cn, LANES), F32),
            VMEM((5, ce + 2, 2, tall, LANES), F32),
            VMEM((3, ce + 2, 2, cn, LANES), F32),
            VMEM((2 * ce * cn, COMPS * cz), BF16),
            pltpu.SemaphoreType.DMA((26 + 8 * (ce // STEP) + ce // OUT_STEP,)),
        ],
        compiler_params=params(48),
        cost_estimate=cost(0, 1 << 10),
    )(count, *in_hbm(start, source, flow, eddy), *faces, *lists)


def edge_kernel(
    ce, cn, cz, blocks, copies_out,
    n_items, facep, facen, own_low, own_high, coef_low, coef_high, got_prev, got_next,
    edge_low, edge_high, items, grad, final_in,
    final, chunks,
    low_out, high_out, table, acc, sems,
):
    east, level = plane_shifts(ce, cz)
    sub = lax.broadcasted_iota(jnp.int32, (SUB, cz), 0)
    has = [x.astype(F32) for x in neighbours()]
    sides = (
        (-1.0, 0, own_low, coef_low, got_prev, edge_low, low_out, 0),
        (1.0, cn - 1, own_high, coef_high, got_next, edge_high, high_out, cn - SUB),
    )
    waits = []
    for side, (sign, row, own, coef, got, edge, out_ref, place) in enumerate(sides):

        def plane(ref, f):
            return ref[f * ce : (f + 1) * ce, :]

        v0 = [plane(own, f) for f in range(5)]
        u = [plane(own, 5 + k) for k in range(3)]
        w = 1.0 + plane(own, 8)
        xv = [plane(got, f) for f in range(5)]
        xu = [plane(got, 5 + k) for k in range(3)]
        xw = 1.0 + plane(got, 8)
        xp = [plane(got, 9 + f) for f in range(5)]
        curv = [plane(coef, k) for k in range(3)]
        inv_v, inv_m = inverses(w)
        delta = one_way(1, sign, w, u[1], xv, inv_v, inv_m, dot3(v0, xu))
        back = one_way(1, -sign, xw, xu[1], v0, *inverses(xw), dot3(xv, u))
        x1 = [xp[f] + back[f] for f in range(5)]
        ends = []
        for far, face in enumerate((facep, facen)):
            hv = [got[PACK * ce + 8 * far + f : PACK * ce + 8 * far + f + 1, :] for f in range(8)]
            fv = [face[f, row : row + 1, :] * has[far] for f in range(5)]
            fu = face[6, row : row + 1, :] * has[far]
            fw = 1.0 + face[8, row : row + 1, :] * has[far]
            ends.append(one_way(1, sign, fw, fu, hv, *inverses(fw), dot3(fv, hv[5:])))
        x1 = [x * has[2 + side] for x in x1]
        total, slope0, slope2 = [], [], []
        for f in range(5):
            a, b = east(delta[f], ends[0][f], ends[1][f])
            h, l = level(delta[f])
            total.append((a + b) + (h + l))
            slope0.append(a - b)
            slope2.append(h - l)
        full = [plane(coef, 6 + c) + delta[c] for c in range(3)]
        add = one_way(1, sign, w, u[1], x1, inv_v, inv_m, dot3(full, xu) + dot3(delta, curv))
        press = (slope0[3], None, slope2[3])
        for c in range(3):
            more = w * total[c] + 0.5 * (u[0] * slope0[c] + u[2] * slope2[c])
            if press[c] is not None:
                more = more - 0.5 * press[c]
            add[c] = add[c] + more * inv_v
        add[3] = add[3] + (total[3] - 0.5 * (slope0[0] + slope2[2])) * (1.0 / 7.0)
        add[4] = add[4] + w * total[4] * inv_m
        ru1, rw, ru0 = plane(coef, 3), 1.0 + plane(coef, 4), plane(coef, 5)
        behind = one_way(1, sign, rw, ru1, delta, *inverses(rw))
        near, far = (0, 1) if side == 0 else (SUB - 1, SUB - 2)
        for f in range(5):
            for e in range(ce):
                rows = jnp.where(
                    sub == near, add[f][e : e + 1, :], jnp.where(sub == far, behind[f][e : e + 1, :], 0.0)
                )
                out_ref[f, e] = edge[f, e] + rows
        copy = pltpu.make_async_copy(out_ref, final.at[:, :, pl.ds(place, SUB), :], sems.at[side])
        copy.start()
        waits.append(copy)
        for behind_row, u0, values in ((0, u[0], add), (1, ru0, behind)):
            force = u0 * jnp.abs(u0)
            at = (2 * side + behind_row) * ce
            for c in range(COMPS):
                hi, lo = split(values[c if c < 3 else 4] * force)
                table[at : at + ce, c * cz : (c + 1) * cz] = hi
                table[4 * ce + at : 5 * ce + at, c * cz : (c + 1) * cz] = lo

    acc[...] = grad[...]
    live = n_items[0]
    for least, size in steps_of(items.shape[0]):

        @pl.when(jnp.logical_and(live > least, live <= size))
        def _():
            lists = [items[k] for k in range(size // LANES)]
            turned = [x.T for x in lists]

            def col(j):
                return jnp.concatenate([x[:, j : j + 1] for x in turned], axis=0)

            key = jnp.concatenate([x[2:3] for x in lists], axis=1)
            rotor_terms(col(0), col(1), col(3), col(4) + col(5) + col(6), key, table, blocks, acc)

    leave_chunks(chunks, acc, copies_out)
    for copy in waits:
        copy.wait()


def edges(n_items, faces, packs, coefs, gots, tiles, items, grad, final, blocks, size):
    _, ce, cn, cz = final.shape
    args = (n_items, *faces, *packs, *coefs, *gots, *tiles, items, grad, final)
    tile = VMEM((5, ce, SUB, cz), F32)
    return pl.pallas_call(
        functools.partial(edge_kernel, ce, cn, cz, blocks, size),
        out_shape=(shape(*final.shape), shape(size * blocks, HALF, LANES)),
        in_specs=[whole(pltpu.SMEM)] + [whole()] * (len(args) - 2) + [whole(pltpu.HBM)],
        out_specs=(whole(pltpu.HBM), whole()),
        scratch_shapes=[
            tile,
            tile,
            VMEM((8 * ce, COMPS * cz), BF16),
            VMEM((blocks * HALF, LANES), F32),
            pltpu.SemaphoreType.DMA((2,)),
        ],
        input_output_aliases={len(args) - 1: 0},
        compiler_params=params(32),
        cost_estimate=cost(1 << 24, 4 << 20),
    )(*args)


def side(own):
    e = lax.axis_index("east")
    return 1 - e if own else e


def raw_kernel(ce, cn, cz, own, *refs):
    if own:
        count, refs = refs[0], refs[1:]
    start, source, flow, eddy, refs = *refs[:4], refs[4:]
    if own:
        lists, (rows, face, items), refs = refs[:4], refs[4:7], refs[7:]
        cells, turbine, sector, weight, sems = refs[4:]
    else:
        rows, sems = refs[0], refs[-1]
        refs = refs[1:]
    tiles_v, tiles_u, tiles_s, tiles_e = refs[:4]
    copies = Copies(sems)
    high = side(own)
    if own:
        held = copies.take(*zip(lists, (cells, turbine, sector, weight)))
        copies.start(held)
    def two_rows(at, to):
        pairs = []
        for h in range(2):
            cut, place = (pl.ds(at, 2), pl.ds(h * LANES, LANES)), pl.ds(to, 2)
            pairs += [
                (start.at[(slice(None), slice(None)) + cut], tiles_v.at[:, :, h, place]),
                (flow.at[(slice(None), slice(None)) + cut], tiles_u.at[:, :, h, place]),
                (eddy.at[(slice(None),) + cut], tiles_e.at[0, :, h, place]),
                (source.at[(slice(None), slice(None)) + cut], tiles_s.at[:, :, h, place]),
            ]
        return pairs

    sides = [copies.take(*two_rows(0, 0)), copies.take(*two_rows(cn - 2, SUB - 2))]

    def both_ways(act):
        for k, taken in enumerate(sides):

            @pl.when(high == k)
            def _():
                act(taken)

    both_ways(copies.start)
    if own:
        ((near, far),) = facing(ce)
        later = copies.take(
            (start.at[:, near], face.at[0:5]),
            (flow.at[:, near], face.at[5:8]),
            (eddy.at[near], face.at[8]),
            (source.at[:, near], face.at[9:14]),
            (start.at[:, far], face.at[14:19]),
            (flow.at[:, far], face.at[19:22]),
        )
        copies.start(later)
        copies.wait(held)
        live = count[0, 0]
        listed = entries(live, cells, turbine, sector, weight, cz)
        edge_items(ce, cn, cz, live, listed, high, items)
        edge_items(ce, cn, cz, live, listed, 1 - high, face.at[FACE:].reshape(-1, cz))

    def plane(ref, f, low, top):
        flat = ref.reshape(ref.shape[0], ce * 2 * SUB, LANES)
        parts = []
        for h in range(2):
            x, y = (flat[f, pl.ds(h * SUB + at, ce, stride=2 * SUB), :] for at in (low, top))
            parts.append(jnp.where(high > 0, y, x))
        return jnp.concatenate(parts, axis=1)

    both_ways(copies.wait)
    planes = [(tiles_v, f, 0) for f in range(5)] + [(tiles_u, k, 0) for k in range(3)] + [(tiles_e, 0, 0)]
    planes += [(tiles_s, f, 0) for f in range(5)]
    planes += [(tiles_v, f, 1) for f in range(5)] + [(tiles_u, k, 1) for k in range(3)] + [(tiles_e, 0, 1)]
    for k, (ref, f, at) in enumerate(planes):
        rows[k * ce : (k + 1) * ce, :] = plane(ref, f, at, SUB - 1 - at)
    if own:
        copies.wait(later)


def edge_items(ce, cn, cz, live, listed, high, out):
    slot, line, level, key, local, load = listed
    north = jnp.bitwise_and(line, cn - 1)
    column = lax.shift_right_logical(line, cn.bit_length() - 1) + lax.axis_index("east") * ce
    edge = high * (cn - 1)
    behind = edge + 1 - 2 * high
    chosen = jnp.where(jnp.logical_and(jnp.logical_or(north == edge, north == behind), slot < live), 1.0, 0.0)
    edge_row = (jnp.where(north == behind, 2 * ce, 0) + column).astype(F32)
    out[...] = jnp.zeros(out.shape, F32)

    def put(q, x):
        out[pl.ds(pl.multiple_of(q * ITEM, ITEM), ITEM), :LANES] = x

    total = gather_edge(chosen, edge_row, level, key, local, load, put)
    out[out.shape[0] - ITEM :, :] = jnp.full((ITEM, cz), total.astype(F32))


def raw_rows(own, start, source, flow, eddy, count=None, lists=()):
    _, ce, cn, cz = start.shape
    out = [shape(RAW * ce, cz)]
    scratch = [
        VMEM((5, ce, 2, SUB, LANES), F32),
        VMEM((3, ce, 2, SUB, LANES), F32),
        VMEM((5, ce, 2, SUB, LANES), F32),
        VMEM((1, ce, 2, SUB, LANES), F32),
    ]
    if own:
        chunks = lists[0].shape[0]
        most = (chunks + 1) * ITEM
        planes = pl.cdiv(most, cn)
        out += [shape(FACE + planes, cn, cz), shape(planes * cn, cz)]
        scratch += [VMEM((chunks, LANES), x.dtype) for x in lists]
    return pl.pallas_call(
        functools.partial(raw_kernel, ce, cn, cz, own),
        out_shape=out,
        in_specs=([whole(pltpu.SMEM)] if own else []) + [whole(pltpu.HBM)] * (4 + len(lists)),
        out_specs=[whole()] * len(out),
        scratch_shapes=scratch + [pltpu.SemaphoreType.DMA((26,))],
        compiler_params=params(16),
        cost_estimate=cost(0, 1 << 10),
    )(*([count] if own else []), *in_hbm(start, source, flow, eddy, *lists))


def joined(ce, own, other, k):
    west = lax.axis_index("east") == 0
    a, b = own[k * ce : (k + 1) * ce, :], other[k * ce : (k + 1) * ce, :]
    return jnp.concatenate([jnp.where(west, a, b), jnp.where(west, b, a)], axis=0)


def join_kernel(ce, cz, own, other, pack, coef):
    sign = (2 * side(True) - 1).astype(F32)
    east, level = plane_shifts(2 * ce, cz)
    raw = [joined(ce, own, other, k) for k in range(RAW)]
    v, u, src, inner, inner_u = raw[:5], raw[5:8], raw[9:14], raw[14:19], raw[19:22]
    w = 1.0 + raw[8]
    inv_v, inv_m = inverses(w)
    total, slope0, slope2 = [], [], []
    for f in range(5):
        a, b = east(v[f])
        h, l = level(v[f])
        total.append((a + b) + (h + l))
        slope0.append(a - b)
        slope2.append(h - l)
    curv = []
    for k in range(3):
        a, b = east(u[k])
        h, l = level(u[k])
        curv.append((a + b) + (h + l) + inner_u[k] - 6.0 * u[k])
    out = one_way(1, -sign, w, u[1], inner, inv_v, inv_m, dot3(v, curv))
    press = (slope0[3], None, slope2[3])
    for c in range(3):
        more = src[c] + w * total[c] + 0.5 * (u[0] * slope0[c] + u[2] * slope2[c])
        if press[c] is not None:
            more = more - 0.5 * press[c]
        out[c] = out[c] + more * inv_v
    out[3] = out[3] + (src[3] + total[3] - 0.5 * (slope0[0] + slope2[2])) * (1.0 / 7.0)
    out[4] = out[4] + (src[4] + w * total[4]) * inv_m
    for k, x in enumerate(raw[:9] + out):
        pack[2 * k * ce : 2 * (k + 1) * ce, :] = x
    for k, x in enumerate(curv + [inner_u[1], raw[22], inner_u[0]]):
        coef[2 * k * ce : 2 * (k + 1) * ce, :] = x


def join_rows(own, other, ce):
    cz = own.shape[1]
    return pl.pallas_call(
        functools.partial(join_kernel, ce, cz),
        out_shape=[shape(PACK * 2 * ce, cz), shape(6 * 2 * ce, cz)],
        in_specs=[whole()] * 2,
        out_specs=[whole()] * 2,
        compiler_params=params(16),
        cost_estimate=cost(0, 1 << 10),
    )(own, other)


def both_kernel(
    ce, cn, cz, blocks, copies_out, n_chunks,
    own, other, pack, coef, got, grad,
    chunks, mine, fix,
    table, acc,
):
    other = other.at[FACE:].reshape(-1, cz)
    wide = 2 * ce
    high = side(True)
    sign = (2 * high - 1).astype(F32)
    north = lax.axis_index("north")
    exists = jnp.where(high > 0, north < lax.axis_size("north") - 1, north > 0).astype(F32)
    east, level = plane_shifts(wide, cz)

    def plane(ref, f):
        return ref[f * wide : (f + 1) * wide, :]

    v0 = [plane(pack, f) for f in range(5)]
    u = [plane(pack, 5 + k) for k in range(3)]
    w = 1.0 + plane(pack, 8)
    xv = [plane(got, f) for f in range(5)]
    xu = [plane(got, 5 + k) for k in range(3)]
    xw = 1.0 + plane(got, 8)
    curv = [plane(coef, k) for k in range(3)]
    inv_v, inv_m = inverses(w)
    delta = one_way(1, sign, w, u[1], xv, inv_v, inv_m, dot3(v0, xu))
    back = one_way(1, -sign, xw, xu[1], v0, *inverses(xw), dot3(xv, u))
    x1 = [(plane(got, 9 + f) + back[f]) * exists for f in range(5)]
    total, slope0, slope2 = [], [], []
    for f in range(5):
        a, b = east(delta[f])
        h, l = level(delta[f])
        total.append((a + b) + (h + l))
        slope0.append(a - b)
        slope2.append(h - l)
    full = [plane(pack, 9 + c) + delta[c] for c in range(3)]
    add = one_way(1, sign, w, u[1], x1, inv_v, inv_m, dot3(full, xu) + dot3(delta, curv))
    press = (slope0[3], None, slope2[3])
    for c in range(3):
        more = w * total[c] + 0.5 * (u[0] * slope0[c] + u[2] * slope2[c])
        if press[c] is not None:
            more = more - 0.5 * press[c]
        add[c] = add[c] + more * inv_v
    add[3] = add[3] + (total[3] - 0.5 * (slope0[0] + slope2[2])) * (1.0 / 7.0)
    add[4] = add[4] + w * total[4] * inv_m
    ru1, rw, ru0 = plane(coef, 3), 1.0 + plane(coef, 4), plane(coef, 5)
    behind = one_way(1, sign, rw, ru1, delta, *inverses(rw))
    west = lax.axis_index("east") == 0
    for k, x in enumerate(add + behind):
        mine[k * ce : (k + 1) * ce, :] = jnp.where(west, x[:ce], x[ce:])
        fix[k * ce : (k + 1) * ce, :] = jnp.where(west, x[ce:], x[:ce])
    for row, u0, values in ((0, u[0], add), (1, ru0, behind)):
        force = u0 * jnp.abs(u0)
        for c in range(COMPS):
            hi, lo = split(values[c if c < 3 else 4] * force)
            table[row * wide : (row + 1) * wide, c * cz : (c + 1) * cz] = hi
            table[(2 + row) * wide : (3 + row) * wide, c * cz : (c + 1) * cz] = lo

    acc[...] = grad[...]
    most = n_chunks

    def chunk(ref, q):
        return ref[q * ITEM : (q + 1) * ITEM, :LANES]

    def terms(lists):
        turned = [x.T for x in lists]

        def col(j):
            return jnp.concatenate([x[:, j : j + 1] for x in turned], axis=0)

        key = jnp.concatenate([x[2:3] for x in lists], axis=1)
        rotor_terms(col(0), col(1), col(3), col(4) + col(5) + col(6), key, table, blocks, acc)

    terms([chunk(own, 0), chunk(other, 0)])
    longest = jnp.max(jnp.maximum(own[own.shape[0] - ITEM :, :LANES], other[other.shape[0] - ITEM :, :LANES]))

    @pl.when(longest > float(LANES))
    def _():
        terms([chunk(ref, q) for ref in (own, other) for q in range(1, most)])

    leave_chunks(chunks, acc, copies_out)


def both_edges(own, other, pack, coef, got, grad, size, blocks, copies_out, n_chunks):
    _, ce, cn, cz = size
    return pl.pallas_call(
        functools.partial(both_kernel, ce, cn, cz, blocks, copies_out, n_chunks),
        out_shape=(shape(copies_out * blocks, HALF, LANES), shape(10 * ce, cz), shape(10 * ce, cz)),
        in_specs=[whole()] * 6,
        out_specs=(whole(), whole(), whole()),
        scratch_shapes=[
            VMEM((8 * ce, COMPS * cz), BF16),
            VMEM((blocks * HALF, LANES), F32),
        ],
        compiler_params=params(32),
        cost_estimate=cost(0, 1 << 10),
    )(own, other, pack, coef, got, grad)


def last_kernel(ce, cn, parts, mine, fix, edge_low, edge_high, final_in, final, out_sum, low_out, high_out, sems):
    cz = edge_low.shape[3]
    sub = lax.broadcasted_iota(jnp.int32, (SUB, cz), 0)
    high = side(True) > 0
    waits = []
    for k, (edge, out, near, far, place) in enumerate(
        ((edge_low, low_out, 0, 1, 0), (edge_high, high_out, SUB - 1, SUB - 2, cn - SUB))
    ):
        from_mine = high if k else jnp.logical_not(high)
        for f in range(5):

            def plane(at):
                span = pl.ds(at * ce, ce)
                return jnp.where(from_mine, mine[span, :], fix[span, :])

            a, b = plane(f), plane(5 + f)
            for e in range(ce):
                rows = jnp.where(sub == near, a[e : e + 1, :], jnp.where(sub == far, b[e : e + 1, :], 0.0))
                out[f, e] = edge[f, e] + rows
        copy = pltpu.make_async_copy(out, final.at[:, :, pl.ds(place, SUB), :], sems.at[k])
        copy.start()
        waits.append(copy)
    sum_kernel(parts, out_sum)
    for copy in waits:
        copy.wait()


def last_step(parts, mine, fix, tiles, final):
    _, ce, cn, cz = final.shape
    return pl.pallas_call(
        functools.partial(last_kernel, ce, cn),
        out_shape=(shape(*final.shape), shape(COMPS, SECT, TURB_DEV)),
        in_specs=[whole()] * 5 + [whole(pltpu.HBM)],
        out_specs=(whole(pltpu.HBM), whole()),
        scratch_shapes=[
            VMEM((5, ce, SUB, cz), F32),
            VMEM((5, ce, SUB, cz), F32),
            pltpu.SemaphoreType.DMA((2,)),
        ],
        input_output_aliases={5: 0},
        compiler_params=params(16),
        cost_estimate=cost(0, 1 << 10),
    )(parts, mine, fix, *tiles, final)


def sum_kernel(parts, out):
    total = jnp.sum(parts[...], axis=0)
    for c in range(COMPS):
        for k in range(SECT):
            at = (k % 2 * COMPS + c) * TURB_DEV
            out[c, k : k + 1, :] = total[k // 2 : k // 2 + 1, at : at + TURB_DEV]


def sum_parts(parts):
    return pl.pallas_call(
        sum_kernel,
        out_shape=shape(COMPS, SECT, TURB_DEV),
        in_specs=[whole()],
        out_specs=whole(),
        compiler_params=params(4),
        cost_estimate=cost(parts.size, parts.size * 4),
    )(parts)


def beside(x, size):
    if size == 2:
        got = lax.ppermute(x[0], "east", [(0, 1), (1, 0)])
        return got, got
    up = [(i, i + 1) for i in range(size - 1)]
    down = [(i + 1, i) for i in range(size - 1)]
    return lax.ppermute(x[1], "east", up), lax.ppermute(x[0], "east", down)


def north_ways(x, size):
    up = [(i, i + 1) for i in range(size - 1)]
    down = [(i + 1, i) for i in range(size - 1)]
    return lax.ppermute(x[1], "north", up), lax.ppermute(x[0], "north", down)


def shards(
    adjoint_start,
    adjoint_source,
    base_flow,
    eddy_visc,
    rotor_count,
    rotor_cell,
    rotor_turbine,
    rotor_sector,
    rotor_weight,
):
    _, ce, cn, cz = adjoint_start.shape
    n_east, n_north = lax.axis_size("east"), lax.axis_size("north")
    count = rotor_count
    slots = rotor_cell.shape[-1]
    lists = [x.reshape(slots // LANES, LANES) for x in (rotor_cell, rotor_turbine, rotor_sector, rotor_weight)]

    fields = adjoint_start, adjoint_source, base_flow, eddy_visc
    if n_east == 2:
        return pair_shards(count, fields, lists, n_north)
    n_faces = 2
    ends = beside(row_ends(adjoint_start, base_flow, n_faces), n_east)
    packs, own = pack(ends, *fields, n_faces)
    gots = north_ways(packs, n_north)
    faces = beside(own, n_east)
    final, *tiles, grad, coef_low, coef_high, items, n_items = sweeps(count, *fields, faces, lists, n_north, False)
    final, chunks = edges(
        n_items, faces, packs, (coef_low, coef_high), gots, tiles, items, grad, final, n_north, n_east
    )
    parts = lax.all_to_all(chunks, ("east", "north"), 0, 0, tiled=True)
    return (final, sum_parts(parts))


def pair_shards(count, fields, lists, n_north):
    ce = fields[0].shape[1]
    swap = [(0, 1), (1, 0)]
    (rows,) = raw_rows(False, *fields)
    other = lax.ppermute(rows, "east", swap)
    own, face, items = raw_rows(True, *fields, count, lists)
    pack_both, coef = join_rows(own, other, ce)
    ways = [(n, n_north + n + 1) for n in range(n_north - 1)] + [(n_north + n, n - 1) for n in range(1, n_north)]
    got = lax.ppermute(pack_both, ("east", "north"), ways)
    faces = (lax.ppermute(face, "east", swap),) * 2
    final, *tiles, grad = sweeps(count, *fields, faces, lists, n_north, True)
    chunks, mine, fix = both_edges(
        items, faces[0], pack_both, coef, got, grad, fields[0].shape, n_north, 2, lists[0].shape[0]
    )
    parts = lax.all_to_all(chunks, ("east", "north"), 0, 0, tiled=True)
    return last_step(parts, mine, lax.ppermute(fix, "east", swap), tiles, final)


def solution(mesh):
    placed = (
        P(None, "east", "north", None),
        P(None, "east", "north", None),
        P(None, "east", "north", None),
        P("east", "north", None),
        P("east", "north"),
        P("east", "north", None),
        P("east", "north", None),
        P("east", "north", None),
        P("east", "north", None),
    )
    return jax.shard_map(
        shards,
        mesh=mesh,
        in_specs=placed,
        out_specs=(P(None, "east", "north", None), P(None, None, "north")),
        check_vma=False,
    )
```

```python
import functools

import jax
import jax.numpy as jnp
from jax import lax
from jax.experimental import pallas as pl
from jax.experimental.pallas import tpu as pltpu
from jax.sharding import PartitionSpec as P

SECT = 8
HALF = SECT // 2
TURB_DEV = 12
COMPS = 4
LANES = 128
SUB = 8
PAD = 8
PACK = 14
FACE = 22
EDGE = 9
RAW = 23
ITEM = 8
STEP = 4
OUT_STEP = 4
ROWS_1 = 8
ROWS_2 = 16
VMEM = pltpu.VMEM
F32 = jnp.float32
BF16 = jnp.bfloat16


def whole(space=VMEM):
    return pl.BlockSpec(memory_space=space)


def in_hbm(*arrays):
    return [pltpu.with_memory_space_constraint(x, pltpu.HBM) for x in arrays]


def shape(*dims):
    return jax.ShapeDtypeStruct(dims, F32)


def params(mib):
    return pltpu.CompilerParams(vmem_limit_bytes=mib << 20)


def cost(flops, size):
    return pl.CostEstimate(flops=flops, bytes_accessed=size, transcendentals=0)


class Copies:
    def __init__(self, sems):
        self.sems, self.used = sems, 0

    def take(self, *pairs):
        first = self.used
        self.used += len(pairs)
        return first, pairs

    def made(self, taken):
        first, pairs = taken
        return [pltpu.make_async_copy(s, d, self.sems.at[first + k]) for k, (s, d) in enumerate(pairs)]

    def start(self, taken):
        for c in self.made(taken):
            c.start()

    def wait(self, taken):
        for c in self.made(taken):
            c.wait()


def neighbours():
    e, n = lax.axis_index("east"), lax.axis_index("north")
    last_e, last_n = lax.axis_size("east") - 1, lax.axis_size("north") - 1
    return [
        jnp.where(e > 0, 1, 0), jnp.where(e < last_e, 1, 0),
        jnp.where(n > 0, 1, 0), jnp.where(n < last_n, 1, 0),
    ]


def facing(ce):
    if lax.axis_size("east") == 2:
        e = lax.axis_index("east")
        return [((1 - e) * (ce - 1), (1 - e) * (ce - 1) + 2 * e - 1)]
    return [(0, 1), (ce - 1, ce - 2)]


def one_way(k, sign, w, u, f, inv_v, inv_m, bend=None):
    pull = (w + (0.5 * sign) * u) * inv_v
    out = [pull * f[c] for c in range(3)]
    out[k] = out[k] - (0.5 * sign) * f[3] * inv_v
    out.append((f[3] - (0.5 * sign) * f[k]) * (1.0 / 7.0))
    m = w * f[4]
    if bend is not None:
        m = m + 0.25 * bend
    out.append(m * inv_m)
    return out


def inverse(x):
    y = pl.reciprocal(x, approx=True)
    return y * (2.0 - x * y)


def inverses(w):
    six = 6.0 * w
    return inverse(six + 1.0), inverse(six + 2.0)


def dot3(a, b):
    return a[0] * b[0] + a[1] * b[1] + a[2] * b[2]


def plane_shifts(rows, cols):
    r = lax.broadcasted_iota(jnp.int32, (rows, cols), 0)
    z = lax.broadcasted_iota(jnp.int32, (rows, cols), 1)

    def east(x, before=0.0, after=0.0):
        return (
            jnp.where(r < rows - 1, pltpu.roll(x, rows - 1, 0), after),
            jnp.where(r > 0, pltpu.roll(x, 1, 0), before),
        )

    def level(x):
        return (
            jnp.where(z < cols - 1, pltpu.roll(x, cols - 1, 1), 0.0),
            jnp.where(z > 0, pltpu.roll(x, 1, 1), 0.0),
        )

    return east, level


def ends_kernel(ce, cn, n_faces, start, flow, *refs):
    outs, tiles_v, tiles_u, sems = refs[:n_faces], *refs[n_faces:]
    copies = Copies(sems)
    taken = []
    for i, (e, _) in enumerate(facing(ce)):
        pairs = []
        for side, first in enumerate((0, cn - SUB)):
            pairs.append((start.at[:, e, pl.ds(first, SUB)], tiles_v.at[i, side]))
            pairs.append((flow.at[:, e, pl.ds(first, SUB)], tiles_u.at[i, side]))
        taken.append(copies.take(*pairs))
        copies.start(taken[-1])
    for i, out in enumerate(outs):
        copies.wait(taken[i])
        for side, row in enumerate((0, SUB - 1)):
            for f in range(8):
                tile = tiles_v[i, side, f] if f < 5 else tiles_u[i, side, f - 5]
                out[side * 8 + f : side * 8 + f + 1, :] = tile[row : row + 1]


def row_ends(start, flow, n_faces):
    _, ce, cn, cz = start.shape
    return pl.pallas_call(
        functools.partial(ends_kernel, ce, cn, n_faces),
        out_shape=[shape(16, cz)] * n_faces,
        in_specs=[whole(pltpu.HBM)] * 2,
        out_specs=[whole()] * n_faces,
        scratch_shapes=[
            VMEM((n_faces, 2, 5, SUB, cz), F32),
            VMEM((n_faces, 2, 3, SUB, cz), F32),
            pltpu.SemaphoreType.DMA((4 * n_faces,)),
        ],
        compiler_params=params(60),
        cost_estimate=cost(0, 1 << 16),
    )(start, flow)


def pack_kernel(ce, cn, cz, n_faces, endp, endn, start, source, flow, eddy, *refs):
    packs, refs = refs[:2], refs[2:]
    faces, refs = refs[:n_faces], refs[n_faces:]
    tiles_v, tiles_u, tiles_s, tiles_e, sems = refs
    has = [x.astype(F32) for x in neighbours()[:2]]
    copies = Copies(sems)
    sides = ((0, 0, 1, -1.0), (cn - SUB, SUB - 1, SUB - 2, 1.0))
    needed = []
    for side, (first, _, _, _) in enumerate(sides):
        pairs = []
        for h in range(2):
            cut = (pl.ds(first, SUB), pl.ds(h * LANES, LANES))
            pairs += [
                (start.at[(slice(None), slice(None)) + cut], tiles_v.at[side, :, :, h]),
                (flow.at[(slice(None), slice(None)) + cut], tiles_u.at[side, :, :, h]),
                (eddy.at[(slice(None),) + cut], tiles_e.at[side, 0, :, h]),
                (source.at[(slice(None), slice(None)) + cut], tiles_s.at[side, :, :, h]),
            ]
        needed.append(copies.take(*pairs))
        copies.start(needed[-1])
    later = []
    for (near, far), face in zip(facing(ce), faces):
        taken = copies.take(
            (start.at[:, near], face.at[0:5]),
            (flow.at[:, near], face.at[5:8]),
            (eddy.at[near], face.at[8]),
            (source.at[:, near], face.at[9:14]),
            (start.at[:, far], face.at[14:19]),
            (flow.at[:, far], face.at[19:22]),
        )
        copies.start(taken)
        later.append(taken)
    east, level = plane_shifts(ce, cz)

    def line(ref, side, f, row):
        flat = ref.reshape(2, ref.shape[1], ce * 2 * SUB, LANES)
        return jnp.concatenate([flat[side, f, pl.ds(h * SUB + row, ce, stride=2 * SUB), :] for h in range(2)], axis=1)

    for side, (_, row, behind, sign) in enumerate(sides):
        copies.wait(needed[side])
        pack = packs[side]
        v = [line(tiles_v, side, f, row) for f in range(5)]
        u = [line(tiles_u, side, k, row) for k in range(3)]
        eddy_row = line(tiles_e, side, 0, row)
        inner = [line(tiles_v, side, f, behind) for f in range(5)]
        inner_u = [line(tiles_u, side, k, behind) for k in range(3)]
        src = [line(tiles_s, side, f, row) for f in range(5)]
        for f, x in enumerate(v + u + [eddy_row]):
            pack[f * ce : (f + 1) * ce, :] = x
        w = 1.0 + eddy_row
        inv_v, inv_m = inverses(w)
        before = [endp[side * 8 + f : side * 8 + f + 1, :] * has[0] for f in range(8)]
        after = [endn[side * 8 + f : side * 8 + f + 1, :] * has[1] for f in range(8)]
        for f in range(8):
            pack[PACK * ce + f : PACK * ce + f + 1, :] = before[f]
            pack[PACK * ce + 8 + f : PACK * ce + 9 + f, :] = after[f]
        total, slope0, slope2 = [], [], []
        for f in range(5):
            a, b = east(v[f], before[f], after[f])
            h, l = level(v[f])
            total.append((a + b) + (h + l))
            slope0.append(a - b)
            slope2.append(h - l)
        curv = []
        for k in range(3):
            a, b = east(u[k], before[5 + k], after[5 + k])
            h, l = level(u[k])
            curv.append((a + b) + (h + l) + inner_u[k] - 6.0 * u[k])
        out = one_way(1, -sign, w, u[1], inner, inv_v, inv_m, dot3(v, curv))
        press = (slope0[3], None, slope2[3])
        for c in range(3):
            more = src[c] + w * total[c] + 0.5 * (u[0] * slope0[c] + u[2] * slope2[c])
            if press[c] is not None:
                more = more - 0.5 * press[c]
            out[c] = out[c] + more * inv_v
        out[3] = out[3] + (src[3] + total[3] - 0.5 * (slope0[0] + slope2[2])) * (1.0 / 7.0)
        out[4] = out[4] + (src[4] + w * total[4]) * inv_m
        for f in range(5):
            pack[(9 + f) * ce : (10 + f) * ce, :] = out[f]
    for taken in later:
        copies.wait(taken)


def pack(ends, start, source, flow, eddy, n_faces):
    _, ce, cn, cz = start.shape
    out = [shape(PACK * ce + 16, cz)] * 2 + [shape(FACE, cn, cz)] * n_faces
    got = pl.pallas_call(
        functools.partial(pack_kernel, ce, cn, cz, n_faces),
        out_shape=out,
        in_specs=[whole()] * 2 + [whole(pltpu.HBM)] * 4,
        out_specs=[whole()] * len(out),
        scratch_shapes=[
            VMEM((2, 5, ce, 2, SUB, LANES), F32),
            VMEM((2, 3, ce, 2, SUB, LANES), F32),
            VMEM((2, 5, ce, 2, SUB, LANES), F32),
            VMEM((2, 1, ce, 2, SUB, LANES), F32),
            pltpu.SemaphoreType.DMA((16 + 6 * n_faces,)),
        ],
        compiler_params=params(60),
        cost_estimate=cost(1 << 22, 4 << 20),
    )(*ends, start, source, flow, eddy)
    return got[:2], got[2:]


def leave_chunks(chunks, acc, copies_out):
    whole_acc = acc[...]
    blocks = whole_acc.shape[0] // HALF
    for n in range(blocks):
        chunk = whole_acc[n * HALF : (n + 1) * HALF]
        for k in range(copies_out):
            chunks[k * blocks + n] = chunk


def split(x):
    high = x.astype(BF16)
    return high, (x - high.astype(F32)).astype(BF16)


def owner_of(turbine):
    return lax.shift_right_logical(turbine * 5462, 16)


def columns(x, first, size):
    return jnp.concatenate([x[:, k : k + 1] for k in range(first // LANES, (first + size) // LANES)], axis=0)


def lines(x, first, size):
    return jnp.concatenate([x[k : k + 1, :] for k in range(first // LANES, (first + size) // LANES)], axis=1)


def steps_of(chunks):
    sizes = [0] + [x for x in (2 * LANES,) if x < chunks * LANES] + [chunks * LANES]
    return list(zip(sizes[:-1], sizes[1:]))


def entries(live, cells, turbine, sector, weight, cz):
    cell, tur = cells[...], turbine[...]
    owner = owner_of(tur)
    pair = sector[...]
    key = (owner * HALF + lax.shift_right_logical(pair, 1)).astype(F32)
    local = (tur - owner * TURB_DEV + jnp.bitwise_and(pair, 1) * (COMPS * TURB_DEV)).astype(F32)
    slot = lax.broadcasted_iota(jnp.int32, cell.shape, 0) * LANES + lax.broadcasted_iota(jnp.int32, cell.shape, 1)
    load = jnp.where(slot < live, weight[...], 0.0)
    line = lax.shift_right_logical(cell, cz.bit_length() - 1)
    level = jnp.bitwise_and(cell, cz - 1).astype(F32)
    return slot, line, level, key, local, load


def gather_edge(chosen, edge_row, level, key, local, load, put):
    chunks = chosen.shape[0]
    lower = lax.broadcasted_iota(jnp.int32, (LANES, LANES), 0) < lax.broadcasted_iota(jnp.int32, (LANES, LANES), 1)
    rank = jnp.dot(chosen.astype(BF16), jnp.where(lower, 1.0, 0.0).astype(BF16), preferred_element_type=F32)
    sums = jnp.sum(chosen, axis=1, keepdims=True)
    so_far = jnp.zeros((1, 1), F32)
    starts = []
    for k in range(chunks):
        starts.append(so_far)
        so_far = so_far + sums[k : k + 1]
    rank = jnp.where(chosen > 0.0, rank + jnp.concatenate(starts, axis=0), -1.0)
    total = jnp.sum(chosen).astype(jnp.int32)
    load_high = load.astype(BF16).astype(F32)
    load_rest = load - load_high
    load_mid = load_rest.astype(BF16).astype(F32)
    load_low = load_rest - load_mid
    blank = jnp.zeros((1, LANES), F32)
    rows = [
        jnp.concatenate([x[k : k + 1] for x in (edge_row, level, key, local, load_high, load_mid, load_low)] + [blank])
        for k in range(chunks)
    ]
    to = lax.broadcasted_iota(jnp.int32, (LANES, LANES), 0).astype(F32)
    listed = jnp.concatenate(rows, axis=1).astype(BF16)

    @pl.loop(0, lax.div(total + (LANES - 1), LANES))
    def _(q):
        first = lax.convert_element_type(q * LANES, F32)
        where = jnp.concatenate(
            [jnp.where(rank[k : k + 1] - first == to, 1.0, 0.0) for k in range(chunks)], axis=1
        ).astype(BF16)
        put(q, lax.dot_general(listed, where, (((1,), (1,)), ((), ())), preferred_element_type=F32))

    return total


def rotor_terms(row, level, turbine, weight, key, table, blocks, acc):
    size = row.shape[0]
    rows, width = table.shape[0] // 2, table.shape[1]
    cz = width // COMPS
    lane_row = lax.broadcasted_iota(jnp.int32, (size, rows), 1).astype(F32)
    pick = jnp.where(row == lane_row, 1.0, 0.0).astype(BF16)
    got = jnp.dot(jnp.concatenate([pick, pick], axis=1), table[...], preferred_element_type=F32)
    here = level == lax.broadcasted_iota(jnp.int32, (size, cz), 1).astype(F32)
    lane = lax.broadcasted_iota(jnp.int32, (size, LANES), 1)
    lane_comp = jnp.bitwise_and(owner_of(lane), COMPS - 1)
    lane_tur = (lane - lane_comp * TURB_DEV).astype(F32)
    spread = jnp.zeros((size, LANES), F32)
    for c in range(COMPS):
        part = jnp.where(here, got[:, c * cz : (c + 1) * cz], 0.0)
        spread = jnp.where(lane_comp == c, jnp.sum(part, axis=1, keepdims=True), spread)
    spread = jnp.where(turbine == lane_tur, spread * weight, 0.0)
    lane_key = lax.broadcasted_iota(jnp.int32, (blocks * HALF, size), 0).astype(F32)
    to = jnp.where(lane_key == key, 1.0, 0.0).astype(BF16)
    high = spread.astype(BF16)
    rest = spread - high.astype(F32)
    mid, low = split(rest)
    parts = jnp.dot(to, jnp.concatenate([high, mid, low], axis=1), preferred_element_type=F32)
    acc[...] += parts[:, :LANES] + parts[:, LANES : 2 * LANES] + parts[:, 2 * LANES :]


def halves(ref, f, i, rows, move=0):
    first, size = rows
    return [ref[f, i, h, pl.ds(PAD + first + move, size), :] for h in range(2)]


def level_shifts(x, first, last):
    up = [pltpu.roll(x[h], LANES - 1, 1) for h in range(2)]
    down = [pltpu.roll(x[h], 1, 1) for h in range(2)]
    return (
        [jnp.where(last, up[1], up[0]), jnp.where(last, 0.0, up[1])],
        [jnp.where(first, 0.0, down[0]), jnp.where(first, down[0], down[1])],
    )


def slab_sweep(ref, i, rows, first, last, src, flow, visc, curv):
    two = range(2)
    w = visc
    inv = [inverses(w[h]) for h in two]
    w2 = [2.0 * w[h] for h in two]

    def sides(f):
        mid = halves(ref, f, i, rows)
        a, b = halves(ref, f, i + 1, rows), halves(ref, f, i - 1, rows)
        n, s = halves(ref, f, i, rows, 1), halves(ref, f, i, rows, -1)
        up, down = level_shifts(mid, first, last)
        return mid, a, b, n, s, up, down

    _, a, b, n, s, up, down = sides(3)
    grad = [[x[h] - y[h] for h in two] for x, y in ((a, b), (n, s), (up, down))]
    q_sum = [(a[h] + b[h]) + (n[h] + s[h]) + (up[h] + down[h]) for h in two]
    out, div, bend = [], [0.0, 0.0], [0.0, 0.0]
    for c in range(3):
        mid, a, b, n, s, up, down = sides(c)
        res = []
        for h in two:
            total = (a[h] + b[h]) + (n[h] + s[h]) + (up[h] + down[h])
            slope = [a[h] - b[h], n[h] - s[h], up[h] - down[h]]
            carried = flow[0][h] * slope[0] + flow[1][h] * slope[1] + flow[2][h] * slope[2]
            res.append((src(c)[h] + 0.5 * (w2[h] * total + (carried - grad[c][h]))) * inv[h][0])
            div[h] = div[h] + slope[c]
            bend[h] = bend[h] + mid[h] * curv[c][h]
        out.append(res)
    out.append([(src(3)[h] + q_sum[h] - 0.5 * div[h]) * (1.0 / 7.0) for h in two])
    _, a, b, n, s, up, down = sides(4)
    res = []
    for h in two:
        total = (a[h] + b[h]) + (n[h] + s[h]) + (up[h] + down[h])
        res.append((src(4)[h] + w[h] * total + 0.25 * bend[h]) * inv[h][1])
    out.append(res)
    return out


def sweeps_kernel(
    ce, cn, cz, blocks, pair,
    count, start, source, flow, eddy, facep, facen, cells, turbine, sector, weight,
    final, edge_low, edge_high, grad, *refs,
):
    if not pair:
        coef_low, coef_high, items, n_items = refs[:4]
    held, v0, u, src, ed, v1, curv, table, sems = refs[-9:]
    copies = Copies(sems)
    two = range(2)
    has = [x > 0 for x in neighbours()[:2]]
    inner = pl.ds(PAD, cn)

    def part(h):
        return pl.ds(h * LANES, LANES)

    def halo(face, near, far, slab):
        pairs = []
        for h in two:
            pairs += [
                (face.at[0:5, :, part(h)], v0.at[:, near, h, inner]),
                (face.at[5:8, :, part(h)], u.at[:, near, h, inner]),
                (face.at[8, :, part(h)], ed.at[0, slab, h]),
                (face.at[9:14, :, part(h)], src.at[:, slab, h]),
                (face.at[14:19, :, part(h)], v0.at[:, far, h, inner]),
                (face.at[19:22, :, part(h)], u.at[:, far, h, inner]),
            ]
        return pairs

    ends = ((facep, 1, 0, 0), (facen, ce + 2, ce + 3, ce + 1))
    halos = [copies.take(*halo(*x)) for x in ends]

    def group(g, size):
        span, own, own2 = pl.ds(g, size), pl.ds(g + 1, size), pl.ds(g + 2, size)
        pairs = []
        for h in two:
            pairs += [
                (start.at[:, span, :, part(h)], v0.at[:, own2, h, inner]),
                (flow.at[:, span, :, part(h)], u.at[:, own2, h, inner]),
                (eddy.at[span, :, part(h)], ed.at[0, own, h]),
                (source.at[:, span, :, part(h)], src.at[:, own, h]),
            ]
        return pairs

    groups = [copies.take(*group(g, STEP)) for g in range(0, ce, STEP)]
    per = len(groups[0][1])
    copies.start(groups[0])
    for exists, taken in zip(has, halos):

        @pl.when(exists)
        def _():
            copies.start(taken)

    for taken in groups[1:]:
        copies.start(taken)

    blank = jnp.zeros((PAD, LANES), F32)
    for ref, fields in ((v0, 5), (u, 3), (v1, 5)):

        @pl.loop(0, ref.shape[1])
        def _(i):
            for f in range(fields):
                for h in two:
                    ref[f, i, h, 0:PAD, :] = blank
                    ref[f, i, h, PAD + cn : PAD + cn + PAD, :] = blank

    for exists, (_, near, _, end) in zip(has, ends):

        @pl.when(jnp.logical_not(exists))
        def _():
            for ref, fields, slab in ((v0, 5, near), (u, 3, near), (v1, 5, end)):
                for f in range(fields):
                    for h in two:
                        ref[f, slab, h, inner, :] = jnp.zeros((cn, LANES), F32)

    def ends_of(size):
        lane = lax.broadcasted_iota(jnp.int32, (size, LANES), 1)
        return lane == 0, lane == LANES - 1

    live = count[0, 0]
    slot, line, level, key, local, load = entries(live, cells, turbine, sector, weight, cz)
    chunks = slot.shape[0]
    if not pair:
        north = jnp.bitwise_and(line, cn - 1)
        east = lax.shift_right_logical(line, cn.bit_length() - 1)
        place = jnp.where(north == 0, 0, jnp.where(north == 1, 1, jnp.where(north == cn - 1, 2, 3)))
        is_edge = jnp.logical_or(north <= 1, north >= cn - 2)
        chosen = jnp.where(jnp.logical_and(is_edge, slot < live), 1.0, 0.0)
        edge_row = (place * ce + east).astype(F32)
        items[...] = jnp.zeros_like(items)

        def put(q, x):
            items[q] = x

        n_items[0] = gather_edge(chosen, edge_row, level, key, local, load, put)

    @pl.when(has[0])
    def _():
        copies.wait(halos[0])

    low_slab, high_slab = jnp.where(has[0], 0, 1), jnp.where(has[1], ce + 2, ce + 1)
    steps = ce // STEP

    @pl.loop(0, steps)
    def _(g):
        copies.wait((groups[0][0] + g * per, group(g * STEP, STEP)))

        @pl.when(jnp.logical_and(g == steps - 1, has[1]))
        def _():
            copies.wait(halos[1])

        @pl.loop(jnp.where(g == 0, low_slab, g * STEP), jnp.where(g == steps - 1, high_slab, (g + 1) * STEP))
        def _(i):
            mid = i + 1
            first, last = ends_of(ROWS_1)
            for r in range(0, cn, ROWS_1):
                rows, at = (r, ROWS_1), pl.ds(r, ROWS_1)
                flows = [halves(u, k, mid, rows) for k in range(3)]
                bends = []
                for k in range(3):
                    a, b = halves(u, k, mid + 1, rows), halves(u, k, mid - 1, rows)
                    n, s = halves(u, k, mid, rows, 1), halves(u, k, mid, rows, -1)
                    up, down = level_shifts(flows[k], first, last)
                    res = [(a[h] + b[h]) + (n[h] + s[h]) + (up[h] + down[h]) - 6.0 * flows[k][h] for h in two]
                    for h in two:
                        curv[k, i, h, at, :] = res[h]
                    bends.append(res)
                out = slab_sweep(
                    v0, mid, rows, first, last,
                    lambda f: [src[f, i, h, at, :] for h in two],
                    flows, [1.0 + ed[0, i, h, at, :] for h in two], bends,
                )
                for f in range(5):
                    for h in two:
                        v1[f, i, h, pl.ds(PAD + r, ROWS_1), :] = out[f][h]

    def leave(e):
        return [(held.at[:, pl.ds(e, OUT_STEP)], final.at[:, pl.ds(e, OUT_STEP)])]

    outs = [copies.take(*leave(e)) for e in range(0, ce, OUT_STEP)]

    @pl.loop(0, ce // OUT_STEP)
    def _(g):
        @pl.loop(0, OUT_STEP)
        def _(k):
            e = g * OUT_STEP + k
            i = e + 1
            first, last = ends_of(ROWS_2)

            for r in range(0, cn, ROWS_2):
                rows, span = (r, ROWS_2), pl.ds(r, ROWS_2)
                flows = [halves(u, k, i + 1, rows) for k in range(3)]
                bends = [[curv[k, i, h, span, :] for h in two] for k in range(3)]
                out = slab_sweep(
                    v1, i, rows, first, last,
                    lambda f: [src[f, i, h, span, :] for h in two],
                    flows, [1.0 + ed[0, i, h, span, :] for h in two], bends,
                )
                at = pl.ds(pl.multiple_of(e * cn + r, ROWS_2), ROWS_2)
                below = pl.ds(pl.multiple_of((ce + e) * cn + r, ROWS_2), ROWS_2)
                for h in two:
                    force = flows[0][h] * jnp.abs(flows[0][h])
                    for f in range(5):
                        held[f, e, span, part(h)] = out[f][h]
                    for c in range(COMPS):
                        hi, lo = split(out[c if c < 3 else 4][h] * force)
                        wide = pl.ds(c * cz + h * LANES, LANES)
                        table[at, wide] = hi
                        table[below, wide] = lo

        copies.start((outs[0][0] + g, leave(g * OUT_STEP)))

    def edge_plane(ref, k, first, tall, row):
        fields, slabs = ref.shape[:2]
        flat = ref.reshape(fields, slabs * 2 * tall, LANES)
        return jnp.concatenate(
            [flat[k, pl.ds((first * 2 + h) * tall + row, ce, stride=2 * tall), :] for h in two], axis=1
        )

    tall = PAD + cn + PAD
    edge_rows = () if pair else ((coef_low, 0, 1), (coef_high, cn - 1, cn - 2))
    for coef, row, behind in edge_rows:
        planes = [edge_plane(curv, k, 1, cn, row) for k in range(3)]
        planes += [edge_plane(u, 1, 2, tall, PAD + behind), edge_plane(ed, 0, 1, cn, behind), edge_plane(u, 0, 2, tall, PAD + behind)]
        planes += [edge_plane(v1, k, 1, tall, PAD + row) for k in range(3)]
        for k, x in enumerate(planes):
            coef[k * ce : (k + 1) * ce, :] = x

    tiles = copies.take((held.at[:, :, 0:SUB, :], edge_low), (held.at[:, :, cn - SUB : cn, :], edge_high))
    copies.start(tiles)

    row_t, level_t, local_t, load_t = line.astype(F32).T, level.T, local.T, load.T
    grad[...] = jnp.zeros_like(grad)
    for least, size in steps_of(chunks):

        @pl.when(jnp.logical_and(live > least, live <= size))
        def _():
            cols = [columns(x, 0, size) for x in (row_t, level_t, local_t, load_t)]
            rotor_terms(*cols, lines(key, 0, size), table, blocks, grad)

    for taken in outs + [tiles]:
        copies.wait(taken)


def sweeps(count, start, source, flow, eddy, faces, lists, blocks, pair):
    _, ce, cn, cz = start.shape
    chunks = lists[0].shape[0]
    tall = PAD + cn + PAD
    more = [shape(EDGE * ce, cz)] * 2 + [shape(chunks, ITEM, LANES), jax.ShapeDtypeStruct((1,), jnp.int32)]
    return pl.pallas_call(
        functools.partial(sweeps_kernel, ce, cn, cz, blocks, pair),
        out_shape=[shape(*start.shape)] + [shape(5, ce, SUB, cz)] * 2 + [shape(blocks * HALF, LANES)] + ([] if pair else more),
        in_specs=[whole(pltpu.SMEM)] + [whole(pltpu.HBM)] * 6 + [whole()] * 4,
        out_specs=[whole(pltpu.HBM), whole(), whole(), whole()] + ([] if pair else [whole()] * 3 + [whole(pltpu.SMEM)]),
        scratch_shapes=[
            VMEM(start.shape, F32),
            VMEM((5, ce + 4, 2, tall, LANES), F32),
            VMEM((3, ce + 4, 2, tall, LANES), F32),
            VMEM((5, ce + 2, 2, cn, LANES), F32),
            VMEM((1, ce + 2, 2, cn, LANES), F32),
            VMEM((5, ce + 2, 2, tall, LANES), F32),
            VMEM((3, ce + 2, 2, cn, LANES), F32),
            VMEM((2 * ce * cn, COMPS * cz), BF16),
            pltpu.SemaphoreType.DMA((26 + 8 * (ce // STEP) + ce // OUT_STEP,)),
        ],
        compiler_params=params(48),
        cost_estimate=cost(0, 1 << 10),
    )(count, *in_hbm(start, source, flow, eddy), *faces, *lists)


def edge_kernel(
    ce, cn, cz, blocks, copies_out,
    n_items, facep, facen, own_low, own_high, coef_low, coef_high, got_prev, got_next,
    edge_low, edge_high, items, grad, final_in,
    final, chunks,
    low_out, high_out, table, acc, sems,
):
    east, level = plane_shifts(ce, cz)
    sub = lax.broadcasted_iota(jnp.int32, (SUB, cz), 0)
    has = [x.astype(F32) for x in neighbours()]
    sides = (
        (-1.0, 0, own_low, coef_low, got_prev, edge_low, low_out, 0),
        (1.0, cn - 1, own_high, coef_high, got_next, edge_high, high_out, cn - SUB),
    )
    waits = []
    for side, (sign, row, own, coef, got, edge, out_ref, place) in enumerate(sides):

        def plane(ref, f):
            return ref[f * ce : (f + 1) * ce, :]

        v0 = [plane(own, f) for f in range(5)]
        u = [plane(own, 5 + k) for k in range(3)]
        w = 1.0 + plane(own, 8)
        xv = [plane(got, f) for f in range(5)]
        xu = [plane(got, 5 + k) for k in range(3)]
        xw = 1.0 + plane(got, 8)
        xp = [plane(got, 9 + f) for f in range(5)]
        curv = [plane(coef, k) for k in range(3)]
        inv_v, inv_m = inverses(w)
        delta = one_way(1, sign, w, u[1], xv, inv_v, inv_m, dot3(v0, xu))
        back = one_way(1, -sign, xw, xu[1], v0, *inverses(xw), dot3(xv, u))
        x1 = [xp[f] + back[f] for f in range(5)]
        ends = []
        for far, face in enumerate((facep, facen)):
            hv = [got[PACK * ce + 8 * far + f : PACK * ce + 8 * far + f + 1, :] for f in range(8)]
            fv = [face[f, row : row + 1, :] * has[far] for f in range(5)]
            fu = face[6, row : row + 1, :] * has[far]
            fw = 1.0 + face[8, row : row + 1, :] * has[far]
            ends.append(one_way(1, sign, fw, fu, hv, *inverses(fw), dot3(fv, hv[5:])))
        x1 = [x * has[2 + side] for x in x1]
        total, slope0, slope2 = [], [], []
        for f in range(5):
            a, b = east(delta[f], ends[0][f], ends[1][f])
            h, l = level(delta[f])
            total.append((a + b) + (h + l))
            slope0.append(a - b)
            slope2.append(h - l)
        full = [plane(coef, 6 + c) + delta[c] for c in range(3)]
        add = one_way(1, sign, w, u[1], x1, inv_v, inv_m, dot3(full, xu) + dot3(delta, curv))
        press = (slope0[3], None, slope2[3])
        for c in range(3):
            more = w * total[c] + 0.5 * (u[0] * slope0[c] + u[2] * slope2[c])
            if press[c] is not None:
                more = more - 0.5 * press[c]
            add[c] = add[c] + more * inv_v
        add[3] = add[3] + (total[3] - 0.5 * (slope0[0] + slope2[2])) * (1.0 / 7.0)
        add[4] = add[4] + w * total[4] * inv_m
        ru1, rw, ru0 = plane(coef, 3), 1.0 + plane(coef, 4), plane(coef, 5)
        behind = one_way(1, sign, rw, ru1, delta, *inverses(rw))
        near, far = (0, 1) if side == 0 else (SUB - 1, SUB - 2)
        for f in range(5):
            for e in range(ce):
                rows = jnp.where(
                    sub == near, add[f][e : e + 1, :], jnp.where(sub == far, behind[f][e : e + 1, :], 0.0)
                )
                out_ref[f, e] = edge[f, e] + rows
        copy = pltpu.make_async_copy(out_ref, final.at[:, :, pl.ds(place, SUB), :], sems.at[side])
        copy.start()
        waits.append(copy)
        for behind_row, u0, values in ((0, u[0], add), (1, ru0, behind)):
            force = u0 * jnp.abs(u0)
            at = (2 * side + behind_row) * ce
            for c in range(COMPS):
                hi, lo = split(values[c if c < 3 else 4] * force)
                table[at : at + ce, c * cz : (c + 1) * cz] = hi
                table[4 * ce + at : 5 * ce + at, c * cz : (c + 1) * cz] = lo

    acc[...] = grad[...]
    live = n_items[0]
    for least, size in steps_of(items.shape[0]):

        @pl.when(jnp.logical_and(live > least, live <= size))
        def _():
            lists = [items[k] for k in range(size // LANES)]
            turned = [x.T for x in lists]

            def col(j):
                return jnp.concatenate([x[:, j : j + 1] for x in turned], axis=0)

            key = jnp.concatenate([x[2:3] for x in lists], axis=1)
            rotor_terms(col(0), col(1), col(3), col(4) + col(5) + col(6), key, table, blocks, acc)

    leave_chunks(chunks, acc, copies_out)
    for copy in waits:
        copy.wait()


def edges(n_items, faces, packs, coefs, gots, tiles, items, grad, final, blocks, size):
    _, ce, cn, cz = final.shape
    args = (n_items, *faces, *packs, *coefs, *gots, *tiles, items, grad, final)
    tile = VMEM((5, ce, SUB, cz), F32)
    return pl.pallas_call(
        functools.partial(edge_kernel, ce, cn, cz, blocks, size),
        out_shape=(shape(*final.shape), shape(size * blocks, HALF, LANES)),
        in_specs=[whole(pltpu.SMEM)] + [whole()] * (len(args) - 2) + [whole(pltpu.HBM)],
        out_specs=(whole(pltpu.HBM), whole()),
        scratch_shapes=[
            tile,
            tile,
            VMEM((8 * ce, COMPS * cz), BF16),
            VMEM((blocks * HALF, LANES), F32),
            pltpu.SemaphoreType.DMA((2,)),
        ],
        input_output_aliases={len(args) - 1: 0},
        compiler_params=params(32),
        cost_estimate=cost(1 << 24, 4 << 20),
    )(*args)


def side(own):
    e = lax.axis_index("east")
    return 1 - e if own else e


def raw_kernel(ce, cn, cz, own, *refs):
    if own:
        count, refs = refs[0], refs[1:]
    start, source, flow, eddy, refs = *refs[:4], refs[4:]
    if own:
        lists, (rows, face, items), refs = refs[:4], refs[4:7], refs[7:]
        cells, turbine, sector, weight, sems = refs[4:]
    else:
        rows, sems = refs[0], refs[-1]
        refs = refs[1:]
    tiles_v, tiles_u, tiles_s, tiles_e = refs[:4]
    copies = Copies(sems)
    high = side(own)
    if own:
        held = copies.take(*zip(lists, (cells, turbine, sector, weight)))
        copies.start(held)
    def two_rows(at, to):
        pairs = []
        for h in range(2):
            cut, place = (pl.ds(at, 2), pl.ds(h * LANES, LANES)), pl.ds(to, 2)
            pairs += [
                (start.at[(slice(None), slice(None)) + cut], tiles_v.at[:, :, h, place]),
                (flow.at[(slice(None), slice(None)) + cut], tiles_u.at[:, :, h, place]),
                (eddy.at[(slice(None),) + cut], tiles_e.at[0, :, h, place]),
                (source.at[(slice(None), slice(None)) + cut], tiles_s.at[:, :, h, place]),
            ]
        return pairs

    sides = [copies.take(*two_rows(0, 0)), copies.take(*two_rows(cn - 2, SUB - 2))]

    def both_ways(act):
        for k, taken in enumerate(sides):

            @pl.when(high == k)
            def _():
                act(taken)

    both_ways(copies.start)
    if own:
        ((near, far),) = facing(ce)
        later = copies.take(
            (start.at[:, near], face.at[0:5]),
            (flow.at[:, near], face.at[5:8]),
            (eddy.at[near], face.at[8]),
            (source.at[:, near], face.at[9:14]),
            (start.at[:, far], face.at[14:19]),
            (flow.at[:, far], face.at[19:22]),
        )
        copies.start(later)
        copies.wait(held)
        live = count[0, 0]
        listed = entries(live, cells, turbine, sector, weight, cz)
        edge_items(ce, cn, cz, live, listed, high, items)
        edge_items(ce, cn, cz, live, listed, 1 - high, face.at[FACE:].reshape(-1, cz))

    def plane(ref, f, low, top):
        flat = ref.reshape(ref.shape[0], ce * 2 * SUB, LANES)
        parts = []
        for h in range(2):
            x, y = (flat[f, pl.ds(h * SUB + at, ce, stride=2 * SUB), :] for at in (low, top))
            parts.append(jnp.where(high > 0, y, x))
        return jnp.concatenate(parts, axis=1)

    both_ways(copies.wait)
    planes = [(tiles_v, f, 0) for f in range(5)] + [(tiles_u, k, 0) for k in range(3)] + [(tiles_e, 0, 0)]
    planes += [(tiles_s, f, 0) for f in range(5)]
    planes += [(tiles_v, f, 1) for f in range(5)] + [(tiles_u, k, 1) for k in range(3)] + [(tiles_e, 0, 1)]
    for k, (ref, f, at) in enumerate(planes):
        rows[k * ce : (k + 1) * ce, :] = plane(ref, f, at, SUB - 1 - at)
    if own:
        copies.wait(later)


def edge_items(ce, cn, cz, live, listed, high, out):
    slot, line, level, key, local, load = listed
    north = jnp.bitwise_and(line, cn - 1)
    column = lax.shift_right_logical(line, cn.bit_length() - 1) + lax.axis_index("east") * ce
    edge = high * (cn - 1)
    behind = edge + 1 - 2 * high
    chosen = jnp.where(jnp.logical_and(jnp.logical_or(north == edge, north == behind), slot < live), 1.0, 0.0)
    edge_row = (jnp.where(north == behind, 2 * ce, 0) + column).astype(F32)
    out[...] = jnp.zeros(out.shape, F32)

    def put(q, x):
        out[pl.ds(pl.multiple_of(q * ITEM, ITEM), ITEM), :LANES] = x

    total = gather_edge(chosen, edge_row, level, key, local, load, put)
    out[out.shape[0] - ITEM :, :] = jnp.full((ITEM, cz), total.astype(F32))


def raw_rows(own, start, source, flow, eddy, count=None, lists=()):
    _, ce, cn, cz = start.shape
    out = [shape(RAW * ce, cz)]
    scratch = [
        VMEM((5, ce, 2, SUB, LANES), F32),
        VMEM((3, ce, 2, SUB, LANES), F32),
        VMEM((5, ce, 2, SUB, LANES), F32),
        VMEM((1, ce, 2, SUB, LANES), F32),
    ]
    if own:
        chunks = lists[0].shape[0]
        most = (chunks + 1) * ITEM
        planes = pl.cdiv(most, cn)
        out += [shape(FACE + planes, cn, cz), shape(planes * cn, cz)]
        scratch += [VMEM((chunks, LANES), x.dtype) for x in lists]
    return pl.pallas_call(
        functools.partial(raw_kernel, ce, cn, cz, own),
        out_shape=out,
        in_specs=([whole(pltpu.SMEM)] if own else []) + [whole(pltpu.HBM)] * (4 + len(lists)),
        out_specs=[whole()] * len(out),
        scratch_shapes=scratch + [pltpu.SemaphoreType.DMA((26,))],
        compiler_params=params(16),
        cost_estimate=cost(0, 1 << 10),
    )(*([count] if own else []), *in_hbm(start, source, flow, eddy, *lists))


def joined(ce, own, other, k):
    west = lax.axis_index("east") == 0
    a, b = own[k * ce : (k + 1) * ce, :], other[k * ce : (k + 1) * ce, :]
    return jnp.concatenate([jnp.where(west, a, b), jnp.where(west, b, a)], axis=0)


def join_kernel(ce, cz, own, other, pack, coef):
    sign = (2 * side(True) - 1).astype(F32)
    east, level = plane_shifts(2 * ce, cz)
    raw = [joined(ce, own, other, k) for k in range(RAW)]
    v, u, src, inner, inner_u = raw[:5], raw[5:8], raw[9:14], raw[14:19], raw[19:22]
    w = 1.0 + raw[8]
    inv_v, inv_m = inverses(w)
    total, slope0, slope2 = [], [], []
    for f in range(5):
        a, b = east(v[f])
        h, l = level(v[f])
        total.append((a + b) + (h + l))
        slope0.append(a - b)
        slope2.append(h - l)
    curv = []
    for k in range(3):
        a, b = east(u[k])
        h, l = level(u[k])
        curv.append((a + b) + (h + l) + inner_u[k] - 6.0 * u[k])
    out = one_way(1, -sign, w, u[1], inner, inv_v, inv_m, dot3(v, curv))
    press = (slope0[3], None, slope2[3])
    for c in range(3):
        more = src[c] + w * total[c] + 0.5 * (u[0] * slope0[c] + u[2] * slope2[c])
        if press[c] is not None:
            more = more - 0.5 * press[c]
        out[c] = out[c] + more * inv_v
    out[3] = out[3] + (src[3] + total[3] - 0.5 * (slope0[0] + slope2[2])) * (1.0 / 7.0)
    out[4] = out[4] + (src[4] + w * total[4]) * inv_m
    for k, x in enumerate(raw[:9] + out):
        pack[2 * k * ce : 2 * (k + 1) * ce, :] = x
    for k, x in enumerate(curv + [inner_u[1], raw[22], inner_u[0]]):
        coef[2 * k * ce : 2 * (k + 1) * ce, :] = x


def join_rows(own, other, ce):
    cz = own.shape[1]
    return pl.pallas_call(
        functools.partial(join_kernel, ce, cz),
        out_shape=[shape(PACK * 2 * ce, cz), shape(6 * 2 * ce, cz)],
        in_specs=[whole()] * 2,
        out_specs=[whole()] * 2,
        compiler_params=params(16),
        cost_estimate=cost(0, 1 << 10),
    )(own, other)


def both_kernel(
    ce, cn, cz, blocks, copies_out, n_chunks,
    own, other, pack, coef, got, grad,
    chunks, mine, fix,
    table, acc,
):
    other = other.at[FACE:].reshape(-1, cz)
    wide = 2 * ce
    high = side(True)
    sign = (2 * high - 1).astype(F32)
    north = lax.axis_index("north")
    exists = jnp.where(high > 0, north < lax.axis_size("north") - 1, north > 0).astype(F32)
    east, level = plane_shifts(wide, cz)

    def plane(ref, f):
        return ref[f * wide : (f + 1) * wide, :]

    v0 = [plane(pack, f) for f in range(5)]
    u = [plane(pack, 5 + k) for k in range(3)]
    w = 1.0 + plane(pack, 8)
    xv = [plane(got, f) for f in range(5)]
    xu = [plane(got, 5 + k) for k in range(3)]
    xw = 1.0 + plane(got, 8)
    curv = [plane(coef, k) for k in range(3)]
    inv_v, inv_m = inverses(w)
    delta = one_way(1, sign, w, u[1], xv, inv_v, inv_m, dot3(v0, xu))
    back = one_way(1, -sign, xw, xu[1], v0, *inverses(xw), dot3(xv, u))
    x1 = [(plane(got, 9 + f) + back[f]) * exists for f in range(5)]
    total, slope0, slope2 = [], [], []
    for f in range(5):
        a, b = east(delta[f])
        h, l = level(delta[f])
        total.append((a + b) + (h + l))
        slope0.append(a - b)
        slope2.append(h - l)
    full = [plane(pack, 9 + c) + delta[c] for c in range(3)]
    add = one_way(1, sign, w, u[1], x1, inv_v, inv_m, dot3(full, xu) + dot3(delta, curv))
    press = (slope0[3], None, slope2[3])
    for c in range(3):
        more = w * total[c] + 0.5 * (u[0] * slope0[c] + u[2] * slope2[c])
        if press[c] is not None:
            more = more - 0.5 * press[c]
        add[c] = add[c] + more * inv_v
    add[3] = add[3] + (total[3] - 0.5 * (slope0[0] + slope2[2])) * (1.0 / 7.0)
    add[4] = add[4] + w * total[4] * inv_m
    ru1, rw, ru0 = plane(coef, 3), 1.0 + plane(coef, 4), plane(coef, 5)
    behind = one_way(1, sign, rw, ru1, delta, *inverses(rw))
    west = lax.axis_index("east") == 0
    for k, x in enumerate(add + behind):
        mine[k * ce : (k + 1) * ce, :] = jnp.where(west, x[:ce], x[ce:])
        fix[k * ce : (k + 1) * ce, :] = jnp.where(west, x[ce:], x[:ce])
    for row, u0, values in ((0, u[0], add), (1, ru0, behind)):
        force = u0 * jnp.abs(u0)
        for c in range(COMPS):
            hi, lo = split(values[c if c < 3 else 4] * force)
            table[row * wide : (row + 1) * wide, c * cz : (c + 1) * cz] = hi
            table[(2 + row) * wide : (3 + row) * wide, c * cz : (c + 1) * cz] = lo

    acc[...] = grad[...]
    most = n_chunks

    def chunk(ref, q):
        return ref[q * ITEM : (q + 1) * ITEM, :LANES]

    def terms(lists):
        turned = [x.T for x in lists]

        def col(j):
            return jnp.concatenate([x[:, j : j + 1] for x in turned], axis=0)

        key = jnp.concatenate([x[2:3] for x in lists], axis=1)
        rotor_terms(col(0), col(1), col(3), col(4) + col(5) + col(6), key, table, blocks, acc)

    terms([chunk(own, 0), chunk(other, 0)])
    longest = jnp.max(jnp.maximum(own[own.shape[0] - ITEM :, :LANES], other[other.shape[0] - ITEM :, :LANES]))

    @pl.when(longest > float(LANES))
    def _():
        terms([chunk(ref, q) for ref in (own, other) for q in range(1, most)])

    leave_chunks(chunks, acc, copies_out)


def both_edges(own, other, pack, coef, got, grad, size, blocks, copies_out, n_chunks):
    _, ce, cn, cz = size
    return pl.pallas_call(
        functools.partial(both_kernel, ce, cn, cz, blocks, copies_out, n_chunks),
        out_shape=(shape(copies_out * blocks, HALF, LANES), shape(10 * ce, cz), shape(10 * ce, cz)),
        in_specs=[whole()] * 6,
        out_specs=(whole(), whole(), whole()),
        scratch_shapes=[
            VMEM((8 * ce, COMPS * cz), BF16),
            VMEM((blocks * HALF, LANES), F32),
        ],
        compiler_params=params(32),
        cost_estimate=cost(0, 1 << 10),
    )(own, other, pack, coef, got, grad)


def last_kernel(ce, cn, parts, mine, fix, edge_low, edge_high, final_in, final, out_sum, low_out, high_out, sems):
    high = side(True) > 0
    waits = []
    for k, (edge, out, rows, place) in enumerate(
        ((edge_low, low_out, (0, 1), 0), (edge_high, high_out, (SUB - 1, SUB - 2), cn - 2))
    ):
        from_mine = high if k else jnp.logical_not(high)
        for part, row in enumerate(rows):
            for f in range(5):
                span = pl.ds((part * 5 + f) * ce, ce)
                add = jnp.where(from_mine, mine[span, :], fix[span, :])
                for e in range(ce):
                    out[f, e, row % 2 : row % 2 + 1, :] = edge[f, e, row : row + 1, :] + add[e : e + 1, :]
        copy = pltpu.make_async_copy(out, final.at[:, :, pl.ds(place, 2), :], sems.at[k])
        copy.start()
        waits.append(copy)
    sum_kernel(parts, out_sum)
    for copy in waits:
        copy.wait()


def last_step(parts, mine, fix, tiles, final):
    _, ce, cn, cz = final.shape
    return pl.pallas_call(
        functools.partial(last_kernel, ce, cn),
        out_shape=(shape(*final.shape), shape(COMPS, SECT, TURB_DEV)),
        in_specs=[whole()] * 5 + [whole(pltpu.HBM)],
        out_specs=(whole(pltpu.HBM), whole()),
        scratch_shapes=[
            VMEM((5, ce, 2, cz), F32),
            VMEM((5, ce, 2, cz), F32),
            pltpu.SemaphoreType.DMA((2,)),
        ],
        input_output_aliases={5: 0},
        compiler_params=params(16),
        cost_estimate=cost(0, 1 << 10),
    )(parts, mine, fix, *tiles, final)


def sum_kernel(parts, out):
    total = jnp.sum(parts[...], axis=0)
    for c in range(COMPS):
        for k in range(SECT):
            at = (k % 2 * COMPS + c) * TURB_DEV
            out[c, k : k + 1, :] = total[k // 2 : k // 2 + 1, at : at + TURB_DEV]


def sum_parts(parts):
    return pl.pallas_call(
        sum_kernel,
        out_shape=shape(COMPS, SECT, TURB_DEV),
        in_specs=[whole()],
        out_specs=whole(),
        compiler_params=params(4),
        cost_estimate=cost(parts.size, parts.size * 4),
    )(parts)


def beside(x, size):
    if size == 2:
        got = lax.ppermute(x[0], "east", [(0, 1), (1, 0)])
        return got, got
    up = [(i, i + 1) for i in range(size - 1)]
    down = [(i + 1, i) for i in range(size - 1)]
    return lax.ppermute(x[1], "east", up), lax.ppermute(x[0], "east", down)


def north_ways(x, size):
    up = [(i, i + 1) for i in range(size - 1)]
    down = [(i + 1, i) for i in range(size - 1)]
    return lax.ppermute(x[1], "north", up), lax.ppermute(x[0], "north", down)


def shards(
    adjoint_start,
    adjoint_source,
    base_flow,
    eddy_visc,
    rotor_count,
    rotor_cell,
    rotor_turbine,
    rotor_sector,
    rotor_weight,
):
    _, ce, cn, cz = adjoint_start.shape
    n_east, n_north = lax.axis_size("east"), lax.axis_size("north")
    count = rotor_count
    slots = rotor_cell.shape[-1]
    lists = [x.reshape(slots // LANES, LANES) for x in (rotor_cell, rotor_turbine, rotor_sector, rotor_weight)]

    fields = adjoint_start, adjoint_source, base_flow, eddy_visc
    if n_east == 2:
        return pair_shards(count, fields, lists, n_north)
    n_faces = 2
    ends = beside(row_ends(adjoint_start, base_flow, n_faces), n_east)
    packs, own = pack(ends, *fields, n_faces)
    gots = north_ways(packs, n_north)
    faces = beside(own, n_east)
    final, *tiles, grad, coef_low, coef_high, items, n_items = sweeps(count, *fields, faces, lists, n_north, False)
    final, chunks = edges(
        n_items, faces, packs, (coef_low, coef_high), gots, tiles, items, grad, final, n_north, n_east
    )
    parts = lax.all_to_all(chunks, ("east", "north"), 0, 0, tiled=True)
    return (final, sum_parts(parts))


def pair_shards(count, fields, lists, n_north):
    ce = fields[0].shape[1]
    swap = [(0, 1), (1, 0)]
    (rows,) = raw_rows(False, *fields)
    other = lax.ppermute(rows, "east", swap)
    own, face, items = raw_rows(True, *fields, count, lists)
    pack_both, coef = join_rows(own, other, ce)
    ways = [(n, n_north + n + 1) for n in range(n_north - 1)] + [(n_north + n, n - 1) for n in range(1, n_north)]
    got = lax.ppermute(pack_both, ("east", "north"), ways)
    faces = (lax.ppermute(face, "east", swap),) * 2
    final, *tiles, grad = sweeps(count, *fields, faces, lists, n_north, True)
    chunks, mine, fix = both_edges(
        items, faces[0], pack_both, coef, got, grad, fields[0].shape, n_north, 2, lists[0].shape[0]
    )
    parts = lax.all_to_all(chunks, ("east", "north"), 0, 0, tiled=True)
    return last_step(parts, mine, lax.ppermute(fix, "east", swap), tiles, final)


def solution(mesh):
    placed = (
        P(None, "east", "north", None),
        P(None, "east", "north", None),
        P(None, "east", "north", None),
        P("east", "north", None),
        P("east", "north"),
        P("east", "north", None),
        P("east", "north", None),
        P("east", "north", None),
        P("east", "north", None),
    )
    return jax.shard_map(
        shards,
        mesh=mesh,
        in_specs=placed,
        out_specs=(P(None, "east", "north", None), P(None, None, "north")),
        check_vma=False,
    )
```
